128 devices in a mesh: dp: 32 (over z, x, y_lo), seq: 4 (over y_hi, core).
Axes of the slice: x: 4, y: 4 (y_hi: 2, y_lo: 2; y = y_hi * 2 + y_lo), z: 4, core: 2. Of those that a mesh axis runs over, the one named last changes fastest.
Arguments:
- tokens: bfloat16 [32, 1024, 1024], P('dp', 'seq'), may hold values from -15 to 15
- lengths: int32 [32, 4], P('dp'), may hold values from 1 to 1021, as said below
- ln_gain: bfloat16 [1024], replicated, may hold values from 0.5 to 1.5
- ln_bias: bfloat16 [1024], replicated, may hold values from -3 to 3
- w_qkv: bfloat16 [1024, 3072], replicated, may hold values from -0.1875 to 0.1875
- b_qkv: bfloat16 [3072], replicated, may hold values from -3 to 3
- w_out: bfloat16 [1024, 1024], replicated, may hold values from -1.5 to 1.5
- b_out: bfloat16 [1024], replicated, may hold values from -3 to 3
- w_in: bfloat16 [1024, 4096], replicated, may hold values from -0.1875 to 0.1875
- b_in: bfloat16 [4096], replicated, may hold values from -3 to 3
- w_down: bfloat16 [4096, 1024], replicated, may hold values from -0.09375 to 0.09375
- b_down: bfloat16 [1024], replicated, may hold values from -3 to 3
- cotangent: bfloat16 [32, 1024, 1024], P('dp', 'seq'), may hold values from -6 to 6
Outputs:
- output: bfloat16 [32, 1024, 1024], P('dp', 'seq')
- grad_tokens: float32 [32, 1024, 1024], P('dp', 'seq')
- grad_ln_gain: float32 [1024], P(('dp', 'seq'))
- grad_ln_bias: float32 [1024], P(('dp', 'seq'))
- grad_w_qkv: float32 [1024, 3072], P(('dp', 'seq'))
- grad_b_qkv: float32 [3072], P(('dp', 'seq'))
- grad_w_out: float32 [1024, 1024], P(('dp', 'seq'))
- grad_b_out: float32 [1024], P(('dp', 'seq'))
- grad_w_in: float32 [1024, 4096], P(('dp', 'seq'))
- grad_b_in: float32 [4096], P(('dp', 'seq'))
- grad_w_down: float32 [4096, 1024], P(('dp', 'seq'))
- grad_b_down: float32 [1024], P(('dp', 'seq'))
The draws below stay inside these ranges and needn't reach their ends.
Inputs may be any that keep to these rules, and one draw needn't show every extreme that they name: Each row's lengths sum to 1024. In each row one document, at a drawn place, starts within the first 256 slots and ends within the last 256; every other document has at most 64 slots.
All inputs are finite; a program needn't handle non-finite values.
Results may differ from the reference program's by a relative error of at most 0.0087.
Values may be sent and summed in bfloat16 or wider, within the bound.
A program may use at most 192 MiB of HBM per device.

```python
import math
import jax
import jax.numpy as jnp
from jax import lax

D = 1024
FF = 4096
HEADS = 16
HEAD = 64
ROT = 16
DOCS = 4
TOK_DEV = 256
ROW = 1024
ROWS = 32


def draw_tokens(key, part):
    key = jax.random.fold_in(key, 5)
    key_scale, key_base = jax.random.split(key, 2)
    row_scale = jnp.exp(jax.random.uniform(key_scale, (ROWS, ROW, 1), jnp.float32, math.log(0.3), math.log(3.0)))
    base = jax.random.truncated_normal(key_base, -5.0, 5.0, (ROWS, ROW, D), jnp.float32)
    return (base * row_scale).astype(jnp.bfloat16)


def draw_lengths(key, part):
    key = jax.random.fold_in(key, 11)
    key_short, key_place = jax.random.split(key)
    shorts = jax.random.randint(key_short, (ROWS, DOCS - 1), 1, TOK_DEV // 4 + 1, jnp.int32)
    first_row = jnp.arange(ROWS, dtype=jnp.int32)[:, None] == 0
    shorts = jnp.where(first_row, 1, shorts).astype(jnp.int32)
    longest = ROW - jnp.sum(shorts, axis=1, keepdims=True)
    place = jax.random.randint(key_place, (ROWS, 1), 0, DOCS, jnp.int32)
    columns = jnp.arange(DOCS, dtype=jnp.int32)[None, :]
    source = jnp.clip(columns - (columns > place).astype(jnp.int32), 0, DOCS - 2)
    picked = jnp.take_along_axis(shorts, source, axis=1)
    return jnp.where(columns == place, longest, picked).astype(jnp.int32)


def levels(rng, shape, cuts, least, top_value):
    loudness, own = 1.0, jax.random.fold_in(rng, 6)
    for axis_at, shards_of in cuts:
        steps = jnp.exp(jax.random.uniform(jax.random.fold_in(own, axis_at), (shards_of,), jnp.float32, least / len(cuts), top_value / len(cuts)))
        loudness = loudness * jnp.repeat(steps, shape[axis_at] // shards_of).reshape([-1 if axis == axis_at else 1 for axis in range(len(shape))])
    return loudness


def noise(stream_key, extent, scale, limit, shards=(), kind=jnp.bfloat16):
    entries = jax.random.normal(stream_key, extent, jnp.float32) * scale
    if len(shards) > 0:
        entries = levels(stream_key, extent, shards, -0.22, 0.18) * entries
    return jnp.clip(entries, min=-limit, max=limit).astype(kind)


def setup_inputs(seed: int = 0) -> dict:
    keys = jax.random.split(jax.random.key(seed), 14)
    tokens = draw_tokens(jax.random.fold_in(keys[13], 71), 0)
    lengths = draw_lengths(jax.random.fold_in(keys[13], 71), 0)
    ln_gain = jnp.clip(1.0 + 0.1 * jax.random.normal(keys[2], (D,), jnp.float32), 0.5, 1.5).astype(jnp.bfloat16)
    ln_bias = noise(keys[3], (D,), 0.3, 3.0)
    w_qkv = noise(keys[4], (D, 3 * D), D ** -0.5, 0.1875)
    b_qkv = noise(keys[5], (3 * D,), 0.3, 3.0)
    w_out = noise(keys[6], (D, D), (max(D // 64, 1)) ** -0.5, 1.5)
    b_out = noise(keys[7], (D,), 0.3, 3.0)
    w_in = noise(keys[8], (D, FF), D ** -0.5, 0.1875)
    b_in = noise(keys[9], (FF,), 0.3, 3.0)
    w_down = noise(keys[10], (FF, D), FF ** -0.5, 0.09375)
    b_down = noise(keys[11], (D,), 0.3, 3.0)
    cotangent = noise(keys[12], (ROWS, ROW, D), 1.0, 6.0, ((0, 32), (1, 4)))
    return {"tokens": tokens, "lengths": lengths, "ln_gain": ln_gain, "ln_bias": ln_bias, "w_qkv": w_qkv, "b_qkv": b_qkv, "w_out": w_out, "b_out": b_out, "w_in": w_in, "b_in": b_in, "w_down": w_down, "b_down": b_down, "cotangent": cotangent}


@jax.custom_vjp
def low(v):
    return lax.optimization_barrier(v.astype(jnp.bfloat16)).astype(jnp.float32)

@jax.custom_vjp
def low_back(v):
    return v

def low_keep(v):
    return (low(v), None)

def low_pass(kept, grad):
    return (grad,)

def back_keep(v):
    return (v, None)

def back_low(kept, grad):
    return (low(grad),)
low.defvjp(low_keep, low_pass)
low_back.defvjp(back_keep, back_low)

def product(left, right):
    return jnp.dot(left, right, precision=lax.Precision.HIGHEST, preferred_element_type=jnp.float32)

def layer_norm(inputs, gain_vec, shift_add):
    centre = inputs - lax.optimization_barrier(jnp.mean(inputs, axis=-1, keepdims=True))
    spread = lax.optimization_barrier(jnp.mean(centre * centre, axis=-1, keepdims=True))
    return centre * lax.rsqrt(spread + 1e-05) * gain_vec + shift_add

def gelu_exact(values):
    return jax.nn.gelu(values, approximate=False)

def rotary(values_in, places):
    half_dims = ROT // 2
    freq_steps = jnp.arange(half_dims, dtype=jnp.float32)
    inverse = jnp.exp(freq_steps * (-2.0 * math.log(10000.0) / ROT))
    angles = places[:, None] * inverse[None, :]
    cosine = jnp.cos(angles)[:, None, :]
    sine = jnp.sin(angles)[:, None, :]
    first_half = values_in[..., :half_dims]
    second_half = values_in[..., half_dims:ROT]
    return jnp.concatenate([first_half * cosine - second_half * sine, second_half * cosine + first_half * sine, values_in[..., ROT:]], axis=-1)

def doc_layout(lengths_row, places):
    doc_ends = jnp.cumsum(lengths_row).astype(jnp.int32)
    doc_starts = (doc_ends - lengths_row).astype(jnp.int32)
    inside = (places[:, None] >= doc_starts[None, :]) & (places[:, None] < doc_ends[None, :])
    member = inside.astype(jnp.int32)
    doc_ids = lax.optimization_barrier(jnp.sum(member * jnp.arange(lengths_row.shape[0], dtype=jnp.int32)[None, :], axis=1)).astype(jnp.int32)
    offsets = (places - lax.optimization_barrier(jnp.sum(member * doc_starts[None, :], axis=1))).astype(jnp.int32)
    return (doc_ids, offsets)

def block_layer(row_input, params, doc_ids, offsets):
    ln_gain, ln_bias, w_qkv, b_qkv, w_out, b_out, w_in, b_in, w_down, b_down = params
    slot_count = row_input.shape[0]
    normed = low(layer_norm(row_input, ln_gain, ln_bias))
    project = low_back(product(normed, w_qkv) + b_qkv)
    places = offsets.astype(jnp.float32)
    queries = project[:, :D].reshape(slot_count, HEADS, HEAD)
    keys_all = project[:, D:2 * D].reshape(slot_count, HEADS, HEAD)
    values = project[:, 2 * D:].reshape(slot_count, HEADS, HEAD)
    queries = low(low_back(rotary(queries, places)))
    keys_all = low(low_back(rotary(keys_all, places)))
    values = low(low_back(values))
    row_slots = jnp.arange(slot_count, dtype=jnp.int32)
    allowed = (doc_ids[:, None] == doc_ids[None, :]) & (row_slots[None, :] <= row_slots[:, None])
    score_scale = 1.0 / math.sqrt(HEAD)

    def one_head(triple):
        query_h, key_h, value_h = triple
        scores = low_back(product(query_h, key_h.T) * score_scale)
        scores = jnp.where(allowed, scores, -jnp.inf)
        row_max = lax.optimization_barrier(jnp.max(scores, axis=-1, keepdims=True))
        exp_scores = jnp.exp(scores - row_max)
        probability = low(exp_scores / lax.optimization_barrier(jnp.sum(exp_scores, axis=-1, keepdims=True)))
        return product(probability, value_h)
    mixed_heads = lax.map(jax.checkpoint(one_head), (queries.transpose(1, 0, 2), keys_all.transpose(1, 0, 2), values.transpose(1, 0, 2)))
    mixed_heads = low(low_back(mixed_heads.transpose(1, 0, 2).reshape(slot_count, D)))
    attn_out = product(mixed_heads, w_out) + b_out
    hidden = low_back(product(normed, w_in) + b_in)
    active = low(gelu_exact(hidden))
    return row_input + attn_out + product(active, w_down) + b_down

def add_pair(first, second):
    return first + second

def reference(tokens, lengths, ln_gain, ln_bias, w_qkv, b_qkv, w_out, b_out, w_in, b_in, w_down, b_down, cotangent):
    params = (ln_gain.astype(jnp.float32), ln_bias.astype(jnp.float32), w_qkv.astype(jnp.float32), b_qkv.astype(jnp.float32), w_out.astype(jnp.float32), b_out.astype(jnp.float32), w_in.astype(jnp.float32), b_in.astype(jnp.float32), w_down.astype(jnp.float32), b_down.astype(jnp.float32))
    row_slots = jnp.arange(tokens.shape[1], dtype=jnp.int32)

    def per_row(totals, row_items):
        row_input, row_lengths, row_cotangent = row_items
        doc_ids, offsets = doc_layout(row_lengths, row_slots)

        def forward(layer_input, weights):
            return block_layer(layer_input, weights, doc_ids, offsets)
        result, pullback = jax.vjp(forward, row_input.astype(jnp.float32), params)
        grad_input, grad_weights = pullback(row_cotangent.astype(jnp.float32))
        return (jax.tree.map(add_pair, totals, grad_weights), (result.astype(jnp.bfloat16), grad_input))
    zero_grads = jax.tree.map(jnp.zeros_like, params)
    totals, outputs = lax.scan(per_row, zero_grads, (tokens, lengths, cotangent))
    return (outputs[0], outputs[1], totals[0], totals[1], totals[2], totals[3], totals[4], totals[5], totals[6], totals[7], totals[8], totals[9])
```

```python
import math

import jax
import jax.numpy as jnp
from jax import lax
from jax.experimental import pallas as pl
from jax.experimental.pallas import tpu as pltpu
from jax.sharding import PartitionSpec as P

HEAD = 64
ROT = 16
ROW = 1024
D = 1024
BLK = 256
BF = jnp.bfloat16
F32 = jnp.float32
MESH = pl.DeviceIdType.MESH
VMEM_LIMIT = 60 * 2**20


def dot_nn(a, b):
    return lax.dot_general(a, b, (((1,), (0,)), ((), ())), preferred_element_type=F32)


def dot_nt(a, b):
    return lax.dot_general(a, b, (((1,), (1,)), ((), ())), preferred_element_type=F32)


def dot_tn(a, b):
    return lax.dot_general(a, b, (((0,), (0,)), ((), ())), preferred_element_type=F32)


def loop(count, step):
    def run(i, carry):
        step(i)
        return carry

    lax.fori_loop(0, count, run, 0)


def at256(i):
    return pl.ds(pl.multiple_of(i * 256, 256), 256)


SCRATCH = [
    ("win", (D, 1024), BF),
    ("wdn", (1024, D), BF),
    ("wqkv", (D, 768), BF),
    ("wout", (BLK, D), BF),
    ("nall", (ROW, D), BF),
    ("call", (ROW, D), BF),
    ("q", (ROW, BLK), BF),
    ("k", (ROW, BLK), BF),
    ("v", (ROW, BLK), BF),
    ("do", (ROW, BLK), BF),
    ("act", (ROW, 1024), BF),
    ("gh", (ROW, 1024), BF),
    ("g_ffn", (2, 4, 2, 4, 32, 1024), BF),
    ("g_qkv", (4, 2, 4, 32, 768), BF),
    ("g_out", (4, 2, 4, 8, 1024), F32),
    ("outp", (ROW, D), F32),
    ("gnp", (ROW, D), F32),
    ("hid", (256, 256), F32),
    ("ga", (256, 256), F32),
    ("sc", (BLK, ROW), F32),
    ("dp", (BLK, ROW), F32),
    ("bias", (BLK, ROW), F32),
    ("pb", (BLK, ROW), BF),
    ("ds", (BLK, ROW), BF),
    ("dk", (ROW, BLK), F32),
    ("dv", (ROW, BLK), F32),
    ("dq", (BLK, BLK), F32),
    ("mx", (BLK, BLK), F32),
    ("mixed", (ROW, BLK), BF),
    ("gp", (ROW, 768), BF),
    ("tab", (3, ROW, 128), F32),
    ("sm", (4, 8, 1024), F32),
    ("smr", (10, 8, 1024), F32),
    ("rxs", (2, 2, BLK, D), BF),
    ("rxp", (2, BLK, D), BF),
    ("r1_ffn", (2, 6, 2, 4, 32, 512), BF),
    ("r2_ffn", (2, 6, 2, 32, 512), BF),
    ("ry_ffn", (2, 32, 1024), BF),
    ("r1_qkv", (2, 6, 4, 32, 384), BF),
    ("r2_qkv", (2, 6, 32, 384), BF),
    ("ry_qkv", (32, 768), BF),
    ("r1_out", (2, 6, 4, 8, 512), F32),
    ("r2_out", (2, 6, 8, 512), F32),
    ("ry_out", (8, 1024), F32),
    ("fin_in", (32, 1024), F32),
    ("fin_dn", (32, 1024), F32),
    ("fin_qkv", (32, 768), F32),
    ("fin_out", (8, 1024), F32),
]
NSEM = 160
NLOC = 8


class Links:
    def __init__(self, send, recv):
        self.send, self.recv, self.count = send, recv, 0

    def copy(self, src, dst, device):
        k = self.count
        self.count += 1
        return pltpu.make_async_remote_copy(
            src_ref=src,
            dst_ref=dst,
            send_sem=self.send.at[k],
            recv_sem=self.recv.at[k],
            device_id=device,
            device_id_type=MESH,
        )


def add_into(dst, sources):
    if len(dst.shape) > 2:
        for i in range(dst.shape[0]):
            add_into(dst.at[i], [s.at[i] for s in sources])
        return
    total = dst[...].astype(F32)
    for s in sources:
        total = total + s[...].astype(F32)
    dst[...] = total.astype(dst.dtype)


class Ring:
    def __init__(self, links, block, pos, right, left, land):
        self.block, self.land = block, land
        self.pos = pos
        self.rt, self.lf, self.opp = (pos + 1) % 4, (pos + 3) % 4, (pos + 2) % 4
        c = links.copy
        self.early = [
            c(block(self.opp, 0), land.at[0], right),
            c(block(self.opp, 1), land.at[1], left),
            c(block(self.rt, 1), land.at[2], right),
            c(block(self.lf, 0), land.at[3], left),
        ]
        self.late = [
            c(block(self.rt, 0), land.at[4], right),
            c(block(self.lf, 1), land.at[5], left),
        ]

    def start(self):
        for c in self.early:
            c.start()

    def middle(self):
        self.early[0].wait_recv()
        add_into(self.block(self.rt, 0), [self.land.at[0]])
        self.late[0].start()
        self.early[1].wait_recv()
        add_into(self.block(self.lf, 1), [self.land.at[1]])
        self.late[1].start()

    def finish(self):
        for c in self.early[2:] + self.late:
            c.wait_recv()
        add_into(self.block(self.pos, 0), [self.land.at[4], self.land.at[3]])
        add_into(self.block(self.pos, 1), [self.land.at[2], self.land.at[5]])
        for c in self.early + self.late:
            c.wait_send()


class Reduce:
    def __init__(self, links, ref, lead, land1, land2, land_y, where):
        z, x, yl, dev = where["z"], where["x"], where["yl"], where["dev"]
        half = ref.shape[-1] // 2
        pre = (slice(None),) * lead
        every = slice(None)
        first, second = pl.ds(0, half), pl.ds(half, half)

        def view(a, h, b, cols):
            return ref.at[pre + (a, h, b, every, cols)]

        zr, zl = dev(z + 1, x, yl), dev(z + 3, x, yl)
        xr, xl = dev(z, x + 1, yl), dev(z, x + 3, yl)
        self.one = [
            Ring(links, lambda t, h: view(every, h, t, first), z, zr, zl, land1.at[0]),
            Ring(links, lambda t, h: view(t, h, every, second), x, xr, xl, land1.at[1]),
        ]
        self.two = [
            Ring(links, lambda t, h: view(t, h, z, first), x, xr, xl, land2.at[0]),
            Ring(links, lambda t, h: view(x, h, t, second), z, zr, zl, land2.at[1]),
        ]
        self.own = ref.at[pre + (x, yl, z)]
        self.land_y = land_y
        self.y = links.copy(ref.at[pre + (x, 1 - yl, z)], land_y, dev(z, x, 1 - yl))

    def steps(self):
        one, two = self.one, self.two
        return [
            lambda: [r.start() for r in one],
            lambda: [r.middle() for r in one],
            lambda: [r.finish() for r in one] + [r.start() for r in two],
            lambda: [r.middle() for r in two],
            lambda: [r.finish() for r in two] + [self.y.start()],
            lambda: self.y.wait(),
        ]


def kernel(*refs):
    (vecs, lens, tokens, cot, w_qkv, w_out, w_in, w_down) = refs[:8]
    (o_out, o_tok, o_wqkv, o_wout, o_win, o_wdn, o_small) = refs[8:15]
    rest = refs[15:]
    R = {name: r for (name, _, _), r in zip(SCRATCH, rest)}
    send, recv, loc = rest[len(SCRATCH) :]
    links = Links(send, recv)

    dpi, s = lax.axis_index("dp"), lax.axis_index("seq")
    z, x, yl = dpi // 8, (dpi // 2) % 4, dpi % 2
    yh, c = s // 2, s % 2

    def dev(zz, xx, yy):
        return ((zz % 4) * 8 + (xx % 4) * 2 + yy, s)

    where = {"z": z, "x": x, "yl": yl, "dev": dev}
    sibling = (dpi, yh * 2 + 1 - c)
    partner = (dpi, (1 - yh) * 2 + c)
    others = [(dpi, (s + d) % 4) for d in (1, 2, 3)]
    swapped = (s * 8 + x * 2 + yl, z)

    loads = [
        pltpu.make_async_copy(w_qkv.at[:, pl.ds(pl.multiple_of(j * 1024 + s * 256, 256), 256)], R["wqkv"].at[:, pl.ds(j * 256, 256)], loc.at[j])
        for j in range(3)
    ]
    loads.append(pltpu.make_async_copy(w_out.at[at256(s), :], R["wout"], loc.at[3]))
    wide = pl.ds(pl.multiple_of(s * 1024, 1024), 1024)
    loads.append(pltpu.make_async_copy(w_in.at[:, wide], R["win"], loc.at[4]))
    loads.append(pltpu.make_async_copy(w_down.at[wide, :], R["wdn"], loc.at[5]))
    for c_ in loads:
        c_.start()

    barrier = pltpu.get_barrier_semaphore()
    meet = [dev(z + d, x, yl) for d in (1, 2, 3)] + [dev(z, x + d, yl) for d in (1, 2, 3)]
    meet += [dev(z, x, 1 - yl)] + others
    for d in meet:
        pl.semaphore_signal(barrier, inc=1, device_id=d, device_id_type=MESH)

    @pl.when(z != s)
    def _():
        pl.semaphore_signal(barrier, inc=1, device_id=swapped, device_id_type=MESH)

    pl.semaphore_wait(barrier, jnp.where(z == s, len(meet), len(meet) + 1))

    own, sib = s, yh * 2 + 1 - c
    par, dia = (1 - yh) * 2 + c, (1 - yh) * 2 + 1 - c
    cal, nal = R["call"], R["nall"]
    cot_p = links.copy(cot, cal.at[at256(own), :], partner)
    cot_s = links.copy(cot, cal.at[at256(own), :], sibling)
    cot_p.start()
    cot_s.start()
    cal[at256(own), :] = cot[...]

    gain, shift = vecs[0:1, :], vecs[1:2, :]

    def standard(rows):
        xin = tokens[rows, :].astype(F32)
        cen = xin - jnp.mean(xin, axis=-1, keepdims=True)
        r = lax.rsqrt(jnp.mean(cen * cen, axis=-1, keepdims=True) + 1e-05)
        return xin, cen * r, r

    def norm_strip(u):
        rows = pl.ds(pl.multiple_of(u * 32, 32), 32)
        _, xhat, _ = standard(rows)
        nal[pl.ds(pl.multiple_of(own * 256 + u * 32, 32), 32), :] = (xhat * gain + shift).astype(BF)

    loop(8, norm_strip)
    mine = nal.at[at256(own), :]
    nrm_p = links.copy(mine, mine, partner)
    nrm_s = links.copy(mine, mine, sibling)
    nrm_p.start()
    nrm_s.start()

    sm, smr = R["sm"], R["smr"]
    sm[0] = jnp.zeros((8, 1024), F32)
    sm[0, 1:2, :] = jnp.sum(cot[...].astype(F32), axis=0, keepdims=True)

    start1 = lens[0, 0]
    start2 = start1 + lens[0, 1]
    start3 = start2 + lens[0, 2]

    def doc_of(t):
        return (t >= start1).astype(jnp.int32) + (t >= start2).astype(jnp.int32) + (t >= start3).astype(jnp.int32)

    tab = R["tab"]

    def tables(u):
        rows = pl.ds(pl.multiple_of(u * 64, 64), 64)
        t = lax.broadcasted_iota(jnp.int32, (64, 128), 0) + u * 64
        lane = lax.broadcasted_iota(jnp.int32, (64, 128), 1) % HEAD
        first = jnp.where(t >= start3, start3, jnp.where(t >= start2, start2, jnp.where(t >= start1, start1, 0)))
        offset = (t - first).astype(F32)
        freq = jnp.zeros((64, 128), F32)
        for i in range(ROT // 2):
            freq = jnp.where(lane % (ROT // 2) == i, math.exp(-2.0 * i * math.log(10000.0) / ROT), freq)
        angle = offset * freq
        cosine, sine = jnp.cos(angle), jnp.sin(angle)
        tab[0, rows, :] = jnp.where(lane < ROT, cosine, 1.0)
        tab[1, rows, :] = jnp.where(lane < ROT // 2, -sine, 0.0)
        tab[2, rows, :] = jnp.where((lane >= ROT // 2) & (lane < ROT), sine, 0.0)

    loop(16, tables)

    def rotate(val, rows, sign):
        parts = []
        for p in range(2):
            a = val[:, p * 128 : (p + 1) * 128]
            up = pltpu.roll(a, 128 - ROT // 2, 1) * tab[1, rows, :]
            down = pltpu.roll(a, ROT // 2, 1) * tab[2, rows, :]
            parts.append(a * tab[0, rows, :] + sign * (up + down))
        return jnp.concatenate(parts, axis=1)

    for c_ in loads:
        c_.wait()

    win, wdn, wqkv, wout = R["win"], R["wdn"], R["wqkv"], R["wout"]
    act, gh, hid, ga, outp, gnp = (R[n] for n in ("act", "gh", "hid", "ga", "outp", "gnp"))

    def block(blk):
        rows = at256(blk)
        for j, name in enumerate(("q", "k", "v")):
            b = vecs[4 + j : 5 + j, at256(s)]
            y = dot_nn(nal[rows, :], wqkv[:, j * 256 : (j + 1) * 256]) + b
            if j < 2:
                y = rotate(y, rows, 1.0)
            y = y.astype(BF)
            R[name][rows, :] = y * jnp.asarray(0.125, BF) if j == 0 else y
        R["do"][rows, :] = dot_nt(cal[rows, :], wout[...]).astype(BF)

        def tile(t):
            cs = at256(t)
            hid[...] = dot_nn(nal[rows, :], win[:, cs]) + vecs[pl.ds(7 + s, 1), cs]
            ga[...] = dot_nt(cal[rows, :], wdn[cs, :])

            def strip(u, total):
                r = pl.ds(pl.multiple_of(u * 32, 32), 32)
                h = hid[r, :]
                cdf = 0.5 + 0.5 * lax.erf(h * (1.0 / math.sqrt(2.0)))
                dens = jnp.exp(-0.5 * h * h) * (1.0 / math.sqrt(2.0 * math.pi))
                to = pl.ds(pl.multiple_of(blk * 256 + u * 32, 32), 32)
                act[to, cs] = (h * cdf).astype(BF)
                g = (ga[r, :] * (cdf + h * dens)).astype(BF)
                gh[to, cs] = g
                return total + jnp.sum(g.astype(F32), axis=0, keepdims=True)

            sm[0, 0:1, cs] += lax.fori_loop(0, 8, strip, jnp.zeros((1, 256), F32))

        loop(4, tile)

        def out_tile(n):
            cs = at256(n)
            outp[rows, cs] = dot_nn(act[rows, :], wdn[:, cs])
            gnp[rows, cs] = dot_nt(gh[rows, :], win[cs, :])

        loop(4, out_tile)

    block(own)
    cot_s.wait_recv()
    nrm_s.wait_recv()
    block(sib)
    theirs = cal.at[at256(par), :]
    cot_p.wait_recv()
    cot_f = links.copy(theirs, theirs, sibling)
    cot_f.start()
    theirs = nal.at[at256(par), :]
    nrm_p.wait_recv()
    nrm_f = links.copy(theirs, theirs, sibling)
    nrm_f.start()
    block(par)
    cot_f.wait_recv()
    nrm_f.wait_recv()
    block(dia)
    for c_ in (cot_s, nrm_s, cot_p, nrm_p, cot_f, nrm_f):
        c_.wait_send()

    g_ffn = R["g_ffn"]

    def ffn_grads(m):
        cs = at256(m)
        res = dot_tn(nal[:, cs], gh[...]).astype(BF)
        g_ffn[0, :, :, m] = res.reshape(4, 2, 32, 1024)
        res = dot_tn(act[:, cs], cal[...]).astype(BF)
        g_ffn[1, m] = res.reshape(2, 4, 32, 1024)

    loop(4, ffn_grads)
    ffn = Reduce(links, g_ffn, 1, R["r1_ffn"], R["r2_ffn"], R["ry_ffn"], where)
    ffn_steps = ffn.steps()
    ffn_steps[0]()

    q, k, v, do = R["q"], R["k"], R["v"], R["do"]
    sc, dp, bias, pb, ds = (R[n] for n in ("sc", "dp", "bias", "pb", "ds"))
    dk, dv, dq, mx, mixed, gp = (R[n] for n in ("dk", "dv", "dq", "mx", "mixed", "gp"))
    rxs, rxp = R["rxs"], R["rxp"]
    dk[...] = jnp.zeros((ROW, BLK), F32)
    dv[...] = jnp.zeros((ROW, BLK), F32)
    to_sib = {}
    to_par = {}

    def attend(i):
        n = 256 * (i + 1)
        rows = pl.ds(256 * i, 256)
        keys = pl.ds(0, n)

        def mask(u):
            r = pl.ds(pl.multiple_of(u * 32, 32), 32)
            tr = lax.broadcasted_iota(jnp.int32, (32, n), 0) + (256 * i + u * 32)
            tc = lax.broadcasted_iota(jnp.int32, (32, n), 1)
            ok = (doc_of(tr) == doc_of(tc)) & (tc <= tr)
            bias[r, keys] = jnp.where(ok, 0.0, -1e30)

        loop(8, mask)
        dq[...] = jnp.zeros((BLK, BLK), F32)
        mx[...] = jnp.zeros((BLK, BLK), F32)

        def head(h):
            lanes = lax.broadcasted_iota(jnp.int32, (BLK, BLK), 1) // HEAD == h
            qh = jnp.where(lanes, q[rows, :], jnp.zeros((), BF))
            doh = jnp.where(lanes, do[rows, :], jnp.zeros((), BF))
            sc[:, keys] = dot_nt(qh, k[keys, :])
            dp[:, keys] = dot_nt(doh, v[keys, :])

            def strip(u):
                r = pl.ds(pl.multiple_of(u * 16, 16), 16)
                a = sc[r, keys] + bias[r, keys]
                e = jnp.exp(a - jnp.max(a, axis=-1, keepdims=True))
                p = e * (1.0 / jnp.sum(e, axis=-1, keepdims=True))
                pb[r, keys] = p.astype(BF)
                g = dp[r, keys]
                inner = jnp.sum(p * g, axis=-1, keepdims=True)
                ds[r, keys] = (p * (g - inner)).astype(BF)

            loop(16, strip)
            mx[...] += jnp.where(lanes, dot_nn(pb[:, keys], v[keys, :]), 0.0)
            dq[...] += jnp.where(lanes, dot_nn(ds[:, keys], k[keys, :]), 0.0)
            dk[keys, :] += dot_tn(ds[:, keys], qh)
            dv[keys, :] += dot_tn(pb[:, keys], doh)

        loop(4, head)
        mixed[rows, :] = mx[...].astype(BF)
        grad_q = (dq[...] * 0.125).astype(BF).astype(F32)
        gp[rows, 0:256] = rotate(grad_q, rows, -1.0).astype(BF)
        grad_k = dk[rows, :].astype(BF).astype(F32)
        gp[rows, 256:512] = rotate(grad_k, rows, -1.0).astype(BF)
        gp[rows, 512:768] = dv[rows, :].astype(BF)
        sm[0, 2:3, 0:768] += jnp.sum(gp[rows, :].astype(F32), axis=0, keepdims=True)

        def project(n_):
            cs = at256(n_)
            o = outp[rows, cs] + dot_nn(mixed[rows, :], wout[:, cs])
            outp[rows, cs] = o
            act[rows, cs] = o.astype(BF)
            g = gnp[rows, cs] + dot_nt(gp[rows, :], wqkv[cs, :])
            gnp[rows, cs] = g
            gh[rows, cs] = g.astype(BF)

        loop(4, project)
        j = i // 2
        cps = [links.copy(st.at[rows, :], rxs.at[j, w], sibling) for w, st in enumerate((act, gh))]
        to_sib[i] = cps

        @pl.when(c != i % 2)
        def _():
            for cp in cps:
                cp.start()

    def pass_on(j):
        for i in (2 * j, 2 * j + 1):

            @pl.when(c != i % 2)
            def _(i=i):
                for cp in to_sib[i]:
                    cp.wait_send()

            @pl.when(c == i % 2)
            def _(i=i):
                for cp in to_sib[i]:
                    cp.wait_recv()

        mine_j = at256(2 * j + c)

        @pl.when(yh != j)
        def _():
            def strip(u):
                r = pl.ds(pl.multiple_of((2 * j + c) * 256 + u * 32, 32), 32)
                ru = pl.ds(pl.multiple_of(u * 32, 32), 32)
                act[r, :] = (outp[r, :] + rxs[j, 0, ru, :].astype(F32)).astype(BF)
                gh[r, :] = (gnp[r, :] + rxs[j, 1, ru, :].astype(F32)).astype(BF)

            loop(8, strip)
            for cp in to_par[j]:
                cp.start()

    for j in (0, 1):
        to_par[j] = [links.copy(st.at[at256(2 * j + c), :], rxp.at[w], partner) for w, st in enumerate((act, gh))]

    attend(3)
    ffn_steps[1]()
    attend(2)
    pass_on(1)
    ffn_steps[2]()
    attend(1)
    ffn_steps[3]()
    attend(0)
    pass_on(0)
    ffn_steps[4]()

    g_qkv, g_out = R["g_qkv"], R["g_out"]

    def qkv_grads(m):
        res = dot_tn(nal[:, at256(m)], gp[...]).astype(BF)
        g_qkv[:, :, m] = res.reshape(4, 2, 32, 768)

    loop(4, qkv_grads)
    g_out[...] = dot_tn(mixed[...], cal[...]).reshape(4, 2, 4, 8, 1024)
    att = [
        Reduce(links, g_qkv, 0, R["r1_qkv"], R["r2_qkv"], R["ry_qkv"], where),
        Reduce(links, g_out, 0, R["r1_out"], R["r2_out"], R["ry_out"], where),
    ]
    att_steps = [r.steps() for r in att]

    def att_step(n):
        for st in att_steps:
            st[n]()

    att_step(0)
    ffn_steps[5]()
    finals = []
    fin_in, fin_dn, fin_qkv, fin_out = (R[n] for n in ("fin_in", "fin_dn", "fin_qkv", "fin_out"))
    mine8 = pl.ds(pl.multiple_of(s * 8, 8), 8)

    def spread(src, dst, lane):
        for d in (1, 2, 3):
            t = (s + d) % 4
            cp = links.copy(src.at[pl.ds(pl.multiple_of(t * 8, 8), 8), lane[0]], dst.at[:, lane[1]], (dpi, t))
            cp.start()
            finals.append(cp)
        dst[:, lane[1]] = src[mine8, lane[0]]

    swaps = []

    def swap(src, dst):
        cp = links.copy(src, dst, swapped)
        swaps.append(cp)

        @pl.when(z != s)
        def _():
            cp.start()

        @pl.when(z == s)
        def _():
            dst[...] = src[...]

    fin_in[...] = ffn.own[0].astype(F32) + ffn.land_y[0].astype(F32)
    fin_dn[...] = ffn.own[1].astype(F32) + ffn.land_y[1].astype(F32)
    spread(fin_in, o_win, (slice(None), wide))
    swap(fin_dn, o_wdn)
    att_step(1)

    for cp0, cp1 in zip(to_par[0], to_par[1]):

        @pl.when(yh == 0)
        def _(cp=cp0, cq=cp1):
            cp.wait_recv()
            cq.wait_send()

        @pl.when(yh == 1)
        def _(cp=cp1, cq=cp0):
            cp.wait_recv()
            cq.wait_send()

    def last_strip(u, carry):
        sg, sb = carry
        ru = pl.ds(pl.multiple_of(u * 16, 16), 16)
        r = pl.ds(pl.multiple_of(own * 256 + u * 16, 16), 16)
        xin, xhat, rs = standard(ru)
        total = outp[r, :] + rxs[yh, 0, ru, :].astype(F32) + rxp[0, ru, :].astype(F32)
        o_out[ru, :] = (xin + total + vecs[2:3, :] + vecs[3:4, :]).astype(BF)
        gn = gnp[r, :] + rxs[yh, 1, ru, :].astype(F32) + rxp[1, ru, :].astype(F32)
        n = gn * gain
        back = rs * (n - jnp.mean(n, axis=-1, keepdims=True) - xhat * jnp.mean(n * xhat, axis=-1, keepdims=True))
        o_tok[ru, :] = cot[ru, :].astype(F32) + back
        sg = sg + jnp.sum(gn * xhat, axis=0, keepdims=True)
        sb = sb + jnp.sum(gn, axis=0, keepdims=True)
        return sg, sb

    zero = jnp.zeros((1, D), F32)
    sg, sb = lax.fori_loop(0, 16, last_strip, (zero, zero))
    sm[0, 3:4, :] = sg
    sm[0, 4:5, :] = sb

    def exchange(level, slot, devices):
        cps = [links.copy(sm.at[level], smr.at[slot + d], t) for d, t in enumerate(devices)]
        for cp in cps:
            cp.start()
        return cps

    def gather(level, slot, cps):
        for cp in cps:
            cp.wait()
        total = sm[level]
        for d in range(len(cps)):
            total = total + smr[slot + d]
        sm[level + 1] = total

    cps = exchange(0, 0, [dev(z + d, x, yl) for d in (1, 2, 3)])
    att_step(2)
    gather(0, 0, cps)
    cps = exchange(1, 3, [dev(z, x + d, yl) for d in (1, 2, 3)])
    att_step(3)
    gather(1, 3, cps)
    cps = exchange(2, 6, [dev(z, x, 1 - yl)])
    att_step(4)
    gather(2, 6, cps)
    cps = exchange(3, 7, others)
    att_step(5)
    fin_qkv[...] = att[0].own[...].astype(F32) + att[0].land_y[...].astype(F32)
    fin_out[...] = att[1].own[...] + att[1].land_y[...]
    for j in range(3):
        spread(fin_qkv, o_wqkv, (pl.ds(j * 256, 256), pl.ds(pl.multiple_of(j * 1024 + s * 256, 256), 256)))
    swap(fin_out, o_wout)
    for cp in cps:
        cp.wait()
    o_small[s] = sm[3]
    for d in range(3):
        o_small[(s + 3 - d) % 4] = smr[7 + d]
    for cp in finals:
        cp.wait()

    @pl.when(z != s)
    def _():
        for cp in swaps:
            cp.wait()

    assert links.count <= NSEM, links.count


def on_device(tokens, lengths, ln_gain, ln_bias, w_qkv, b_qkv, w_out, b_out, w_in, b_in, w_down, b_down, cotangent):
    vecs = jnp.concatenate([ln_gain, ln_bias, b_out, b_down, b_qkv, b_in, jnp.zeros((5 * D,), BF)])
    vecs = vecs.reshape(16, D).astype(F32)
    V = pl.BlockSpec(memory_space=pltpu.VMEM)
    H = pl.BlockSpec(memory_space=pl.ANY)
    S = pl.BlockSpec(memory_space=pltpu.SMEM)
    sds = jax.ShapeDtypeStruct
    outs = pl.pallas_call(
        kernel,
        out_shape=[
            sds((BLK, D), BF),
            sds((BLK, D), F32),
            sds((8, 3 * D), F32),
            sds((8, D), F32),
            sds((8, 4 * D), F32),
            sds((32, D), F32),
            sds((4, 8, 1024), F32),
        ],
        in_specs=[V, S, V, V, H, H, H, H],
        out_specs=[V] * 7,
        scratch_shapes=[pltpu.VMEM(shape, dt) for _, shape, dt in SCRATCH]
        + [pltpu.SemaphoreType.DMA((NSEM,)), pltpu.SemaphoreType.DMA((NSEM,)), pltpu.SemaphoreType.DMA((NLOC,))],
        compiler_params=pltpu.CompilerParams(collective_id=0, has_side_effects=True, vmem_limit_bytes=VMEM_LIMIT),
        name="layer",
    )(vecs, lengths, tokens[0], cotangent[0], w_qkv, w_out, w_in, w_down)
    out, grad_tokens, g_wqkv, g_wout, g_win, g_wdn, small = outs
    index = lax.axis_index("dp") * 4 + lax.axis_index("seq")

    def share(vec):
        n = vec.shape[0] // 128
        return lax.dynamic_slice_in_dim(vec, index * n, n)

    g_bin = share(small[:, 0].reshape(4096))
    g_bout = share(jnp.sum(small[:, 1], axis=0))
    g_bqkv = share(small[:, 2, :768].reshape(4, 3, 256).transpose(1, 0, 2).reshape(3072))
    g_gain = share(jnp.sum(small[:, 3], axis=0))
    g_bias = share(jnp.sum(small[:, 4], axis=0))
    return (out[None], grad_tokens[None], g_gain, g_bias, g_wqkv, g_bqkv, g_wout, g_bout, g_win, g_bin, g_wdn, g_bout)


def solution(mesh):
    act, vec, mat = P("dp", "seq", None), P(("dp", "seq")), P(("dp", "seq"), None)
    return jax.shard_map(
        on_device,
        mesh=mesh,
        in_specs=(act, P("dp", None)) + (P(),) * 10 + (act,),
        out_specs=(act, act, vec, vec, mat, vec, mat, vec, mat, vec, mat, vec),
        check_vma=False,
    )
```

```python
import math

import jax
import jax.numpy as jnp
from jax import lax
from jax.experimental import pallas as pl
from jax.experimental.pallas import tpu as pltpu
from jax.sharding import PartitionSpec as P

HEAD = 64
ROT = 16
ROW = 1024
D = 1024
BLK = 256
BF = jnp.bfloat16
F32 = jnp.float32
MESH = pl.DeviceIdType.MESH
VMEM_LIMIT = 63 * 2**20


def dot_nn(a, b):
    return lax.dot_general(a, b, (((1,), (0,)), ((), ())), preferred_element_type=F32)


def dot_nt(a, b):
    return lax.dot_general(a, b, (((1,), (1,)), ((), ())), preferred_element_type=F32)


def dot_tn(a, b):
    return lax.dot_general(a, b, (((0,), (0,)), ((), ())), preferred_element_type=F32)


def loop(count, step):
    def run(i, carry):
        step(i)
        return carry

    lax.fori_loop(0, count, run, 0)


def at256(i):
    return pl.ds(pl.multiple_of(i * 256, 256), 256)


SCRATCH = [
    ("vecs", (16, D), F32),
    ("win", (2, D, 1024), BF),
    ("wdn", (2, 1024, D), BF),
    ("wqkv", (2, 2, D, 384), BF),
    ("wout", (2, BLK, D), BF),
    ("nall", (ROW, D), BF),
    ("call", (ROW, D), BF),
    ("q", (2, ROW, 128), BF),
    ("k", (2, ROW, 128), BF),
    ("v", (2, ROW, 128), BF),
    ("do", (2, ROW, 128), BF),
    ("kt", (2, 128, ROW), BF),
    ("vt", (2, 128, ROW), BF),
    ("qh", (2, BLK, 128), BF),
    ("doh", (2, BLK, 128), BF),
    ("act", (ROW, 1024), BF),
    ("gh", (ROW, 1024), BF),
    ("g_ffn", (2, 2, 4, 4, 4, 16, 1024), BF),
    ("g_qkv", (2, 4, 2, 4, 32, 384), BF),
    ("g_out", (4, 2, 4, 16, 512), BF),
    ("outp", (512, D), F32),
    ("gnp", (512, D), F32),
    ("sc", (2, ROW, BLK), F32),
    ("dp", (2, ROW, BLK), F32),
    ("bias", (ROW, BLK), F32),
    ("dk", (ROW, 128), F32),
    ("dv", (ROW, 128), F32),
    ("dq", (128, BLK), F32),
    ("mx", (128, BLK), F32),
    ("xr", (512, 1024), BF),
    ("tab", (2, ROW, 128), F32),
    ("mr", (2, BLK, 128), F32),
    ("sm", (4, 8, 1024), F32),
    ("smr", (10, 8, 1024), F32),
    ("rxs", (2, BLK, D), BF),
    ("r1z_ffn", (2, 6, 2, 4, 2, 16, 512), BF),
    ("r1x_ffn", (2, 6, 2, 2, 4, 16, 512), BF),
    ("r2_ffn", (2, 2, 6, 2, 2, 16, 512), BF),
    ("r3_ffn", (2, 3, 2, 16, 1024), BF),
    ("r1z_qkv", (2, 6, 4, 32, 256), BF),
    ("r1x_qkv", (2, 6, 4, 32, 256), BF),
    ("r2_qkv", (2, 2, 6, 32, 256), BF),
    ("r3_qkv", (2, 1, 32, 384), BF),
    ("r1z_out", (6, 4, 16, 256), BF),
    ("r1x_out", (6, 4, 16, 256), BF),
    ("r2_out", (2, 6, 16, 256), BF),
    ("r3_out", (1, 16, 512), BF),
    ("fin_ffn", (2, 2, 16, 1024), F32),
    ("fin_qkv", (2, 32, 384), F32),
    ("fin_out", (16, 512), F32),
]
CH = 256
NSEM = 200
NLOC = 20


class Links:
    def __init__(self, send, recv):
        self.send, self.recv, self.count = send, recv, 0

    def copy(self, src, dst, device):
        k = self.count
        self.count += 1
        return pltpu.make_async_remote_copy(
            src_ref=src,
            dst_ref=dst,
            send_sem=self.send.at[k],
            recv_sem=self.recv.at[k],
            device_id=device,
            device_id_type=MESH,
        )


def add_into(dst, sources):
    if len(dst.shape) > 2:
        for i in range(dst.shape[0]):
            add_into(dst.at[i], [s.at[i] for s in sources])
        return
    total = dst[...].astype(F32)
    for s in sources:
        total = total + s[...].astype(F32)
    dst[...] = total.astype(dst.dtype)


class Ring:
    def __init__(self, links, block, pos, right, left, land):
        self.block, self.land = block, land
        self.pos = pos
        self.rt, self.lf, self.opp = (pos + 1) % 4, (pos + 3) % 4, (pos + 2) % 4
        c = links.copy
        self.early = [
            c(block(self.opp, 0), land.at[0], right),
            c(block(self.opp, 1), land.at[1], left),
            c(block(self.rt, 1), land.at[2], right),
            c(block(self.lf, 0), land.at[3], left),
        ]
        self.late = [
            c(block(self.rt, 0), land.at[4], right),
            c(block(self.lf, 1), land.at[5], left),
        ]

    def start(self):
        for c in self.early:
            c.start()

    def middle(self):
        self.early[0].wait_recv()
        add_into(self.block(self.rt, 0), [self.land.at[0]])
        self.late[0].start()
        self.early[1].wait_recv()
        add_into(self.block(self.lf, 1), [self.land.at[1]])
        self.late[1].start()

    def finish(self):
        for c in self.early[2:] + self.late:
            c.wait_recv()
        add_into(self.block(self.pos, 0), [self.land.at[4], self.land.at[3]])
        add_into(self.block(self.pos, 1), [self.land.at[2], self.land.at[5]])
        for c in self.early + self.late:
            c.wait_send()


class Reduce:
    def __init__(self, links, ref, lead, lands, pos, at_z, at_x, last, after, half):
        z, x, y = pos
        pre = (slice(None),) * lead
        every = slice(None)
        first, second = pl.ds(0, half), pl.ds(half, ref.shape[-1] - half)
        ny = ref.shape[lead + 1] // 2
        land1z, land1x, land2z, land2x, self.land_y = lands

        def view(a, h, b, cols):
            hh = h if ny == 1 else pl.ds(h * ny, ny)
            return ref.at[pre + (a, hh, b, every, cols)]

        zr, zl, xr, xl = at_z(1), at_z(3), at_x(1), at_x(3)
        self.one = [
            Ring(links, lambda t, h: view(every, h, t, first), z, zr, zl, land1z),
            Ring(links, lambda t, h: view(t, h, every, second), x, xr, xl, land1x),
        ]
        self.two = [
            Ring(links, lambda t, h: view(t, h, z, first), x, xr, xl, land2z),
            Ring(links, lambda t, h: view(x, h, t, second), z, zr, zl, land2x),
        ]
        self.own = ref.at[pre + (x, y, z)]
        self.last = [links.copy(ref.at[pre + (x, ty, z)], self.land_y.at[n], d) for n, (ty, d) in enumerate(last)]
        self.after = after
        self.at = 0

    def result(self, index=()):
        total = self.own[index or ...].astype(F32)
        for n in range(len(self.last)):
            total = total + self.land_y[(n,) + index].astype(F32)
        return total

    def step(self):
        one, two = self.one, self.two
        if self.at == 0:
            for r in one:
                r.start()
        elif self.at == 1:
            for r in one:
                r.middle()
        elif self.at == 2:
            for r, n in zip(one, two):
                r.finish()
            for n in two:
                n.start()
        elif self.at == 3:
            for r in two:
                r.middle()
        elif self.at == 4:
            for r in two:
                r.finish()
            for cp in self.last:
                cp.start()
        elif self.at == 5:
            for cp in self.last:
                cp.wait()
            self.after(self)
        self.at += 1


def kernel(*refs):
    small, (lens, tokens, cot, w_qkv, w_out, w_in, w_down) = refs[:6], refs[6:13]
    (o_out, o_tok, o_wqkv, o_wout, o_win, o_wdn, o_small) = refs[13:20]
    rest = refs[20:]
    R = {name: r for (name, _, _), r in zip(SCRATCH, rest)}
    send, recv, loc = rest[len(SCRATCH) :]
    links = Links(send, recv)

    dpi, s = lax.axis_index("dp"), lax.axis_index("seq")
    z, x, yl = dpi // 8, (dpi // 2) % 4, dpi % 2
    yh, c = s // 2, s % 2
    y = yh * 2 + yl

    def dev(zz, xx, yy, cc):
        return ((zz % 4) * 8 + (xx % 4) * 2 + (yy % 4) % 2, ((yy % 4) // 2) * 2 + cc)

    def at_z(d):
        return dev(z + d, x, y, c)

    def at_x(d):
        return dev(z, x + d, y, c)

    def at_y(d):
        return dev(z, x, y + d, c)

    sibling = dev(z, x, y, 1 - c)
    partner = dev(z, x, y + 2, c)
    diagonal = dev(z, x, y + 2, 1 - c)

    loads = []

    def load(src, dst):
        cp = pltpu.make_async_copy(src, dst, loc.at[len(loads)])
        cp.start()
        loads.append(cp)

    for a in range(2):
        wide = pl.ds(pl.multiple_of((2 * a + c) * 1024, 1024), 1024)
        load(w_in.at[:, wide], R["win"].at[a])
        load(w_down.at[wide, :], R["wdn"].at[a])
    for w, sw in enumerate((s, (1 - yh) * 2 + c)):
        load(w_out.at[at256(sw), :], R["wout"].at[w])
        for g in range(2):
            for j in range(3):
                cols = pl.ds(pl.multiple_of(j * 1024 + sw * 256 + g * 128, 128), 128)
                load(w_qkv.at[:, cols], R["wqkv"].at[w, g, :, pl.ds(j * 128, 128)])

    meet = [at_x(d) for d in (1, 2, 3)] + [at_y(d) for d in (1, 2, 3)] + [sibling, diagonal]
    for d in (1, 2, 3):
        for cc in (c, 1 - c):
            meet += [dev(z + d, x, y, cc), dev(z + d, x, y + 2, cc)]
    barrier = pltpu.get_barrier_semaphore()
    for d in meet:
        pl.semaphore_signal(barrier, inc=1, device_id=d, device_id_type=MESH)
    pl.semaphore_wait(barrier, len(meet))

    own, sib = s, yh * 2 + 1 - c
    par, dia = (1 - yh) * 2 + c, (1 - yh) * 2 + 1 - c
    cal, nal = R["call"], R["nall"]
    cot_s = links.copy(cot, cal.at[at256(own), :], sibling)
    cot_p = links.copy(cot, cal.at[at256(own), :], partner)
    cot_s.start()
    cot_p.start()
    cal[at256(own), :] = cot[...]

    vecs, row = R["vecs"], 0
    for ref in small:
        for i in range(ref.shape[0] // D):
            vecs[row : row + 1, :] = ref[pl.ds(i * D, D)].astype(F32).reshape(1, D)
            row += 1
    gain, shift = vecs[0:1, :], vecs[1:2, :]
    mr = R["mr"]

    def norm_strip(u, carry):
        rows = pl.ds(pl.multiple_of(u * 32, 32), 32)
        xin = tokens[rows, :].astype(F32)
        mean = jnp.mean(xin, axis=-1, keepdims=True)
        cen = xin - mean
        r = lax.rsqrt(jnp.mean(cen * cen, axis=-1, keepdims=True) + 1e-05)
        mr[0, rows, :] = jnp.broadcast_to(mean, (32, 128))
        mr[1, rows, :] = jnp.broadcast_to(r, (32, 128))
        nal[pl.ds(pl.multiple_of(own * 256 + u * 32, 32), 32), :] = (cen * r * gain + shift).astype(BF)
        return carry

    lax.fori_loop(0, 8, norm_strip, 0, unroll=2)
    mine = nal.at[at256(own), :]
    nrm_s = links.copy(mine, mine, sibling)
    nrm_p = links.copy(mine, mine, partner)
    nrm_s.start()
    nrm_p.start()

    sm, smr = R["sm"], R["smr"]
    sm[0] = jnp.zeros((8, 1024), F32)
    sm[0, 4:5, :] = jnp.sum(cot[...].astype(F32), axis=0, keepdims=True)

    start1 = lens[0, 0]
    start2 = start1 + lens[0, 1]
    start3 = start2 + lens[0, 2]

    def first_of(t):
        return jnp.where(t >= start3, start3, jnp.where(t >= start2, start2, jnp.where(t >= start1, start1, 0)))

    tab = R["tab"]

    def tables(u):
        rows = pl.ds(pl.multiple_of(u * 64, 64), 64)
        t = lax.broadcasted_iota(jnp.int32, (64, 128), 0) + u * 64
        lane = lax.broadcasted_iota(jnp.int32, (64, 128), 1) % HEAD
        offset = (t - first_of(t)).astype(F32)
        freq = jnp.zeros((64, 128), F32)
        for i in range(ROT // 2):
            freq = jnp.where(lane % (ROT // 2) == i, math.exp(-2.0 * i * math.log(10000.0) / ROT), freq)
        angle = offset * freq
        cosine, sine = jnp.cos(angle), jnp.sin(angle)
        tab[0, rows, :] = jnp.where(lane < ROT, cosine, 1.0)
        tab[1, rows, :] = jnp.where(lane < ROT // 2, -sine, jnp.where(lane < ROT, sine, 0.0))

    loop(16, tables)
    low_lane = lax.broadcasted_iota(jnp.int32, (BLK, 128), 1) % HEAD < ROT // 2

    def rotate(val, rows, sign):
        other = jnp.where(low_lane, pltpu.roll(val, 128 - ROT // 2, 1), pltpu.roll(val, ROT // 2, 1))
        return val * tab[0, rows, :] + sign * other * tab[1, rows, :]

    for cp in loads:
        cp.wait()

    win, wdn, wqkv, wout = R["win"], R["wdn"], R["wqkv"], R["wout"]
    act, gh, outp, gnp = (R[n] for n in ("act", "gh", "outp", "gnp"))
    hid, ga = R["sc"].at[0, pl.ds(0, 512)], R["dp"].at[0, pl.ds(0, 512)]
    q, k, v, do, kt, vt, qh, doh = (R[n] for n in ("q", "k", "v", "do", "kt", "vt", "qh", "doh"))

    def qkv_block(blk):
        rows = at256(blk)
        for g in range(2):
            yv = dot_nn(nal[rows, :], wqkv[0, g])
            for j, dst in enumerate((q, k, v)):
                b = vecs[4 + j : 5 + j, pl.ds(pl.multiple_of(s * 256 + g * 128, 128), 128)]
                part = yv[:, j * 128 : (j + 1) * 128] + b
                if j < 2:
                    part = rotate(part, rows, 1.0)
                part = part.astype(BF)
                dst[g, rows, :] = part * jnp.asarray(0.125, BF) if j == 0 else part
                if j > 0:
                    (kt, vt)[j - 1][g, :, rows] = jnp.transpose(part)
        d = dot_nt(cal[rows, :], wout[0]).astype(BF)
        do[0, rows, :] = d[:, 0:128]
        do[1, rows, :] = d[:, 128:256]

    here = pl.ds(pl.multiple_of(yh * 512, 512), 512)
    there = pl.ds(pl.multiple_of((1 - yh) * 512, 512), 512)

    def ffn_tiles(a):
        half = pl.ds(a * 512, 512)

        def tile(t):
            cs = at256(t)
            hid[...] = dot_nn(nal[here, :], win[a, :, cs]) + vecs[pl.ds(7 + 2 * a + c, 1), cs]
            ga[...] = dot_nt(cal[here, :], wdn[a, cs, :])

            def strip(u, total):
                r = pl.ds(pl.multiple_of(u * 32, 32), 32)
                h = hid[r, :]
                cdf = 0.5 + 0.5 * lax.erf(h * (1.0 / math.sqrt(2.0)))
                dens = jnp.exp(-0.5 * h * h) * (1.0 / math.sqrt(2.0 * math.pi))
                to = pl.ds(pl.multiple_of(a * 512 + u * 32, 32), 32)
                act[to, cs] = (h * cdf).astype(BF)
                grad = (ga[r, :] * (cdf + h * dens)).astype(BF)
                gh[to, cs] = grad
                return total + jnp.sum(grad.astype(F32).reshape(4, 8, 256), axis=0)

            total = lax.fori_loop(0, 16, strip, jnp.zeros((8, 256), F32), unroll=2)
            sm[0, a : a + 1, cs] = jnp.sum(total, axis=0, keepdims=True)

        loop(4, tile)

    g_ffn = R["g_ffn"]

    def ffn_grads(a):
        half = pl.ds(a * 512, 512)

        def part(m):
            cs = at256(m)
            res = dot_tn(nal[here, cs], gh[half, :]).astype(BF)
            g_ffn[a, 0, :, :, m] = res.reshape(4, 4, 16, 1024)
            res = dot_tn(act[half, cs], cal[here, :]).astype(BF)
            g_ffn[a, 1, m] = res.reshape(4, 4, 16, 1024)

        loop(4, part)

    def ffn_out(n):
        cs = at256(n)
        top, low = pl.ds(0, 512), pl.ds(512, 512)
        outp[:, cs] = dot_nn(act[top, :], wdn[0, :, cs]) + dot_nn(act[low, :], wdn[1, :, cs])
        gnp[:, cs] = dot_nt(gh[top, :], win[0, cs, :]) + dot_nt(gh[low, :], win[1, cs, :])

    finals = []

    def put(src, dst, device, sends=None, arrives=None):
        cp = links.copy(src, dst, device)
        finals.append((cp, sends, arrives))
        if sends is None:
            cp.start()
        else:
            pl.when(sends)(cp.start)

    def keep(src, dst, here_too):
        @pl.when(here_too)
        def _():
            dst[...] = src[...]

    fin_ffn, fin_qkv, fin_out = R["fin_ffn"], R["fin_qkv"], R["fin_out"]

    def ffn_done(a):
        def done(red):
            for w in range(2):
                fin_ffn[a, w] = red.result((w,))
            cols = pl.ds(pl.multiple_of((2 * a + c) * 1024, 1024), 1024)
            theirs = pl.ds(pl.multiple_of((1 - c) * 8, 8), 8)
            put(fin_ffn.at[a, 0, theirs, :], o_win.at[:, cols], sibling)
            o_win[:, cols] = fin_ffn[a, 0, pl.ds(pl.multiple_of(c * 8, 8), 8), :]
            to = dev(2 * a + c, x, y, z // 2)
            for h in range(2):
                rows, right = pl.ds(h * 16, 16), z % 2 == h
                here_too = (z == 2 * a + c) & (z // 2 == c)
                from_here = (z == 2 * c + h) & (z % 2 == c)
                sends = right & jnp.logical_not(here_too)
                arrives = (z // 2 == a) & jnp.logical_not(from_here)
                put(fin_ffn.at[a, 1], o_wdn.at[rows, :], to, sends, arrives)
                keep(fin_ffn.at[a, 1], o_wdn.at[rows, :], right & here_too)

        return done

    def qkv_done(g):
        def done(red):
            fin_qkv[g] = red.result()
            for j in range(3):
                src_l = pl.ds(j * 128, 128)
                dst_l = pl.ds(pl.multiple_of(j * 1024 + s * 256 + g * 128, 128), 128)
                for d in (1, 2, 3):
                    t = (s + d) % 4
                    put(fin_qkv.at[g, pl.ds(pl.multiple_of(t * 8, 8), 8), src_l], o_wqkv.at[:, dst_l], (dpi, t))
                o_wqkv[:, dst_l] = fin_qkv[g, pl.ds(pl.multiple_of(s * 8, 8), 8), src_l]

        return done

    def out_done(red):
        fin_out[...] = red.result()
        for cc in range(2):
            to = dev(s, x, (z // 2) * 2 + yl, cc)
            src = fin_out.at[pl.ds(cc * 8, 8), :]
            for h in range(2):
                dst, right = o_wout.at[:, pl.ds(h * 512, 512)], z % 2 == h
                here_too = (z == s) & (z // 2 == yh) & (c == cc)
                from_here = (z == 2 * yh + h) & (s == z)
                sends = right & jnp.logical_not(here_too)
                arrives = (c == cc) & jnp.logical_not(from_here)
                put(src, dst, to, sends, arrives)
                keep(src, dst, right & here_too)

    def place(yy):
        return (yy % 2) * 2 + (yy % 4) // 2

    def reduce_ffn(a):
        last = [(place(y + d), at_y(d)) for d in (1, 2, 3)]
        lands = (R["r1z_ffn"].at[a], R["r1x_ffn"].at[a], R["r2_ffn"].at[a, 0], R["r2_ffn"].at[a, 1], R["r3_ffn"].at[a])
        return Reduce(links, g_ffn.at[a], 1, lands, (z, x, place(y)), at_z, at_x, last, ffn_done(a), 512)

    last_yl = [(1 - yl, dev(z, x, yh * 2 + 1 - yl, c))]

    def reduce_qkv(g):
        half = 256 if g == 0 else 128
        one, two = pl.ds(0, half), pl.ds(0, 384 - half)
        lands = (R["r1z_qkv"].at[g, :, :, :, one], R["r1x_qkv"].at[g, :, :, :, two])
        lands += (R["r2_qkv"].at[g, 0, :, :, one], R["r2_qkv"].at[g, 1, :, :, two], R["r3_qkv"].at[g])
        return Reduce(links, R["g_qkv"].at[g], 0, lands, (z, x, yl), at_z, at_x, last_yl, qkv_done(g), half)

    def reduce_out():
        lands = (R["r1z_out"], R["r1x_out"], R["r2_out"].at[0], R["r2_out"].at[1], R["r3_out"])
        return Reduce(links, R["g_out"], 0, lands, (z, x, yl), at_z, at_x, last_yl, out_done, 256)

    sc, dp, bias = R["sc"], R["dp"], R["bias"]
    pb = [win.at[0, :, pl.ds(u * 256, 256)] for u in range(2)]
    ds = [win.at[0, :, pl.ds(512 + u * 256, 256)] for u in range(2)]
    dk, dv, dq, mx = (R[n] for n in ("dk", "dv", "dq", "mx"))
    xo, xr = act, R["xr"]
    g_qkv, g_out = R["g_qkv"], R["g_out"]

    def attend(g, i):
        n = 256 * (i + 1)
        rows = pl.ds(256 * i, 256)
        keys = pl.ds(0, n)
        chunks = [pl.ds(j * CH, CH) for j in range(n // CH)]

        def fold(a, op):
            return op(a.reshape(CH // 8, 8, BLK), axis=0)

        def mask(j):
            tk = lax.broadcasted_iota(jnp.int32, (128, BLK), 0) + j * 128
            tq = lax.broadcasted_iota(jnp.int32, (128, BLK), 1) + 256 * i
            ok = (tk >= first_of(tq)) & (tk <= tq)
            bias[pl.ds(pl.multiple_of(j * 128, 128), 128), :] = jnp.where(ok, 0.0, -1e30)

        loop(n // 128, mask)
        heads = range(2)
        tops, stats = [], []
        for u in heads:
            lanes = lax.broadcasted_iota(jnp.int32, (BLK, 128), 1) // HEAD == u
            qh[u] = jnp.where(lanes, q[g, rows, :], jnp.zeros((), BF))
            doh[u] = jnp.where(lanes, do[g, rows, :], jnp.zeros((), BF))
        for u in heads:
            top = jnp.full((8, BLK), -1e30, F32)
            for ch in chunks:
                a = dot_nt(k[g, ch, :], qh[u]) + bias[ch, :]
                sc[u, ch, :] = a
                top = jnp.maximum(top, fold(a, jnp.max))
            tops.append(jnp.max(top, axis=0, keepdims=True))
        for u in heads:
            total, inner = jnp.zeros((8, BLK), F32), jnp.zeros((8, BLK), F32)
            for ch in chunks:
                gr = dot_nt(v[g, ch, :], doh[u])
                dp[u, ch, :] = gr
                e = jnp.exp(sc[u, ch, :] - tops[u])
                sc[u, ch, :] = e
                total, inner = total + fold(e, jnp.sum), inner + fold(e * gr, jnp.sum)
            inv = 1.0 / jnp.sum(total, axis=0, keepdims=True)
            stats.append((inv, jnp.sum(inner, axis=0, keepdims=True) * inv))
        for u in heads:
            inv, inner = stats[u]
            for j, ch in enumerate(chunks):
                p = sc[u, ch, :] * inv
                p_low = p.astype(BF)
                d_low = (p * (dp[u, ch, :] - inner)).astype(BF)
                pb[u][ch, :] = p_low
                ds[u][ch, :] = d_low
                if i == 3 and u == 0:
                    dk[ch, :] = dot_nn(d_low, qh[u])
                    dv[ch, :] = dot_nn(p_low, doh[u])
                else:
                    dk[ch, :] += dot_nn(d_low, qh[u])
                    dv[ch, :] += dot_nn(p_low, doh[u])
        for u in heads:
            hr = pl.ds(u * HEAD, HEAD)
            mx[hr, :] = dot_nn(vt[g, hr, keys], pb[u][keys, :])
            dq[hr, :] = dot_nn(kt[g, hr, keys], ds[u][keys, :])

        def place_in(j, val):
            xo[rows, pl.ds(g * 512 + j * 128, 128)] = val

        place_in(3, jnp.transpose(mx[...]).astype(BF))
        grad_q = jnp.transpose(dq[...] * 0.125).astype(BF).astype(F32)
        place_in(0, rotate(grad_q, rows, -1.0).astype(BF))
        grad_k = dk[rows, :].astype(BF).astype(F32)
        place_in(1, rotate(grad_k, rows, -1.0).astype(BF))
        place_in(2, dv[rows, :].astype(BF))

    back = []

    def send_back(g):
        cols = pl.ds(g * 512, 512)
        cp = links.copy(xo.at[there, cols], xr.at[:, cols], partner)
        cp.start()
        back.append(cp)

    def qkv_grads(g):
        def part(m):
            res = dot_tn(nal[:, at256(m)], xo[:, pl.ds(g * 512, 384)]).astype(BF)
            g_qkv[g, :, :, m] = res.reshape(4, 2, 32, 384)

        loop(4, part)

    def bias_grads(g):
        total = jnp.zeros((8, 384), F32)

        def part(u, total):
            r = pl.ds(pl.multiple_of(u * 64, 64), 64)
            return total + jnp.sum(xo[r, pl.ds(g * 512, 384)].astype(F32).reshape(8, 8, 384), axis=0)

        total = jnp.sum(lax.fori_loop(0, 16, part, total), axis=0, keepdims=True)
        for j in range(3):
            for h in range(2):
                val = jnp.where(yh == h, total[:, j * 128 : (j + 1) * 128], 0.0)
                sm[0, 2 + h : 3 + h, pl.ds(j * 256 + g * 128, 128)] = val

    def out_grads(g):
        res = dot_tn(xo[:, pl.ds(g * 512 + 384, 128)], cal[...]).astype(BF).reshape(2, 2, 2, 16, 1024)
        for h in range(2):
            for n in range(2):
                g_out[pl.ds(2 * g, 2), :, 2 * h + n] = res[:, :, h, :, n * 512 : (n + 1) * 512]

    def project(rows_of, src, w):
        def part(n):
            cs = at256(n)
            add_o = dot_nn(src[rows_of, pl.ds(384, 128)], wout[w, 0:128, cs]) + dot_nn(
                src[rows_of, pl.ds(896, 128)], wout[w, 128:256, cs]
            )
            outp[:, cs] += add_o
            add_g = dot_nt(src[rows_of, pl.ds(0, 384)], wqkv[w, 0, cs, :]) + dot_nt(
                src[rows_of, pl.ds(512, 384)], wqkv[w, 1, cs, :]
            )
            gnp[:, cs] += add_g

        loop(4, part)

    cot_s.wait_recv()
    nrm_s.wait_recv()
    ffn_tiles(0)
    ffn_grads(0)
    red0 = reduce_ffn(0)
    red0.step()
    ffn_tiles(1)
    ffn_grads(1)
    red1 = reduce_ffn(1)
    red1.step()
    red0.step()
    loop(4, ffn_out)
    qkv_block(own)
    qkv_block(sib)
    theirs = cal.at[at256(par), :]
    cot_p.wait_recv()
    cot_f = links.copy(theirs, theirs, sibling)
    cot_f.start()
    theirs = nal.at[at256(par), :]
    nrm_p.wait_recv()
    nrm_f = links.copy(theirs, theirs, sibling)
    nrm_f.start()
    qkv_block(par)
    cot_f.wait_recv()
    nrm_f.wait_recv()
    qkv_block(dia)
    for cp in (cot_s, nrm_s, cot_p, nrm_p, cot_f, nrm_f):
        cp.wait_send()

    attend(0, 3)
    red0.step()
    attend(0, 2)
    red1.step()
    attend(0, 1)
    attend(0, 0)
    send_back(0)
    qkv_grads(0)
    red2 = reduce_qkv(0)
    red2.step()
    red0.step()
    attend(1, 3)
    red0.step()
    red1.step()
    attend(1, 2)
    red2.step()
    attend(1, 1)
    red0.step()
    attend(1, 0)
    send_back(1)
    red1.step()
    qkv_grads(1)
    red3 = reduce_qkv(1)
    red3.step()
    for g in range(2):
        out_grads(g)
    red4 = reduce_out()
    red4.step()
    red2.step()
    project(here, xo, 0)
    red1.step()
    for g in range(2):
        bias_grads(g)
    red2.step()
    red3.step()
    red4.step()
    red1.step()

    for cp in back:
        cp.wait_recv()
    project(pl.ds(0, 512), xr, 1)
    stage = gh
    theirs_at, mine_at = (1 - c) * 256, c * 256
    rxs = R["rxs"]

    def stage_strip(u):
        r = pl.ds(pl.multiple_of(u * 64, 64), 64)
        rr = pl.ds(pl.multiple_of(theirs_at + u * 64, 64), 64)
        stage[r, :] = outp[rr, :].astype(BF)
        stage[pl.ds(pl.multiple_of(256 + u * 64, 64), 64), :] = gnp[rr, :].astype(BF)

    loop(4, stage_strip)
    swap = [links.copy(stage.at[pl.ds(w * 256, 256), :], rxs.at[w], sibling) for w in range(2)]
    for cp in swap:
        cp.start()
    red2.step()
    red3.step()
    red4.step()
    for cp in swap:
        cp.wait()

    def last_strip(u, carry):
        sg, sb = carry
        ru = pl.ds(pl.multiple_of(u * 32, 32), 32)
        r = pl.ds(pl.multiple_of(mine_at + u * 32, 32), 32)
        xin = tokens[ru, :].astype(F32)
        total = outp[r, :] + rxs[0, ru, :].astype(F32)
        o_out[ru, :] = (xin + total + vecs[2:3, :] + vecs[3:4, :]).astype(BF)
        gn = gnp[r, :] + rxs[1, ru, :].astype(F32)
        rs = mr[1, ru, 0:1]
        hat = (xin - mr[0, ru, 0:1]) * rs
        n = gn * gain
        grad = n - jnp.mean(n, axis=-1, keepdims=True) - hat * jnp.mean(n * hat, axis=-1, keepdims=True)
        o_tok[ru, :] = cot[ru, :].astype(F32) + grad * rs
        sg = sg + jnp.sum((gn * hat).reshape(4, 8, D), axis=0)
        sb = sb + jnp.sum(gn.reshape(4, 8, D), axis=0)
        return sg, sb

    zero = jnp.zeros((8, D), F32)
    sg, sb = lax.fori_loop(0, 8, last_strip, (zero, zero), unroll=2)
    sm[0, 5:6, :] = jnp.sum(sg, axis=0, keepdims=True)
    sm[0, 6:7, :] = jnp.sum(sb, axis=0, keepdims=True)

    def exchange(level, slot, devices):
        cps = [links.copy(sm.at[level], smr.at[slot + d], t) for d, t in enumerate(devices)]
        for cp in cps:
            cp.start()
        return cps

    def gather(level, slot, cps):
        for cp in cps:
            cp.wait()
        total = sm[level]
        for d in range(len(cps)):
            total = total + smr[slot + d]
        sm[level + 1] = total

    cps = exchange(0, 0, [at_z(d) for d in (1, 2, 3)])
    red3.step()
    red4.step()
    gather(0, 0, cps)
    cps = exchange(1, 3, [at_x(d) for d in (1, 2, 3)])
    red2.step()
    red3.step()
    red4.step()
    gather(1, 3, cps)
    cps = exchange(2, 6, [at_y(d) for d in (1, 2, 3)])
    red3.step()
    red4.step()
    gather(2, 6, cps)
    cps = exchange(3, 9, [sibling])
    for cp in cps:
        cp.wait()
    o_small[c] = sm[3]
    o_small[1 - c] = smr[9]
    for cp in back:
        cp.wait_send()
    for cp, sends, arrives in finals:
        if sends is None:
            cp.wait()
        else:
            pl.when(sends)(cp.wait_send)
            pl.when(arrives)(cp.wait_recv)
    for r in (red0, red1, red2, red3, red4):
        assert r.at == 6, r.at
    assert links.count <= NSEM, links.count


def hand_over(*refs):
    raw, small = refs[:6], refs[6]
    outs, vec, line = refs[7:13], refs[13:18], refs[18]
    for src, dst in zip(raw, outs):
        dst[...] = src[...]
    index = lax.axis_index("dp") * 4 + lax.axis_index("seq")
    for r, row in enumerate((5, 6, None, 4, None)):
        if row is not None:
            line[r : r + 1, 0:D] = small[0, row : row + 1, :] + small[1, row : row + 1, :]
    for t in range(4):
        line[4:5, t * 1024 : (t + 1) * 1024] = small[t % 2, t // 2 : t // 2 + 1, :]
        for j in range(3):
            line[2:3, pl.ds(j * 1024 + t * 256, 256)] = small[t % 2, 2 + t // 2 : 3 + t // 2, j * 256 : (j + 1) * 256]
    for r, out in enumerate(vec):
        n = out.shape[0]
        at = index * n
        part = line[r : r + 1, pl.ds(pl.multiple_of((at // 128) * 128, 128), 256)]
        part = pltpu.roll(jnp.broadcast_to(part, (8, 256)), (256 - at % 128) % 256, 1)
        out[...] = part[0, 0:n]


def on_device(tokens, lengths, ln_gain, ln_bias, w_qkv, b_qkv, w_out, b_out, w_in, b_in, w_down, b_down, cotangent):
    V = pl.BlockSpec(memory_space=pltpu.VMEM)
    H = pl.BlockSpec(memory_space=pl.ANY)
    S = pl.BlockSpec(memory_space=pltpu.SMEM)
    sds = jax.ShapeDtypeStruct
    outs = pl.pallas_call(
        kernel,
        out_shape=[
            sds((BLK, D), BF),
            sds((BLK, D), F32),
            sds((8, 3 * D), F32),
            sds((8, D), F32),
            sds((8, 4 * D), F32),
            sds((32, D), F32),
            sds((2, 8, 1024), F32),
        ],
        in_specs=[V] * 6 + [S, V, V, H, H, H, H],
        out_specs=[V] * 7,
        scratch_shapes=[pltpu.VMEM(shape, dt) for _, shape, dt in SCRATCH]
        + [pltpu.SemaphoreType.DMA((NSEM,)), pltpu.SemaphoreType.DMA((NSEM,)), pltpu.SemaphoreType.DMA((NLOC,))],
        compiler_params=pltpu.CompilerParams(collective_id=0, has_side_effects=True, vmem_limit_bytes=VMEM_LIMIT),
        name="layer",
    )(ln_gain, ln_bias, b_out, b_down, b_qkv, b_in, lengths, tokens[0], cotangent[0], w_qkv, w_out, w_in, w_down)
    vec = [sds((n // 128,), F32) for n in (D, D, 3 * D, D, 4 * D)]
    finals = pl.pallas_call(
        hand_over,
        out_shape=[sds(o.shape, o.dtype) for o in outs[:6]] + vec,
        in_specs=[V] * 7,
        out_specs=[V] * 11,
        scratch_shapes=[pltpu.VMEM((8, 4 * D + 128), F32)],
        name="shares",
    )(*outs)
    out, grad_tokens, g_wqkv, g_wout, g_win, g_wdn, g_gain, g_bias, g_bqkv, g_bout, g_bin = finals
    return (out[None], grad_tokens[None], g_gain, g_bias, g_wqkv, g_bqkv, g_wout, g_bout, g_win, g_bin, g_wdn, g_bout)


def solution(mesh):
    act, vec, mat = P("dp", "seq", None), P(("dp", "seq")), P(("dp", "seq"), None)
    return jax.shard_map(
        on_device,
        mesh=mesh,
        in_specs=(act, P("dp", None)) + (P(),) * 10 + (act,),
        out_specs=(act, act, vec, vec, mat, vec, mat, vec, mat, vec, mat, vec),
        check_vma=False,
    )
```

```python
import math

import jax
import jax.numpy as jnp
from jax import lax
from jax.experimental import pallas as pl
from jax.experimental.pallas import tpu as pltpu
from jax.sharding import PartitionSpec as P

HEAD = 64
ROT = 16
ROW = 1024
D = 1024
BLK = 256
BF = jnp.bfloat16
F32 = jnp.float32
MESH = pl.DeviceIdType.MESH
VMEM_LIMIT = 63 * 2**20


def dot_nn(a, b):
    return lax.dot_general(a, b, (((1,), (0,)), ((), ())), preferred_element_type=F32)


def dot_nt(a, b):
    return lax.dot_general(a, b, (((1,), (1,)), ((), ())), preferred_element_type=F32)


def dot_tn(a, b):
    return lax.dot_general(a, b, (((0,), (0,)), ((), ())), preferred_element_type=F32)


def loop(count, step):
    def run(i, carry):
        step(i)
        return carry

    lax.fori_loop(0, count, run, 0)


def at256(i):
    return pl.ds(pl.multiple_of(i * 256, 256), 256)


SCRATCH = [
    ("vecs", (16, D), F32),
    ("win", (2, D, 1024), BF),
    ("wdn", (2, 1024, D), BF),
    ("wqkv", (2, 2, D, 384), BF),
    ("wout", (2, BLK, D), BF),
    ("nall", (ROW, D), BF),
    ("call", (ROW, D), BF),
    ("kt", (2, 128, ROW), BF),
    ("vt", (2, 128, ROW), BF),
    ("qh", (2, BLK, 128), BF),
    ("doh", (2, BLK, 128), BF),
    ("act", (ROW, 1024), BF),
    ("gh", (ROW, 1024), BF),
    ("g_ffn", (2, 2, 4, 4, 4, 16, 1024), BF),
    ("g_qkv", (2, 4, 2, 4, 32, 384), BF),
    ("g_out", (4, 2, 4, 16, 512), BF),
    ("outp", (512, D), F32),
    ("gnp", (512, D), F32),
    ("xo", (ROW, 1024), BF),
    ("pb", (2, ROW, BLK), BF),
    ("ds", (2, ROW, BLK), BF),
    ("dk", (ROW, 128), F32),
    ("dv", (ROW, 128), F32),
    ("dq", (128, BLK), F32),
    ("mx", (128, BLK), F32),
    ("xr", (512, 1024), BF),
    ("tab", (2, ROW, 128), F32),
    ("mr", (2, BLK, 128), F32),
    ("sm", (2, 8, 1024), F32),
    ("smr", (22, 8, 1024), F32),
    ("ln", (2, 8, 256), F32),
    ("lnr", (22, 8, 256), F32),
    ("rxs", (2, BLK, D), BF),
    ("r1z_ffn", (2, 6, 2, 4, 2, 16, 512), BF),
    ("r1x_ffn", (2, 6, 2, 2, 4, 16, 512), BF),
    ("r2_ffn", (2, 2, 6, 2, 2, 16, 512), BF),
    ("r3_ffn", (2, 3, 2, 16, 1024), BF),
    ("r1z_qkv", (2, 6, 4, 32, 256), BF),
    ("r1x_qkv", (2, 6, 4, 32, 256), BF),
    ("r2_qkv", (2, 2, 7, 32, 256), BF),
    ("r1z_out", (6, 4, 16, 256), BF),
    ("r1x_out", (6, 4, 16, 256), BF),
    ("r2_out", (2, 7, 16, 256), BF),
    ("fin_ffn", (2, 2, 16, 1024), F32),
    ("fin_qkv", (2, 32, 384), F32),
    ("fin_out", (16, 512), F32),
]
PIECE = 32
NSEM = 384
NLOC = 24


class Links:
    def __init__(self, send, recv):
        self.send, self.recv, self.count = send, recv, 0

    def copy(self, src, dst, device):
        k = self.count
        self.count += 1
        return pltpu.make_async_remote_copy(
            src_ref=src,
            dst_ref=dst,
            send_sem=self.send.at[k],
            recv_sem=self.recv.at[k],
            device_id=device,
            device_id_type=MESH,
        )


class Pieces:
    def __init__(self, links, src, dst, device, rows):
        self.whole = links.copy(src, dst, device)
        k = links.count - 1
        self.parts = []
        for at in range(0, src.shape[0], rows):
            part = pl.ds(at, rows)
            links.count = k
            self.parts.append(links.copy(src.at[part], dst.at[part], device))
        self.wait, self.wait_send, self.wait_recv = self.whole.wait, self.whole.wait_send, self.whole.wait_recv

    def start(self):
        for cp in self.parts:
            cp.start()


def add_into(dst, sources):
    if len(dst.shape) > 2:
        for i in range(dst.shape[0]):
            add_into(dst.at[i], [s.at[i] for s in sources])
        return
    total = dst[...].astype(F32)
    for s in sources:
        total = total + s[...].astype(F32)
    dst[...] = total.astype(dst.dtype)


class Ring:
    def __init__(self, links, block, pos, right, left, land):
        self.block, self.land = block, land
        self.pos = pos
        self.rt, self.lf, self.opp = (pos + 1) % 4, (pos + 3) % 4, (pos + 2) % 4
        c = links.copy
        self.early = [
            c(block(self.opp, 0), land.at[0], right),
            c(block(self.opp, 1), land.at[1], left),
            c(block(self.rt, 1), land.at[2], right),
            c(block(self.lf, 0), land.at[3], left),
        ]
        self.late = [
            c(block(self.rt, 0), land.at[4], right),
            c(block(self.lf, 1), land.at[5], left),
        ]

    def start(self):
        for c in self.early:
            c.start()

    def middle(self):
        self.early[0].wait_recv()
        add_into(self.block(self.rt, 0), [self.land.at[0]])
        self.late[0].start()
        self.early[1].wait_recv()
        add_into(self.block(self.lf, 1), [self.land.at[1]])
        self.late[1].start()

    def finish(self):
        for c in self.early[2:] + self.late:
            c.wait_recv()
        add_into(self.block(self.pos, 0), [self.land.at[4], self.land.at[3]])
        add_into(self.block(self.pos, 1), [self.land.at[2], self.land.at[5]])
        for c in self.early + self.late:
            c.wait_send()


class Reduce:
    def __init__(self, links, ref, lands, pos, at_z, at_x, last, after, col, width):
        z, x, y = pos
        every = slice(None)
        first, second = pl.ds(col, width // 2), pl.ds(col + width // 2, width // 2)
        land1z, land1x, land2z, land2x, self.land_y = lands

        def view(a, h, b, cols):
            return ref.at[a, pl.ds(h * 2, 2), b, every, cols]

        zr, zl, xr, xl = at_z(1), at_z(3), at_x(1), at_x(3)
        self.one = [
            Ring(links, lambda t, h: view(every, h, t, first), z, zr, zl, land1z),
            Ring(links, lambda t, h: view(t, h, every, second), x, xr, xl, land1x),
        ]
        self.two = [
            Ring(links, lambda t, h: view(t, h, z, first), x, xr, xl, land2z),
            Ring(links, lambda t, h: view(x, h, t, second), z, zr, zl, land2x),
        ]
        both = pl.ds(col, width)
        self.own = ref.at[x, y, z, every, both]
        self.last = [links.copy(ref.at[x, ty, z, every, both], self.land_y.at[n], d) for n, (ty, d) in enumerate(last)]
        self.after = after
        self.at = 0

    def result_into(self, dst):
        total = self.own[...].astype(F32)
        for n in range(3):
            total = total + self.land_y[n].astype(F32)
        dst[...] = total

    def step(self):
        one, two = self.one, self.two
        if self.at == 0:
            for r in one:
                r.start()
        elif self.at == 1:
            for r in one:
                r.middle()
        elif self.at == 2:
            for r, n in zip(one, two):
                r.finish()
            for n in two:
                n.start()
        elif self.at == 3:
            for r in two:
                r.middle()
        elif self.at == 4:
            for r in two:
                r.finish()
            for cp in self.last:
                cp.start()
        elif self.at == 5:
            for cp in self.last:
                cp.wait()
            self.after(self)
        self.at += 1


class ReduceShort:
    def __init__(self, links, ref, lands, pos, at_z, at_x, far, after, half):
        z, x, yl = pos
        every = slice(None)
        cols = (pl.ds(0, half), pl.ds(half, ref.shape[-1] - half))
        land1z, land1x, land2z, land2x = lands
        self.one = [
            Ring(links, lambda t, h: ref.at[every, h, t, every, cols[0]], z, at_z(1), at_z(3), land1z),
            Ring(links, lambda t, h: ref.at[t, h, every, every, cols[1]], x, at_x(1), at_x(3), land1x),
        ]
        self.own = [ref.at[x, yl, z, :, c] for c in cols]
        self.lands = (land2z, land2x)
        self.two = [
            [links.copy(ref.at[tx, ty, z, :, cols[0]], land2z.at[n], d) for n, (tx, ty, d) in enumerate(far[0])],
            [links.copy(ref.at[x, ty, tz, :, cols[1]], land2x.at[n], d) for n, (tz, ty, d) in enumerate(far[1])],
        ]
        self.cols, self.after, self.at = cols, after, 0

    def step(self):
        if self.at == 0:
            for r in self.one:
                r.start()
        elif self.at == 1:
            for r in self.one:
                r.middle()
        elif self.at == 2:
            for r, cps in zip(self.one, self.two):
                r.finish()
                for cp in cps:
                    cp.start()
        elif self.at == 3:
            for cps in self.two:
                for cp in cps:
                    cp.wait()
            self.after(self)
        self.at += 1

    def result_into(self, dst):
        for own, land, cols in zip(self.own, self.lands, self.cols):
            total = own[...].astype(F32)
            for n in range(7):
                total = total + land[n].astype(F32)
            dst[:, cols] = total


def kernel(*refs):
    small, (lens, tokens, cot, w_qkv, w_out, w_in, w_down) = refs[:6], refs[6:13]
    (o_out, o_tok, o_wqkv, o_wout, o_win, o_wdn, o_small, o_ln) = refs[13:21]
    rest = refs[21:]
    R = {name: r for (name, _, _), r in zip(SCRATCH, rest)}
    send, recv, loc = rest[len(SCRATCH) :]
    links = Links(send, recv)

    dpi, s = lax.axis_index("dp"), lax.axis_index("seq")
    z, x, yl = dpi // 8, (dpi // 2) % 4, dpi % 2
    yh, c = s // 2, s % 2
    y, y_other = yh * 2 + yl, yh * 2 + 1 - yl

    def dev(zz, xx, yy, cc):
        return ((zz % 4) * 8 + (xx % 4) * 2 + (yy % 4) % 2, ((yy % 4) // 2) * 2 + cc)

    def at_z(d):
        return dev(z + d, x, y, c)

    def at_x(d):
        return dev(z, x + d, y, c)

    def at_y(d):
        return dev(z, x, y + d, c)

    sibling = dev(z, x, y, 1 - c)
    partner = dev(z, x, y + 2, c)
    diagonal = dev(z, x, y + 2, 1 - c)

    meet = [at_x(d) for d in (1, 2, 3)] + [at_y(d) for d in (1, 2, 3)] + [sibling, diagonal]
    for d in (1, 2, 3):
        for cc in (c, 1 - c):
            meet += [dev(z + d, x, y, cc), dev(z + d, x, y + 2, cc)]
    plane = [(dz, dx) for dz in range(4) for dx in range(4) if dz or dx]
    meet += [dev(z + dz, x + dx, y, c) for dz, dx in plane if dz and dx]
    for d in (1, 2, 3):
        meet += [dev(z + d, x, y_other, c), dev(z, x + d, y_other, c)]
    meet += [dev(z, x, y + 1, 1 - c), dev(z, x, y + 3, 1 - c)]
    barrier = pltpu.get_barrier_semaphore()
    for d in meet:
        pl.semaphore_signal(barrier, inc=1, device_id=d, device_id_type=MESH)

    loads = []

    def load(src, dst):
        cp = pltpu.make_async_copy(src, dst, loc.at[len(loads)])
        cp.start()
        loads.append(cp)

    for w, sw in enumerate((s, (1 - yh) * 2 + c)):
        load(w_out.at[at256(sw), :], R["wout"].at[w])
    for a in range(2):
        for h in range(2):
            wide = pl.ds(pl.multiple_of((2 * a + c) * 1024 + h * 512, 512), 512)
            load(w_in.at[:, wide], R["win"].at[a, :, pl.ds(h * 512, 512)])
            load(w_down.at[wide, :], R["wdn"].at[a, pl.ds(h * 512, 512), :])
    for w, sw in enumerate((s, (1 - yh) * 2 + c)):
        for g in range(2):
            for j in range(3):
                cols = pl.ds(pl.multiple_of(j * 1024 + sw * 256 + g * 128, 128), 128)
                load(w_qkv.at[:, cols], R["wqkv"].at[w, g, :, pl.ds(j * 128, 128)])

    def loaded(first, count):
        for cp in loads[first : first + count]:
            cp.wait()

    own, sib = s, yh * 2 + 1 - c
    par, dia = (1 - yh) * 2 + c, (1 - yh) * 2 + 1 - c
    cal, nal = R["call"], R["nall"]
    cot_s = Pieces(links, cot, cal.at[at256(own), :], sibling, PIECE)
    cot_p = links.copy(cot, cal.at[at256(own), :], partner)
    cal[at256(own), :] = cot[...]

    vecs, row = R["vecs"], 0
    for ref in small:
        for i in range(ref.shape[0] // D):
            vecs[row : row + 1, :] = ref[pl.ds(i * D, D)].astype(F32).reshape(1, D)
            row += 1
    gain, shift = vecs[0:1, :], vecs[1:2, :]
    mr = R["mr"]

    def norm_strip(u, carry):
        rows = pl.ds(pl.multiple_of(u * 32, 32), 32)
        xin = tokens[rows, :].astype(F32)
        mean = jnp.mean(xin, axis=-1, keepdims=True)
        cen = xin - mean
        r = lax.rsqrt(jnp.mean(cen * cen, axis=-1, keepdims=True) + 1e-05)
        mr[0, rows, :] = jnp.broadcast_to(mean, (32, 128))
        mr[1, rows, :] = jnp.broadcast_to(r, (32, 128))
        nal[pl.ds(pl.multiple_of(own * 256 + u * 32, 32), 32), :] = (cen * r * gain + shift).astype(BF)
        return carry

    lax.fori_loop(0, 8, norm_strip, 0, unroll=2)
    mine = nal.at[at256(own), :]
    nrm_s = Pieces(links, mine, mine, sibling, PIECE)
    nrm_p = links.copy(mine, mine, partner)
    pl.semaphore_wait(barrier, len(meet))
    for cp in (cot_s, nrm_s, nrm_p):
        cp.start()

    sm, smr = R["sm"], R["smr"]
    sm[0] = jnp.zeros((8, 1024), F32)
    sm[0, 4:5, :] = jnp.sum(cot[...].astype(F32), axis=0, keepdims=True)

    start1 = lens[0, 0]
    start2 = start1 + lens[0, 1]
    start3 = start2 + lens[0, 2]

    def first_of(t):
        return jnp.where(t >= start3, start3, jnp.where(t >= start2, start2, jnp.where(t >= start1, start1, 0)))

    tab = R["tab"]

    def tables(u):
        rows = pl.ds(pl.multiple_of(u * 64, 64), 64)
        t = lax.broadcasted_iota(jnp.int32, (64, 128), 0) + u * 64
        lane = lax.broadcasted_iota(jnp.int32, (64, 128), 1) % HEAD
        offset = (t - first_of(t)).astype(F32)
        freq = jnp.zeros((64, 128), F32)
        for i in range(ROT // 2):
            freq = jnp.where(lane % (ROT // 2) == i, math.exp(-2.0 * i * math.log(10000.0) / ROT), freq)
        angle = offset * freq
        cosine, sine = jnp.cos(angle), jnp.sin(angle)
        tab[0, rows, :] = jnp.where(lane < ROT, cosine, 1.0)
        tab[1, rows, :] = jnp.where(lane < ROT // 2, -sine, jnp.where(lane < ROT, sine, 0.0))

    def tables_():
        loop(16, tables)

    low_lane = lax.broadcasted_iota(jnp.int32, (BLK, 128), 1) % HEAD < ROT // 2

    def rotate(val, rows, sign):
        other = jnp.where(low_lane, pltpu.roll(val, 128 - ROT // 2, 1), pltpu.roll(val, ROT // 2, 1))
        return val * tab[0, rows, :] + sign * other * tab[1, rows, :]

    win, wdn, wqkv, wout = R["win"], R["wdn"], R["wqkv"], R["wout"]
    act, gh, outp, gnp = (R[n] for n in ("act", "gh", "outp", "gnp"))
    hid, ga = outp.at[:, pl.ds(0, 256)], gnp.at[:, pl.ds(0, 256)]
    kt, vt, qh, doh = (R[n] for n in ("kt", "vt", "qh", "doh"))
    xo, xr = R["xo"], R["xr"]
    q, k, v, do = ([xo.at[:, pl.ds(g * 512 + j * 128, 128)] for g in range(2)] for j in range(4))

    def qkv_block(blk):
        rows = at256(blk)
        for g in range(2):
            yv = dot_nn(nal[rows, :], wqkv[0, g])
            for j, dst in enumerate((q, k, v)):
                b = vecs[4 + j : 5 + j, pl.ds(pl.multiple_of(s * 256 + g * 128, 128), 128)]
                part = yv[:, j * 128 : (j + 1) * 128] + b
                if j < 2:
                    part = rotate(part, rows, 1.0)
                part = part.astype(BF)
                dst[g][rows, :] = part * jnp.asarray(0.125, BF) if j == 0 else part
                if j > 0:
                    (kt, vt)[j - 1][g, :, rows] = jnp.transpose(part)

    here = pl.ds(pl.multiple_of(yh * 512, 512), 512)
    there = pl.ds(pl.multiple_of((1 - yh) * 512, 512), 512)

    def grad_mixed(rows):
        for w, (dst, at) in enumerate(((do, rows), (q, pl.ds(pl.multiple_of(rows.start + (1 - 2 * yh) * 512, 256), 256)))):
            d = dot_nt(cal[rows, :], wout[w]).astype(BF)
            for g in range(2):
                dst[g][at, :] = d[:, g * 128 : (g + 1) * 128]

    def tile(a, t, at, count):
        cs = at256(t)
        near = pl.ds(pl.multiple_of(at, 256), count)
        rows = pl.ds(pl.multiple_of(yh * 512 + at, 256), count)
        hid[near, :] = dot_nn(nal[rows, :], win[a, :, cs]) + vecs[pl.ds(7 + 2 * a + c, 1), cs]
        ga[near, :] = dot_nt(cal[rows, :], wdn[a, cs, :])

        def strip(u, total):
            r = pl.ds(pl.multiple_of(at + u * 32, 32), 32)
            h = hid[r, :]
            cdf = 0.5 + 0.5 * lax.erf(h * (1.0 / math.sqrt(2.0)))
            dens = jnp.exp(-0.5 * h * h) * (1.0 / math.sqrt(2.0 * math.pi))
            to = pl.ds(pl.multiple_of(a * 512 + at + u * 32, 32), 32)
            act[to, cs] = (h * cdf).astype(BF)
            grad = (ga[r, :] * (cdf + h * dens)).astype(BF)
            gh[to, cs] = grad
            return total + jnp.sum(grad.astype(F32).reshape(4, 8, 256), axis=0)

        total = lax.fori_loop(0, count // 32, strip, jnp.zeros((8, 256), F32), unroll=2)
        sm[0, a : a + 1, cs] += jnp.sum(total, axis=0, keepdims=True)

    def tiles(a, h):
        loaded(2 + 4 * a + 2 * h, 2)
        loop(2, lambda i: tile(a, 2 * h + i, 0, 512))

    g_ffn = R["g_ffn"]

    def grads_in(a, h):
        half = pl.ds(a * 512, 512)

        def part(m):
            res = dot_tn(nal[here, at256(m)], gh[half, pl.ds(h * 512, 512)]).astype(BF)
            g_ffn[a, 0, :, :, m, :, pl.ds(h * 512, 512)] = res.reshape(4, 4, 16, 512)

        loop(4, part)

    def grads_down(a):
        half = pl.ds(a * 512, 512)

        def part(m):
            res = dot_tn(act[half, at256(m)], cal[here, :]).astype(BF)
            g_ffn[a, 1, m] = res.reshape(4, 4, 16, 1024)

        loop(4, part)

    def ffn_out(n):
        cs = at256(n)
        top, low = pl.ds(0, 512), pl.ds(512, 512)
        outp[:, cs] = dot_nn(act[top, :], wdn[0, :, cs]) + dot_nn(act[low, :], wdn[1, :, cs])
        gnp[:, cs] = dot_nt(gh[top, :], win[0, cs, :]) + dot_nt(gh[low, :], win[1, cs, :])

    finals = []

    def put(src, dst, device, sends=None, arrives=None):
        cp = links.copy(src, dst, device)
        finals.append((cp, sends, arrives))
        if sends is None:
            cp.start()
        else:
            pl.when(sends)(cp.start)

    def keep(src, dst, here_too):
        @pl.when(here_too)
        def _():
            dst[...] = src[...]

    fin_ffn, fin_qkv, fin_out = R["fin_ffn"], R["fin_qkv"], R["fin_out"]

    def in_done(a, col, width):
        def done(red):
            cols = pl.ds(pl.multiple_of((2 * a + c) * 1024 + col, 512), width)
            fin = fin_ffn.at[a, 0, :, pl.ds(col, width)]
            red.result_into(fin)
            put(fin.at[pl.ds(pl.multiple_of((1 - c) * 8, 8), 8), :], o_win.at[:, cols], sibling)
            o_win[:, cols] = fin[pl.ds(pl.multiple_of(c * 8, 8), 8), :]

        return done

    def down_done(a):
        def done(red):
            red.result_into(fin_ffn.at[a, 1])
            to = dev(2 * a + c, x, y, z // 2)
            for h in range(2):
                rows, right = pl.ds(h * 16, 16), z % 2 == h
                here_too = (z == 2 * a + c) & (z // 2 == c)
                from_here = (z == 2 * c + h) & (z % 2 == c)
                sends = right & jnp.logical_not(here_too)
                arrives = (z // 2 == a) & jnp.logical_not(from_here)
                put(fin_ffn.at[a, 1], o_wdn.at[rows, :], to, sends, arrives)
                keep(fin_ffn.at[a, 1], o_wdn.at[rows, :], right & here_too)

        return done

    def qkv_done(g):
        def done(red):
            red.result_into(fin_qkv.at[g])
            for j in range(3):
                src_l = pl.ds(j * 128, 128)
                dst_l = pl.ds(pl.multiple_of(j * 1024 + s * 256 + g * 128, 128), 128)
                for d in (1, 2, 3):
                    t = (s + d) % 4
                    put(fin_qkv.at[g, pl.ds(pl.multiple_of(t * 8, 8), 8), src_l], o_wqkv.at[:, dst_l], (dpi, t))
                o_wqkv[:, dst_l] = fin_qkv[g, pl.ds(pl.multiple_of(s * 8, 8), 8), src_l]

        return done

    def out_done(red):
        red.result_into(fin_out)
        for cc in range(2):
            to = dev(s, x, (z // 2) * 2 + yl, cc)
            src = fin_out.at[pl.ds(cc * 8, 8), :]
            for h in range(2):
                dst, right = o_wout.at[:, pl.ds(h * 512, 512)], z % 2 == h
                here_too = (z == s) & (z // 2 == yh) & (c == cc)
                from_here = (z == 2 * yh + h) & (s == z)
                sends = right & jnp.logical_not(here_too)
                arrives = (c == cc) & jnp.logical_not(from_here)
                put(src, dst, to, sends, arrives)
                keep(src, dst, right & here_too)

    def place(yy):
        return (yy % 2) * 2 + (yy % 4) // 2

    def reduce_ffn(a, w, col, width, done):
        last = [(place(y + d), at_y(d)) for d in (1, 2, 3)]
        half = pl.ds(col // 2, width // 2)
        lands = (R["r1z_ffn"].at[a, :, w, :, :, :, half], R["r1x_ffn"].at[a, :, w, :, :, :, half])
        lands += (R["r2_ffn"].at[a, 0, :, w, :, :, half], R["r2_ffn"].at[a, 1, :, w, :, :, half])
        lands += (R["r3_ffn"].at[a, :, w, :, pl.ds(col, width)],)
        return Reduce(links, g_ffn.at[a, w], lands, (z, x, place(y)), at_z, at_x, last, done, col, width)

    def reduce_in(a, col, width):
        return reduce_ffn(a, 0, col, width, in_done(a, col, width))

    def reduce_down(a):
        return reduce_ffn(a, 1, 0, 1024, down_done(a))

    def reduce_qkv(g):
        half = 256 if g == 0 else 128
        one, two = pl.ds(0, half), pl.ds(0, 384 - half)
        lands = (R["r1z_qkv"].at[g, :, :, :, one], R["r1x_qkv"].at[g, :, :, :, two])
        lands += (R["r2_qkv"].at[g, 0, :, :, one], R["r2_qkv"].at[g, 1, :, :, two])
        return ReduceShort(links, R["g_qkv"].at[g], lands, (z, x, yl), at_z, at_x, far, qkv_done(g), half)

    def reduce_out():
        lands = (R["r1z_out"], R["r1x_out"], R["r2_out"].at[0], R["r2_out"].at[1])
        return ReduceShort(links, R["g_out"], lands, (z, x, yl), at_z, at_x, far, out_done, 256)

    far = [
        [((x + d) % 4, ty, dev(z, x + d, ry, c)) for d in range(4) for ty, ry in ((yl, y), (1 - yl, y_other)) if d or ty is not yl],
        [((z + d) % 4, ty, dev(z + d, x, ry, c)) for d in range(4) for ty, ry in ((yl, y), (1 - yl, y_other)) if d or ty is not yl],
    ]

    pb, ds = R["pb"], R["ds"]
    dk, dv, dq, mx = (R[n] for n in ("dk", "dv", "dq", "mx"))
    g_qkv, g_out = R["g_qkv"], R["g_out"]

    def attend(g, i):
        n = 256 * (i + 1)
        rows = pl.ds(256 * i, 256)
        keys = pl.ds(0, n)
        chunks = [pl.ds(j * 256, 256) for j in range(n // 256)]

        def sc(u, ch):
            return outp.at[pl.ds(u * 256, 256), ch]

        def dp(u, ch):
            return gnp.at[pl.ds(u * 256, 256), ch]

        def fold(a, op):
            return op(a.reshape(32, 8, BLK), axis=0)

        tq = lax.broadcasted_iota(jnp.int32, (1, BLK), 1) + 256 * i
        first_key = first_of(tq)

        def allowed(j):
            tk = lax.broadcasted_iota(jnp.int32, (BLK, BLK), 0) + 256 * j
            return (tk >= first_key) & (tk <= tq) if j == i else tk >= first_key

        heads = range(2)
        tops, stats = [], []
        for u in heads:
            lanes = lax.broadcasted_iota(jnp.int32, (BLK, 128), 1) // HEAD == u
            qh[u] = jnp.where(lanes, q[g][rows, :], jnp.zeros((), BF))
            doh[u] = jnp.where(lanes, do[g][rows, :], jnp.zeros((), BF))
        for u in heads:
            top = jnp.full((8, BLK), -1e30, F32)
            for j, ch in enumerate(chunks):
                a = jnp.where(allowed(j), dot_nt(k[g][ch, :], qh[u]), -1e30)
                sc(u, ch)[...] = a
                top = jnp.maximum(top, fold(a, jnp.max))
            tops.append(jnp.max(top, axis=0, keepdims=True))
        for u in heads:
            total, inner = jnp.zeros((8, BLK), F32), jnp.zeros((8, BLK), F32)
            for ch in chunks:
                gr = dot_nt(v[g][ch, :], doh[u])
                dp(u, ch)[...] = gr
                e = jnp.exp(sc(u, ch)[...] - tops[u])
                sc(u, ch)[...] = e
                total, inner = total + fold(e, jnp.sum), inner + fold(e * gr, jnp.sum)
            inv = 1.0 / jnp.sum(total, axis=0, keepdims=True)
            stats.append((inv, jnp.sum(inner, axis=0, keepdims=True) * inv))
        for u in heads:
            inv, inner = stats[u]
            for j, ch in enumerate(chunks):
                p = sc(u, ch)[...] * inv
                p_low = p.astype(BF)
                d_low = (p * (dp(u, ch)[...] - inner)).astype(BF)
                pb[u, ch, :] = p_low
                ds[u, ch, :] = d_low
                if i == 3 and u == 0:
                    dk[ch, :] = dot_nn(d_low, qh[u])
                    dv[ch, :] = dot_nn(p_low, doh[u])
                else:
                    dk[ch, :] += dot_nn(d_low, qh[u])
                    dv[ch, :] += dot_nn(p_low, doh[u])
        for u in heads:
            hr = pl.ds(u * HEAD, HEAD)
            mx[hr, :] = dot_nn(vt[g, hr, keys], pb[u, keys, :])
            dq[hr, :] = dot_nn(kt[g, hr, keys], ds[u, keys, :])

        def place_in(j, val):
            xo[rows, pl.ds(g * 512 + j * 128, 128)] = val

        place_in(3, jnp.transpose(mx[...]).astype(BF))
        grad_q = jnp.transpose(dq[...] * 0.125).astype(BF).astype(F32)
        place_in(0, rotate(grad_q, rows, -1.0).astype(BF))
        grad_k = dk[rows, :].astype(BF).astype(F32)
        place_in(1, rotate(grad_k, rows, -1.0).astype(BF))
        place_in(2, dv[rows, :].astype(BF))

    back = []

    def send_back(g):
        cols = pl.ds(g * 512, 512)
        cp = links.copy(xo.at[there, cols], xr.at[:, cols], partner)
        cp.start()
        back.append(cp)

    def qkv_grads(g):
        def part(m):
            res = dot_tn(nal[:, at256(m)], xo[:, pl.ds(g * 512, 384)]).astype(BF)
            g_qkv[g, :, :, m] = res.reshape(4, 2, 32, 384)

        loop(4, part)

    def bias_grads(g):
        total = jnp.zeros((8, 384), F32)

        def part(u, total):
            r = pl.ds(pl.multiple_of(u * 64, 64), 64)
            return total + jnp.sum(xo[r, pl.ds(g * 512, 384)].astype(F32).reshape(8, 8, 384), axis=0)

        total = jnp.sum(lax.fori_loop(0, 16, part, total), axis=0, keepdims=True)
        for j in range(3):
            for h in range(2):
                val = jnp.where(yh == h, total[:, j * 128 : (j + 1) * 128], 0.0)
                sm[0, 2 + h : 3 + h, pl.ds(j * 256 + g * 128, 128)] = val

    def out_grads(g):
        res = dot_tn(xo[:, pl.ds(g * 512 + 384, 128)], cal[...]).astype(BF).reshape(2, 2, 2, 16, 1024)
        for h in range(2):
            for n in range(2):
                g_out[pl.ds(2 * g, 2), :, 2 * h + n] = res[:, :, h, :, n * 512 : (n + 1) * 512]

    mine_at, theirs_at = c * 256, (1 - c) * 256

    def project(src, base, w, pairs, at):
        dst = pl.ds(pl.multiple_of(at, 256), 256)
        rows = pl.ds(pl.multiple_of(base + at, 256), 256)

        def part(n):
            cs = at256(n)
            add_o, add_g = outp[dst, cs], gnp[dst, cs]
            for g in pairs:
                add_o += dot_nn(src[rows, pl.ds(g * 512 + 384, 128)], wout[w, pl.ds(g * 128, 128), cs])
                add_g += dot_nt(src[rows, pl.ds(g * 512, 384)], wqkv[w, g, cs, :])
            outp[dst, cs], gnp[dst, cs] = add_o, add_g

        loop(4, part)

    stage, rxs = gh, R["rxs"]

    def stage_strip(u):
        r = pl.ds(pl.multiple_of(u * 64, 64), 64)
        rr = pl.ds(pl.multiple_of(theirs_at + u * 64, 64), 64)
        stage[r, :] = outp[rr, :].astype(BF)
        stage[pl.ds(pl.multiple_of(256 + u * 64, 64), 64), :] = gnp[rr, :].astype(BF)

    pairs_y = [at_y(d) for d in (1, 2, 3)] + [dev(z, x, y + d, 1 - c) for d in range(4)]
    plane_devices = [dev(z + dz, x + dx, y, c) for dz, dx in plane]
    early, late = (sm, smr), (R["ln"], R["lnr"])

    def exchange(level, slot, bufs, devices):
        cps = [links.copy(bufs[0].at[level], bufs[1].at[slot + d], t) for d, t in enumerate(devices)]
        for cp in cps:
            cp.start()
        return cps

    def plane_sum(bufs, cps):
        for cp in cps:
            cp.wait()
        total = bufs[0][0]
        for d in range(len(cps)):
            total = total + bufs[1][d]
        bufs[0][1] = total

    def finish_sums(bufs, cps, out):
        for cp in cps:
            cp.wait()
        same, other = bufs[0][1], bufs[1][18]
        for d in range(3):
            same = same + bufs[1][15 + d]
            other = other + bufs[1][19 + d]
        out[c], out[1 - c] = same, other

    def send_grad_mixed():
        for g in range(2):
            cp = links.copy(q[g].at[there, :], do[g].at[here, :], partner)
            cp.start()
            back_do.append(cp)

    back_do = []

    def forward(buf):
        rows = buf.at[at256(par), :]
        cp = Pieces(links, rows, rows, sibling, PIECE)
        cp.start()
        return cp

    def sum_strip(u, carry):
        sg, sb = carry
        ru = pl.ds(pl.multiple_of(u * 32, 32), 32)
        r = pl.ds(pl.multiple_of(mine_at + u * 32, 32), 32)
        gn = gnp[r, :] + rxs[1, ru, :].astype(F32)
        gnp[r, :] = gn
        hat = (tokens[ru, :].astype(F32) - mr[0, ru, 0:1]) * mr[1, ru, 0:1]
        return sg + jnp.sum((gn * hat).reshape(4, 8, D), axis=0), sb + jnp.sum(gn.reshape(4, 8, D), axis=0)

    def norm_sums():
        zero = jnp.zeros((8, D), F32)
        for r, val in enumerate(lax.fori_loop(0, 8, sum_strip, (zero, zero), unroll=2)):
            val = jnp.sum(val, axis=0, keepdims=True)
            for n in range(4):
                R["ln"][0, 4 * r + n : 4 * r + n + 1, :] = val[:, n * 256 : (n + 1) * 256]

    def last_strip(u, carry):
        ru = pl.ds(pl.multiple_of(u * 32, 32), 32)
        r = pl.ds(pl.multiple_of(mine_at + u * 32, 32), 32)
        xin = tokens[ru, :].astype(F32)
        total = outp[r, :] + rxs[0, ru, :].astype(F32)
        o_out[ru, :] = (xin + total + vecs[2:3, :] + vecs[3:4, :]).astype(BF)
        rs = mr[1, ru, 0:1]
        hat = (xin - mr[0, ru, 0:1]) * rs
        n = gnp[r, :] * gain
        grad = n - jnp.mean(n, axis=-1, keepdims=True) - hat * jnp.mean(n * hat, axis=-1, keepdims=True)
        o_tok[ru, :] = cot[ru, :].astype(F32) + grad * rs
        return carry

    own_heads = (xo, yh * 512, 0, (0, 1))

    tables_()
    loaded(0, 2)
    grad_mixed(at256(own))
    loaded(2, 2)
    loop(2, lambda i: tile(0, i, c * 256, 256))
    cot_s.wait_recv()
    grad_mixed(at256(sib))
    send_grad_mixed()
    cot_p.start()
    nrm_s.wait_recv()
    loop(2, lambda i: tile(0, i, (1 - c) * 256, 256))
    grads_in(0, 0)
    red_a = reduce_in(0, 0, 512)
    red_a.step()
    tiles(0, 1)
    grads_in(0, 1)
    red_b = reduce_in(0, 512, 512)
    red_b.step()
    grads_down(0)
    red_a.step()
    red_c = reduce_down(0)
    red_c.step()
    tiles(1, 0)
    red_b.step()
    tiles(1, 1)
    grads_in(1, 0)
    grads_in(1, 1)
    red_a.step()
    red_d = reduce_in(1, 0, 1024)
    red_d.step()
    grads_down(1)
    red_c.step()
    red_e = reduce_down(1)
    red_e.step()
    loaded(10, 12)
    qkv_block(own)
    qkv_block(sib)
    nrm_p.wait_recv()
    nrm_f = forward(nal)
    for cp in back_do:
        cp.wait_send()
    qkv_block(par)
    nrm_f.wait_recv()
    qkv_block(dia)
    for cp in back_do:
        cp.wait_recv()
    red_b.step()
    attend(0, 3)
    red_a.step()
    attend(0, 2)
    red_d.step()
    attend(0, 1)
    attend(0, 0)
    send_back(0)
    qkv_grads(0)
    red2 = reduce_qkv(0)
    red2.step()
    attend(1, 3)
    red_c.step()
    attend(1, 2)
    attend(1, 1)
    attend(1, 0)
    send_back(1)
    red_e.step()
    qkv_grads(1)
    red3 = reduce_qkv(1)
    red3.step()
    red2.step()
    cot_p.wait_recv()
    cot_f = forward(cal)
    for g in range(2):
        bias_grads(g)
    sums = exchange(0, 0, early, plane_devices)
    cot_f.wait_recv()
    for g in range(2):
        out_grads(g)
    red4 = reduce_out()
    red4.step()
    loop(2, ffn_out)
    red_d.step()
    red_a.step()
    red_b.step()
    loop(2, lambda n: ffn_out(n + 2))
    red_c.step()
    red3.step()
    red4.step()
    red2.step()
    plane_sum(early, sums)
    sums = exchange(1, 15, early, pairs_y)
    project(*own_heads, theirs_at)
    red_e.step()
    red_a.step()
    red_b.step()
    back[0].wait_recv()
    project(xr, 0, 1, (0,), theirs_at)
    red_d.step()
    red_c.step()
    project(*own_heads, mine_at)
    red3.step()
    red4.step()
    project(xr, 0, 1, (0,), mine_at)
    red_e.step()
    red_d.step()
    red2.step()
    red_b.step()
    red_c.step()
    finish_sums(early, sums, o_small)
    back[1].wait_recv()
    project(xr, 0, 1, (1,), theirs_at)
    loop(4, stage_strip)
    swap = [Pieces(links, stage.at[pl.ds(w * 256, 256), :], rxs.at[w], sibling, PIECE) for w in range(2)]
    for cp in swap:
        cp.start()
    project(xr, 0, 1, (1,), mine_at)
    red_e.step()
    red3.step()
    red_d.step()
    for cp in swap:
        cp.wait()
    norm_sums()
    sums = exchange(0, 0, late, plane_devices)
    lax.fori_loop(0, 8, last_strip, 0, unroll=2)
    red4.step()
    red_e.step()
    plane_sum(late, sums)
    sums = exchange(1, 15, late, pairs_y)
    for cp in (cot_s, nrm_s, cot_p, nrm_p, cot_f, nrm_f):
        cp.wait_send()
    finish_sums(late, sums, o_ln)
    for cp in back:
        cp.wait_send()
    for cp, sends, arrives in finals:
        if sends is None:
            cp.wait()
        else:
            pl.when(sends)(cp.wait_send)
            pl.when(arrives)(cp.wait_recv)
    assert [r.at for r in (red_a, red_b, red_c, red_d, red_e)] == [6] * 5
    assert [r.at for r in (red2, red3, red4)] == [4] * 3
    assert links.count <= NSEM, links.count


def hand_over(*refs):
    raw, small, ln = refs[:6], refs[6], refs[7]
    outs, vec, line = refs[8:14], refs[14:20], refs[20]
    for src, dst in zip(raw, outs):
        dst[...] = src[...]
    index = lax.axis_index("dp") * 4 + lax.axis_index("seq")
    for r in (3, 5):
        line[r : r + 1, 0:D] = small[0, 4:5, :] + small[1, 4:5, :]
    for r in range(2):
        for n in range(4):
            row = slice(4 * r + n, 4 * r + n + 1)
            line[r : r + 1, n * 256 : (n + 1) * 256] = ln[0, row, :] + ln[1, row, :]
    for t in range(4):
        line[4:5, t * 1024 : (t + 1) * 1024] = small[t % 2, t // 2 : t // 2 + 1, :]
        for j in range(3):
            line[2:3, pl.ds(j * 1024 + t * 256, 256)] = small[t % 2, 2 + t // 2 : 3 + t // 2, j * 256 : (j + 1) * 256]
    for r, out in enumerate(vec):
        n = out.shape[0]
        at = index * n
        part = line[r : r + 1, pl.ds(pl.multiple_of((at // 128) * 128, 128), 256)]
        part = pltpu.roll(jnp.broadcast_to(part, (8, 256)), (256 - at % 128) % 256, 1)
        out[...] = part[0, 0:n]


def on_device(tokens, lengths, ln_gain, ln_bias, w_qkv, b_qkv, w_out, b_out, w_in, b_in, w_down, b_down, cotangent):
    V = pl.BlockSpec(memory_space=pltpu.VMEM)
    H = pl.BlockSpec(memory_space=pl.ANY)
    S = pl.BlockSpec(memory_space=pltpu.SMEM)
    sds = jax.ShapeDtypeStruct
    outs = pl.pallas_call(
        kernel,
        out_shape=[
            sds((BLK, D), BF),
            sds((BLK, D), F32),
            sds((8, 3 * D), F32),
            sds((8, D), F32),
            sds((8, 4 * D), F32),
            sds((32, D), F32),
            sds((2, 8, 1024), F32),
            sds((2, 8, 256), F32),
        ],
        in_specs=[V] * 6 + [S, V, V, H, H, H, H],
        out_specs=[V] * 8,
        scratch_shapes=[pltpu.VMEM(shape, dt) for _, shape, dt in SCRATCH]
        + [pltpu.SemaphoreType.DMA((NSEM,)), pltpu.SemaphoreType.DMA((NSEM,)), pltpu.SemaphoreType.DMA((NLOC,))],
        compiler_params=pltpu.CompilerParams(collective_id=0, has_side_effects=True, vmem_limit_bytes=VMEM_LIMIT),
        name="layer",
    )(ln_gain, ln_bias, b_out, b_down, b_qkv, b_in, lengths, tokens[0], cotangent[0], w_qkv, w_out, w_in, w_down)
    vec = [sds((n // 128,), F32) for n in (D, D, 3 * D, D, 4 * D, D)]
    finals = pl.pallas_call(
        hand_over,
        out_shape=[sds(o.shape, o.dtype) for o in outs[:6]] + vec,
        in_specs=[V] * 8,
        out_specs=[V] * 12,
        scratch_shapes=[pltpu.VMEM((8, 4 * D + 128), F32)],
        name="shares",
    )(*outs)
    out, grad_tokens, g_wqkv, g_wout, g_win, g_wdn, g_gain, g_bias, g_bqkv, g_bout, g_bin, g_bdown = finals
    return (out[None], grad_tokens[None], g_gain, g_bias, g_wqkv, g_bqkv, g_wout, g_bout, g_win, g_bin, g_wdn, g_bdown)


def solution(mesh):
    act, vec, mat = P("dp", "seq", None), P(("dp", "seq")), P(("dp", "seq"), None)
    return jax.shard_map(
        on_device,
        mesh=mesh,
        in_specs=(act, P("dp", None)) + (P(),) * 10 + (act,),
        out_specs=(act, act, vec, vec, mat, vec, mat, vec, mat, vec, mat, vec),
        check_vma=False,
    )
```

```python
import math

import jax
import jax.numpy as jnp
from jax import lax
from jax.experimental import pallas as pl
from jax.experimental.pallas import tpu as pltpu
from jax.sharding import PartitionSpec as P

HEAD = 64
ROT = 16
ROW = 1024
D = 1024
BLK = 256
BF = jnp.bfloat16
F32 = jnp.float32
MESH = pl.DeviceIdType.MESH
VMEM_LIMIT = 63 * 2**20


def dot_nn(a, b):
    return lax.dot_general(a, b, (((1,), (0,)), ((), ())), preferred_element_type=F32)


def dot_nt(a, b):
    return lax.dot_general(a, b, (((1,), (1,)), ((), ())), preferred_element_type=F32)


def dot_tn(a, b):
    return lax.dot_general(a, b, (((0,), (0,)), ((), ())), preferred_element_type=F32)


def loop(count, step):
    def run(i, carry):
        step(i)
        return carry

    lax.fori_loop(0, count, run, 0)


def at256(i):
    return pl.ds(pl.multiple_of(i * 256, 256), 256)


SCRATCH = [
    ("vecs", (16, D), F32),
    ("win", (2, D, 1024), BF),
    ("wdn", (2, 1024, D), BF),
    ("wqkv", (2, 2, D, 384), BF),
    ("wout", (2, BLK, D), BF),
    ("nall", (ROW, D), BF),
    ("call", (ROW, D), BF),
    ("kt", (2, 128, ROW), BF),
    ("vt", (2, 128, ROW), BF),
    ("qh", (2, BLK, 128), BF),
    ("doh", (2, BLK, 128), BF),
    ("act", (ROW, 1024), BF),
    ("gh", (ROW, 1024), BF),
    ("g_ffn", (2, 2, 4, 4, 4, 16, 1024), BF),
    ("g_qkv", (2, 4, 2, 4, 32, 384), BF),
    ("g_out", (4, 2, 4, 16, 512), BF),
    ("outp", (512, D), F32),
    ("gnp", (512, D), F32),
    ("xo", (ROW, 1024), BF),
    ("pb", (2, ROW, BLK), BF),
    ("ds", (2, ROW, BLK), BF),
    ("dk", (ROW, 128), F32),
    ("dv", (ROW, 128), F32),
    ("dq", (128, BLK), F32),
    ("mx", (128, BLK), F32),
    ("xr", (512, 1024), BF),
    ("tab", (2, ROW, 128), F32),
    ("mr", (2, BLK, 128), F32),
    ("sm", (2, 8, 1024), F32),
    ("smr", (22, 8, 1024), F32),
    ("ln", (2, 8, 256), F32),
    ("lnr", (22, 8, 256), F32),
    ("rxs", (2, BLK, D), BF),
    ("r1z_ffn", (2, 6, 2, 4, 2, 16, 512), BF),
    ("r1x_ffn", (2, 6, 2, 2, 4, 16, 512), BF),
    ("r2_ffn", (2, 2, 6, 2, 2, 16, 512), BF),
    ("r3_ffn", (2, 3, 2, 16, 1024), BF),
    ("r1z_qkv", (2, 6, 4, 32, 256), BF),
    ("r1x_qkv", (2, 6, 4, 32, 256), BF),
    ("r2_qkv", (2, 2, 7, 32, 256), BF),
    ("r1z_out", (6, 4, 16, 256), BF),
    ("r1x_out", (6, 4, 16, 256), BF),
    ("r2_out", (2, 7, 16, 256), BF),
    ("fin_ffn", (2, 2, 16, 1024), F32),
    ("fin_qkv", (2, 32, 384), F32),
    ("fin_out", (16, 512), F32),
]
PIECE = 32
NSEND = 63
NRECV = 89
NLOC = 10


class Links:
    def __init__(self, send, recv, away):
        self.send, self.recv, self.away = send, recv, away
        self.sends = self.recvs = 0

    def new_send(self):
        self.sends += 1
        return self.send.at[self.sends - 1]

    def new_recv(self):
        self.recvs += 1
        return self.recv.at[self.recvs - 1]

    def copy(self, src, dst, device, send=None, recv=None):
        return pltpu.make_async_remote_copy(
            src_ref=src,
            dst_ref=dst,
            send_sem=self.new_send() if send is None else send,
            recv_sem=self.new_recv() if recv is None else recv,
            device_id=device,
            device_id_type=MESH,
        )

    def whole(self, view, send, recv):
        return self.copy(view, view, self.away, send, recv)


class Group:
    def __init__(self, links, view, copies):
        send, recv = links.new_send(), links.new_recv()
        self.parts = [links.copy(src, dst, d, send, recv) for src, dst, d in copies]
        whole = links.whole(view, send, recv)
        self.wait, self.wait_send, self.wait_recv = whole.wait, whole.wait_send, whole.wait_recv

    def start(self):
        for cp in self.parts:
            cp.start()


def pieces(links, src, dst, device, rows):
    cuts = [pl.ds(at, rows) for at in range(0, src.shape[0], rows)]
    return Group(links, src, [(src.at[p], dst.at[p], device) for p in cuts])


def add_into(dst, sources):
    if len(dst.shape) > 2:
        for i in range(dst.shape[0]):
            add_into(dst.at[i], [s.at[i] for s in sources])
        return
    total = dst[...].astype(F32)
    for s in sources:
        total = total + s[...].astype(F32)
    dst[...] = total.astype(dst.dtype)


class Ring:
    def __init__(self, links, block, pos, right, left, land):
        self.block, self.land = block, land
        self.pos = pos
        self.rt, self.lf, self.opp = (pos + 1) % 4, (pos + 3) % 4, (pos + 2) % 4
        send, near, far = links.new_send(), links.new_recv(), links.new_recv()

        def c(t, half, slot, device):
            return links.copy(block(t, half), land.at[slot], device, send, near if slot < 2 else far)

        self.early = [c(self.opp, 0, 0, right), c(self.opp, 1, 1, left), c(self.rt, 1, 2, right), c(self.lf, 0, 3, left)]
        self.late = [c(self.rt, 0, 4, right), c(self.lf, 1, 5, left)]
        self.near = links.whole(land.at[pl.ds(0, 2)], send, near)
        self.far = links.whole(land.at[pl.ds(2, 4)], send, far)
        self.sent = links.whole(land, send, far)

    def start(self):
        for c in self.early:
            c.start()

    def middle(self):
        self.near.wait_recv()
        add_into(self.block(self.rt, 0), [self.land.at[0]])
        self.late[0].start()
        add_into(self.block(self.lf, 1), [self.land.at[1]])
        self.late[1].start()

    def finish(self):
        self.far.wait_recv()
        add_into(self.block(self.pos, 0), [self.land.at[4], self.land.at[3]])
        add_into(self.block(self.pos, 1), [self.land.at[2], self.land.at[5]])
        self.sent.wait_send()


class Reduce:
    def __init__(self, links, ref, lands, pos, at_z, at_x, last, after, col, width):
        z, x, y = pos
        every = slice(None)
        first, second = pl.ds(col, width // 2), pl.ds(col + width // 2, width // 2)
        land1z, land1x, land2z, land2x, self.land_y = lands

        def view(a, h, b, cols):
            return ref.at[a, pl.ds(h * 2, 2), b, every, cols]

        zr, zl, xr, xl = at_z(1), at_z(3), at_x(1), at_x(3)
        self.one = [
            Ring(links, lambda t, h: view(every, h, t, first), z, zr, zl, land1z),
            Ring(links, lambda t, h: view(t, h, every, second), x, xr, xl, land1x),
        ]
        self.two = [
            Ring(links, lambda t, h: view(t, h, z, first), x, xr, xl, land2z),
            Ring(links, lambda t, h: view(x, h, t, second), z, zr, zl, land2x),
        ]
        both = pl.ds(col, width)
        self.own = ref.at[x, y, z, every, both]
        self.last = Group(links, self.land_y, [(ref.at[x, ty, z, every, both], self.land_y.at[n], d) for n, (ty, d) in enumerate(last)])
        self.after = after
        self.at = 0

    def result_into(self, dst):
        total = self.own[...].astype(F32)
        for n in range(3):
            total = total + self.land_y[n].astype(F32)
        dst[...] = total

    def step(self):
        one, two = self.one, self.two
        if self.at == 0:
            for r in one:
                r.start()
        elif self.at == 1:
            for r in one:
                r.middle()
        elif self.at == 2:
            for r, n in zip(one, two):
                r.finish()
            for n in two:
                n.start()
        elif self.at == 3:
            for r in two:
                r.middle()
        elif self.at == 4:
            for r in two:
                r.finish()
            self.last.start()
        elif self.at == 5:
            self.last.wait()
            self.after(self)
        self.at += 1


class ReduceShort:
    def __init__(self, links, ref, lands, pos, at_z, at_x, far, after, half):
        z, x, yl = pos
        every = slice(None)
        cols = (pl.ds(0, half), pl.ds(half, ref.shape[-1] - half))
        land1z, land1x, land2z, land2x = lands
        self.one = [
            Ring(links, lambda t, h: ref.at[every, h, t, every, cols[0]], z, at_z(1), at_z(3), land1z),
            Ring(links, lambda t, h: ref.at[t, h, every, every, cols[1]], x, at_x(1), at_x(3), land1x),
        ]
        self.own = [ref.at[x, yl, z, :, c] for c in cols]
        self.lands = (land2z, land2x)
        self.two = [
            Group(links, land2z, [(ref.at[tx, ty, z, :, cols[0]], land2z.at[n], d) for n, (tx, ty, d) in enumerate(far[0])]),
            Group(links, land2x, [(ref.at[x, ty, tz, :, cols[1]], land2x.at[n], d) for n, (tz, ty, d) in enumerate(far[1])]),
        ]
        self.cols, self.after, self.at = cols, after, 0

    def step(self):
        if self.at == 0:
            for r in self.one:
                r.start()
        elif self.at == 1:
            for r in self.one:
                r.middle()
        elif self.at == 2:
            for r, cps in zip(self.one, self.two):
                r.finish()
                cps.start()
        elif self.at == 3:
            for cps in self.two:
                cps.wait()
            self.after(self)
        self.at += 1

    def result_into(self, dst):
        for own, land, cols in zip(self.own, self.lands, self.cols):
            total = own[...].astype(F32)
            for n in range(7):
                total = total + land[n].astype(F32)
            dst[:, cols] = total


def kernel(*refs):
    small, (lens, tokens, cot, w_qkv, w_out, w_in, w_down) = refs[:6], refs[6:13]
    (o_out, o_tok, o_wqkv, o_wout, o_win, o_wdn, o_small, o_ln) = refs[13:21]
    rest = refs[21:]
    R = {name: r for (name, _, _), r in zip(SCRATCH, rest)}
    send, recv, loc = rest[len(SCRATCH) :]

    dpi, s = lax.axis_index("dp"), lax.axis_index("seq")
    z, x, yl = dpi // 8, (dpi // 2) % 4, dpi % 2
    yh, c = s // 2, s % 2
    y, y_other = yh * 2 + yl, yh * 2 + 1 - yl

    def dev(zz, xx, yy, cc):
        return ((zz % 4) * 8 + (xx % 4) * 2 + (yy % 4) % 2, ((yy % 4) // 2) * 2 + cc)

    def at_z(d):
        return dev(z + d, x, y, c)

    def at_x(d):
        return dev(z, x + d, y, c)

    def at_y(d):
        return dev(z, x, y + d, c)

    sibling = dev(z, x, y, 1 - c)
    partner = dev(z, x, y + 2, c)
    diagonal = dev(z, x, y + 2, 1 - c)

    links = Links(send, recv, sibling)
    meet = [at_x(d) for d in (1, 2, 3)] + [at_y(d) for d in (1, 2, 3)] + [sibling, diagonal]
    for d in (1, 2, 3):
        for cc in (c, 1 - c):
            meet += [dev(z + d, x, y, cc), dev(z + d, x, y + 2, cc)]
    plane = [(dz, dx) for dz in range(4) for dx in range(4) if dz or dx]
    meet += [dev(z + dz, x + dx, y, c) for dz, dx in plane if dz and dx]
    for d in (1, 2, 3):
        meet += [dev(z + d, x, y_other, c), dev(z, x + d, y_other, c)]
    meet += [dev(z, x, y + 1, 1 - c), dev(z, x, y + 3, 1 - c)]
    barrier = pltpu.get_barrier_semaphore()
    for d in meet:
        pl.semaphore_signal(barrier, inc=1, device_id=d, device_id_type=MESH)

    loads = []

    def load(src, dst, n):
        cp = pltpu.make_async_copy(src, dst, loc.at[n])
        cp.start()
        return cp

    heads_of = (s, (1 - yh) * 2 + c)
    for w, sw in enumerate(heads_of):
        load(w_out.at[at256(sw), :], R["wout"].at[w], 0)
    loads.append(pltpu.make_async_copy(R["wout"], R["wout"], loc.at[0]))
    for a in range(2):
        for h in range(2):
            n = 1 + 4 * a + 2 * h
            wide = pl.ds(pl.multiple_of((2 * a + c) * 1024 + h * 512, 512), 512)
            loads.append(load(w_in.at[:, wide], R["win"].at[a, :, pl.ds(h * 512, 512)], n))
            loads.append(load(w_down.at[wide, :], R["wdn"].at[a, pl.ds(h * 512, 512), :], n + 1))
    for w, sw in enumerate(heads_of):
        for g in range(2):
            for j in range(3):
                cols = pl.ds(pl.multiple_of(j * 1024 + sw * 256 + g * 128, 128), 128)
                load(w_qkv.at[:, cols], R["wqkv"].at[w, g, :, pl.ds(j * 128, 128)], 9)
    loads.append(pltpu.make_async_copy(R["wqkv"], R["wqkv"], loc.at[9]))

    def loaded(first, count):
        for cp in loads[first : first + count]:
            cp.wait()

    own, sib = s, yh * 2 + 1 - c
    par, dia = (1 - yh) * 2 + c, (1 - yh) * 2 + 1 - c
    cal, nal = R["call"], R["nall"]
    cot_s = pieces(links, cot, cal.at[at256(own), :], sibling, PIECE)
    cot_p = links.copy(cot, cal.at[at256(own), :], partner)
    cal[at256(own), :] = cot[...]

    vecs, row = R["vecs"], 0
    for ref in small:
        for i in range(ref.shape[0] // D):
            vecs[row : row + 1, :] = ref[pl.ds(i * D, D)].astype(F32).reshape(1, D)
            row += 1
    gain, shift = vecs[0:1, :], vecs[1:2, :]
    mr = R["mr"]

    def norm_strip(u, carry):
        rows = pl.ds(pl.multiple_of(u * 32, 32), 32)
        xin = tokens[rows, :].astype(F32)
        mean = jnp.mean(xin, axis=-1, keepdims=True)
        cen = xin - mean
        r = lax.rsqrt(jnp.mean(cen * cen, axis=-1, keepdims=True) + 1e-05)
        mr[0, rows, :] = jnp.broadcast_to(mean, (32, 128))
        mr[1, rows, :] = jnp.broadcast_to(r, (32, 128))
        nal[pl.ds(pl.multiple_of(own * 256 + u * 32, 32), 32), :] = (cen * r * gain + shift).astype(BF)
        return carry

    lax.fori_loop(0, 8, norm_strip, 0, unroll=2)
    mine = nal.at[at256(own), :]
    nrm_s = pieces(links, mine, mine, sibling, PIECE)
    nrm_p = links.copy(mine, mine, partner)
    pl.semaphore_wait(barrier, len(meet))
    for cp in (cot_s, nrm_s, nrm_p):
        cp.start()

    sm, smr = R["sm"], R["smr"]
    sm[0] = jnp.zeros((8, 1024), F32)
    sm[0, 4:5, :] = jnp.sum(cot[...].astype(F32), axis=0, keepdims=True)

    start1 = lens[0, 0]
    start2 = start1 + lens[0, 1]
    start3 = start2 + lens[0, 2]

    def first_of(t):
        return jnp.where(t >= start3, start3, jnp.where(t >= start2, start2, jnp.where(t >= start1, start1, 0)))

    tab = R["tab"]

    def tables(u):
        rows = pl.ds(pl.multiple_of(u * 64, 64), 64)
        t = lax.broadcasted_iota(jnp.int32, (64, 128), 0) + u * 64
        lane = lax.broadcasted_iota(jnp.int32, (64, 128), 1) % HEAD
        offset = (t - first_of(t)).astype(F32)
        freq = jnp.zeros((64, 128), F32)
        for i in range(ROT // 2):
            freq = jnp.where(lane % (ROT // 2) == i, math.exp(-2.0 * i * math.log(10000.0) / ROT), freq)
        angle = offset * freq
        cosine, sine = jnp.cos(angle), jnp.sin(angle)
        tab[0, rows, :] = jnp.where(lane < ROT, cosine, 1.0)
        tab[1, rows, :] = jnp.where(lane < ROT // 2, -sine, jnp.where(lane < ROT, sine, 0.0))

    def tables_():
        loop(16, tables)

    low_lane = lax.broadcasted_iota(jnp.int32, (BLK, 128), 1) % HEAD < ROT // 2

    def rotate(val, rows, sign):
        other = jnp.where(low_lane, pltpu.roll(val, 128 - ROT // 2, 1), pltpu.roll(val, ROT // 2, 1))
        return val * tab[0, rows, :] + sign * other * tab[1, rows, :]

    win, wdn, wqkv, wout = R["win"], R["wdn"], R["wqkv"], R["wout"]
    act, gh, outp, gnp = (R[n] for n in ("act", "gh", "outp", "gnp"))
    hid, ga = outp.at[:, pl.ds(0, 256)], gnp.at[:, pl.ds(0, 256)]
    kt, vt, qh, doh = (R[n] for n in ("kt", "vt", "qh", "doh"))
    xo, xr = R["xo"], R["xr"]
    q, k, v, do = ([xo.at[:, pl.ds(g * 512 + j * 128, 128)] for g in range(2)] for j in range(4))

    def qkv_block(blk):
        rows = at256(blk)
        for g in range(2):
            yv = dot_nn(nal[rows, :], wqkv[0, g])
            for j, dst in enumerate((q, k, v)):
                b = vecs[4 + j : 5 + j, pl.ds(pl.multiple_of(s * 256 + g * 128, 128), 128)]
                part = yv[:, j * 128 : (j + 1) * 128] + b
                if j < 2:
                    part = rotate(part, rows, 1.0)
                part = part.astype(BF)
                dst[g][rows, :] = part * jnp.asarray(0.125, BF) if j == 0 else part
                if j > 0:
                    (kt, vt)[j - 1][g, :, rows] = jnp.transpose(part)

    here = pl.ds(pl.multiple_of(yh * 512, 512), 512)
    there = pl.ds(pl.multiple_of((1 - yh) * 512, 512), 512)

    def grad_mixed(rows):
        for w, (dst, at) in enumerate(((do, rows), (q, pl.ds(pl.multiple_of(rows.start + (1 - 2 * yh) * 512, 256), 256)))):
            d = dot_nt(cal[rows, :], wout[w]).astype(BF)
            for g in range(2):
                dst[g][at, :] = d[:, g * 128 : (g + 1) * 128]

    def tile(a, t, at, count):
        cs = at256(t)
        near = pl.ds(pl.multiple_of(at, 256), count)
        rows = pl.ds(pl.multiple_of(yh * 512 + at, 256), count)
        hid[near, :] = dot_nn(nal[rows, :], win[a, :, cs]) + vecs[pl.ds(7 + 2 * a + c, 1), cs]
        ga[near, :] = dot_nt(cal[rows, :], wdn[a, cs, :])

        def strip(u, total):
            r = pl.ds(pl.multiple_of(at + u * 32, 32), 32)
            h = hid[r, :]
            cdf = 0.5 + 0.5 * lax.erf(h * (1.0 / math.sqrt(2.0)))
            dens = jnp.exp(-0.5 * h * h) * (1.0 / math.sqrt(2.0 * math.pi))
            to = pl.ds(pl.multiple_of(a * 512 + at + u * 32, 32), 32)
            act[to, cs] = (h * cdf).astype(BF)
            grad = (ga[r, :] * (cdf + h * dens)).astype(BF)
            gh[to, cs] = grad
            return total + jnp.sum(grad.astype(F32).reshape(4, 8, 256), axis=0)

        total = lax.fori_loop(0, count // 32, strip, jnp.zeros((8, 256), F32), unroll=2)
        sm[0, a : a + 1, cs] += jnp.sum(total, axis=0, keepdims=True)

    def tiles(a, h):
        loaded(1 + 4 * a + 2 * h, 2)
        loop(2, lambda i: tile(a, 2 * h + i, 0, 512))

    g_ffn = R["g_ffn"]

    def grads_in(a, col, width):
        half = pl.ds(a * 512, 512)

        def part(m):
            res = dot_tn(nal[here, at256(m)], gh[half, pl.ds(col, width)]).astype(BF)
            g_ffn[a, 0, :, :, m, :, pl.ds(col, width)] = res.reshape(4, 4, 16, width)

        loop(4, part)

    def grads_down(a):
        half = pl.ds(a * 512, 512)

        def part(m):
            res = dot_tn(act[half, at256(m)], cal[here, :]).astype(BF)
            g_ffn[a, 1, m] = res.reshape(4, 4, 16, 1024)

        loop(4, part)

    finals = []

    shared = [(links.new_send(), links.new_recv()) for _ in range(2)]

    def put(src, dst, device, sends, arrives):
        cp = links.copy(src, dst, device)
        finals.append((cp, sends, arrives))
        pl.when(sends)(cp.start)

    def keep(src, dst, here_too):
        @pl.when(here_too)
        def _():
            dst[...] = src[...]

    fin_ffn, fin_qkv, fin_out = R["fin_ffn"], R["fin_qkv"], R["fin_out"]

    def in_done(a, col, width):
        def done(red):
            cols = pl.ds(pl.multiple_of((2 * a + c) * 1024 + col, 512), width)
            fin = fin_ffn.at[a, 0, :, pl.ds(col, width)]
            red.result_into(fin)
            links.copy(fin.at[pl.ds(pl.multiple_of((1 - c) * 8, 8), 8), :], o_win.at[:, cols], sibling, *shared[0]).start()
            o_win[:, cols] = fin[pl.ds(pl.multiple_of(c * 8, 8), 8), :]

        return done

    def down_done(a):
        def done(red):
            red.result_into(fin_ffn.at[a, 1])
            to = dev(2 * a + c, x, y, z // 2)
            for h in range(2):
                rows, right = pl.ds(h * 16, 16), z % 2 == h
                here_too = (z == 2 * a + c) & (z // 2 == c)
                from_here = (z == 2 * c + h) & (z % 2 == c)
                sends = right & jnp.logical_not(here_too)
                arrives = (z // 2 == a) & jnp.logical_not(from_here)
                put(fin_ffn.at[a, 1], o_wdn.at[rows, :], to, sends, arrives)
                keep(fin_ffn.at[a, 1], o_wdn.at[rows, :], right & here_too)

        return done

    def qkv_done(g):
        def done(red):
            red.result_into(fin_qkv.at[g])
            for j in range(3):
                src_l = pl.ds(j * 128, 128)
                dst_l = pl.ds(pl.multiple_of(j * 1024 + s * 256 + g * 128, 128), 128)
                for d in (1, 2, 3):
                    t = (s + d) % 4
                    src = fin_qkv.at[g, pl.ds(pl.multiple_of(t * 8, 8), 8), src_l]
                    links.copy(src, o_wqkv.at[:, dst_l], (dpi, t), *shared[1]).start()
                o_wqkv[:, dst_l] = fin_qkv[g, pl.ds(pl.multiple_of(s * 8, 8), 8), src_l]

        return done

    def out_done(red):
        red.result_into(fin_out)
        for cc in range(2):
            to = dev(s, x, (z // 2) * 2 + yl, cc)
            src = fin_out.at[pl.ds(cc * 8, 8), :]
            for h in range(2):
                dst, right = o_wout.at[:, pl.ds(h * 512, 512)], z % 2 == h
                here_too = (z == s) & (z // 2 == yh) & (c == cc)
                from_here = (z == 2 * yh + h) & (s == z)
                sends = right & jnp.logical_not(here_too)
                arrives = (c == cc) & jnp.logical_not(from_here)
                put(src, dst, to, sends, arrives)
                keep(src, dst, right & here_too)

    def place(yy):
        return (yy % 2) * 2 + (yy % 4) // 2

    def reduce_ffn(a, w, col, width, done):
        last = [(place(y + d), at_y(d)) for d in (1, 2, 3)]
        half = pl.ds(col // 2, width // 2)
        lands = (R["r1z_ffn"].at[a, :, w, :, :, :, half], R["r1x_ffn"].at[a, :, w, :, :, :, half])
        lands += (R["r2_ffn"].at[a, 0, :, w, :, :, half], R["r2_ffn"].at[a, 1, :, w, :, :, half])
        lands += (R["r3_ffn"].at[a, :, w, :, pl.ds(col, width)],)
        return Reduce(links, g_ffn.at[a, w], lands, (z, x, place(y)), at_z, at_x, last, done, col, width)

    def reduce_in(a, col, width):
        return reduce_ffn(a, 0, col, width, in_done(a, col, width))

    def reduce_down(a):
        return reduce_ffn(a, 1, 0, 1024, down_done(a))

    def reduce_qkv(g):
        half = 256 if g == 0 else 128
        one, two = pl.ds(0, half), pl.ds(0, 384 - half)
        lands = (R["r1z_qkv"].at[g, :, :, :, one], R["r1x_qkv"].at[g, :, :, :, two])
        lands += (R["r2_qkv"].at[g, 0, :, :, one], R["r2_qkv"].at[g, 1, :, :, two])
        return ReduceShort(links, R["g_qkv"].at[g], lands, (z, x, yl), at_z, at_x, far, qkv_done(g), half)

    def reduce_out():
        lands = (R["r1z_out"], R["r1x_out"], R["r2_out"].at[0], R["r2_out"].at[1])
        return ReduceShort(links, R["g_out"], lands, (z, x, yl), at_z, at_x, far, out_done, 256)

    far = [
        [((x + d) % 4, ty, dev(z, x + d, ry, c)) for d in range(4) for ty, ry in ((yl, y), (1 - yl, y_other)) if d or ty is not yl],
        [((z + d) % 4, ty, dev(z + d, x, ry, c)) for d in range(4) for ty, ry in ((yl, y), (1 - yl, y_other)) if d or ty is not yl],
    ]

    pb, ds = R["pb"], R["ds"]
    dk, dv, dq, mx = (R[n] for n in ("dk", "dv", "dq", "mx"))
    g_qkv, g_out = R["g_qkv"], R["g_out"]

    def attend(g, i):
        n = 256 * (i + 1)
        rows = pl.ds(256 * i, 256)
        keys = pl.ds(0, n)
        chunks = [pl.ds(j * 256, 256) for j in range(n // 256)]

        def sc(u, ch):
            return outp.at[pl.ds(u * 256, 256), ch]

        def dp(u, ch):
            return gnp.at[pl.ds(u * 256, 256), ch]

        def fold(a, op):
            return op(a.reshape(32, 8, BLK), axis=0)

        tq = lax.broadcasted_iota(jnp.int32, (1, BLK), 1) + 256 * i
        first_key = first_of(tq)

        def allowed(j):
            tk = lax.broadcasted_iota(jnp.int32, (BLK, BLK), 0) + 256 * j
            return (tk >= first_key) & (tk <= tq) if j == i else tk >= first_key

        heads = range(2)
        tops, stats = [], []
        for u in heads:
            lanes = lax.broadcasted_iota(jnp.int32, (BLK, 128), 1) // HEAD == u
            qh[u] = jnp.where(lanes, q[g][rows, :], jnp.zeros((), BF))
            doh[u] = jnp.where(lanes, do[g][rows, :], jnp.zeros((), BF))
        for u in heads:
            top = jnp.full((8, BLK), -1e30, F32)
            for j, ch in enumerate(chunks):
                a = jnp.where(allowed(j), dot_nt(k[g][ch, :], qh[u]), -1e30)
                sc(u, ch)[...] = a
                top = jnp.maximum(top, fold(a, jnp.max))
            tops.append(jnp.max(top, axis=0, keepdims=True))
        for u in heads:
            total, inner = jnp.zeros((8, BLK), F32), jnp.zeros((8, BLK), F32)
            for ch in chunks:
                gr = dot_nt(v[g][ch, :], doh[u])
                dp(u, ch)[...] = gr
                e = jnp.exp(sc(u, ch)[...] - tops[u])
                sc(u, ch)[...] = e
                total, inner = total + fold(e, jnp.sum), inner + fold(e * gr, jnp.sum)
            inv = 1.0 / jnp.sum(total, axis=0, keepdims=True)
            stats.append((inv, jnp.sum(inner, axis=0, keepdims=True) * inv))
        for u in heads:
            inv, inner = stats[u]
            for j, ch in enumerate(chunks):
                p = sc(u, ch)[...] * inv
                p_low = p.astype(BF)
                d_low = (p * (dp(u, ch)[...] - inner)).astype(BF)
                pb[u, ch, :] = p_low
                ds[u, ch, :] = d_low
                if i == 3 and u == 0:
                    dk[ch, :] = dot_nn(d_low, qh[u])
                    dv[ch, :] = dot_nn(p_low, doh[u])
                else:
                    dk[ch, :] += dot_nn(d_low, qh[u])
                    dv[ch, :] += dot_nn(p_low, doh[u])
        for u in heads:
            hr = pl.ds(u * HEAD, HEAD)
            mx[hr, :] = dot_nn(vt[g, hr, keys], pb[u, keys, :])
            dq[hr, :] = dot_nn(kt[g, hr, keys], ds[u, keys, :])

        def place_in(j, val):
            xo[rows, pl.ds(g * 512 + j * 128, 128)] = val

        place_in(3, jnp.transpose(mx[...]).astype(BF))
        grad_q = jnp.transpose(dq[...] * 0.125).astype(BF).astype(F32)
        place_in(0, rotate(grad_q, rows, -1.0).astype(BF))
        grad_k = dk[rows, :].astype(BF).astype(F32)
        place_in(1, rotate(grad_k, rows, -1.0).astype(BF))
        place_in(2, dv[rows, :].astype(BF))

    back = []

    def send_back(g):
        cols = pl.ds(g * 512, 512)
        cp = links.copy(xo.at[there, cols], xr.at[:, cols], partner)
        cp.start()
        back.append(cp)

    def qkv_grads(g):
        def part(m):
            res = dot_tn(nal[:, at256(m)], xo[:, pl.ds(g * 512, 384)]).astype(BF)
            g_qkv[g, :, :, m] = res.reshape(4, 2, 32, 384)

        loop(4, part)

    def bias_grads(g):
        total = jnp.zeros((8, 384), F32)

        def part(u, total):
            r = pl.ds(pl.multiple_of(u * 64, 64), 64)
            return total + jnp.sum(xo[r, pl.ds(g * 512, 384)].astype(F32).reshape(8, 8, 384), axis=0)

        total = jnp.sum(lax.fori_loop(0, 16, part, total), axis=0, keepdims=True)
        for j in range(3):
            for h in range(2):
                val = jnp.where(yh == h, total[:, j * 128 : (j + 1) * 128], 0.0)
                sm[0, 2 + h : 3 + h, pl.ds(j * 256 + g * 128, 128)] = val

    def out_grads(g):
        res = dot_tn(xo[:, pl.ds(g * 512 + 384, 128)], cal[...]).astype(BF).reshape(2, 2, 2, 16, 1024)
        for h in range(2):
            for n in range(2):
                g_out[pl.ds(2 * g, 2), :, 2 * h + n] = res[:, :, h, :, n * 512 : (n + 1) * 512]

    mine_at, theirs_at = c * 256, (1 - c) * 256

    def outputs(n):
        cs = at256(n)
        top, low, every = pl.ds(0, 512), pl.ds(512, 512), pl.ds(0, 512)
        o = dot_nn(act[top, :], wdn[0, :, cs]) + dot_nn(act[low, :], wdn[1, :, cs])
        g = dot_nt(gh[top, :], win[0, cs, :]) + dot_nt(gh[low, :], win[1, cs, :])
        for src, rows, w, p in ((xo, here, 0, 0), (xo, here, 0, 1), (xr, every, 1, 0)):
            o += dot_nn(src[rows, pl.ds(p * 512 + 384, 128)], wout[w, pl.ds(p * 128, 128), cs])
            g += dot_nt(src[rows, pl.ds(p * 512, 384)], wqkv[w, p, cs, :])
        outp[:, cs], gnp[:, cs] = o, g

    def project_last(at):
        rows = pl.ds(pl.multiple_of(at, 256), 256)

        def part(n):
            cs = at256(n)
            outp[rows, cs] += dot_nn(xr[rows, pl.ds(896, 128)], wout[1, pl.ds(128, 128), cs])
            gnp[rows, cs] += dot_nt(xr[rows, pl.ds(512, 384)], wqkv[1, 1, cs, :])

        loop(4, part)

    stage, rxs = gh, R["rxs"]

    def stage_strip(u):
        r = pl.ds(pl.multiple_of(u * 64, 64), 64)
        rr = pl.ds(pl.multiple_of(theirs_at + u * 64, 64), 64)
        stage[r, :] = outp[rr, :].astype(BF)
        stage[pl.ds(pl.multiple_of(256 + u * 64, 64), 64), :] = gnp[rr, :].astype(BF)

    pairs_y = [at_y(d) for d in (1, 2, 3)] + [dev(z, x, y + d, 1 - c) for d in range(4)]
    plane_devices = [dev(z + dz, x + dx, y, c) for dz, dx in plane]
    early, late = (sm, smr), (R["ln"], R["lnr"])

    def exchange(level, slot, bufs, devices):
        view = bufs[1].at[pl.ds(slot, len(devices))]
        cps = Group(links, view, [(bufs[0].at[level], bufs[1].at[slot + d], t) for d, t in enumerate(devices)])
        cps.start()
        return cps

    def plane_sum(bufs, cps):
        cps.wait()
        total = bufs[0][0]
        for d in range(15):
            total = total + bufs[1][d]
        bufs[0][1] = total

    def finish_sums(bufs, cps, out):
        cps.wait()
        same, other = bufs[0][1], bufs[1][18]
        for d in range(3):
            same = same + bufs[1][15 + d]
            other = other + bufs[1][19 + d]
        out[c], out[1 - c] = same, other

    def send_grad_mixed():
        for g in range(2):
            cp = links.copy(q[g].at[there, :], do[g].at[here, :], partner)
            cp.start()
            back_do.append(cp)

    back_do = []

    def forward(buf):
        rows = buf.at[at256(par), :]
        cp = pieces(links, rows, rows, sibling, PIECE)
        cp.start()
        return cp

    def sum_strip(u, carry):
        sg, sb = carry
        ru = pl.ds(pl.multiple_of(u * 32, 32), 32)
        r = pl.ds(pl.multiple_of(mine_at + u * 32, 32), 32)
        gn = gnp[r, :] + rxs[1, ru, :].astype(F32)
        gnp[r, :] = gn
        hat = (tokens[ru, :].astype(F32) - mr[0, ru, 0:1]) * mr[1, ru, 0:1]
        return sg + jnp.sum((gn * hat).reshape(4, 8, D), axis=0), sb + jnp.sum(gn.reshape(4, 8, D), axis=0)

    def norm_sums():
        zero = jnp.zeros((8, D), F32)
        for r, val in enumerate(lax.fori_loop(0, 8, sum_strip, (zero, zero), unroll=2)):
            val = jnp.sum(val, axis=0, keepdims=True)
            for n in range(4):
                R["ln"][0, 4 * r + n : 4 * r + n + 1, :] = val[:, n * 256 : (n + 1) * 256]

    def last_strip(u, carry):
        ru = pl.ds(pl.multiple_of(u * 32, 32), 32)
        r = pl.ds(pl.multiple_of(mine_at + u * 32, 32), 32)
        xin = tokens[ru, :].astype(F32)
        total = outp[r, :] + rxs[0, ru, :].astype(F32)
        o_out[ru, :] = (xin + total + vecs[2:3, :] + vecs[3:4, :]).astype(BF)
        rs = mr[1, ru, 0:1]
        hat = (xin - mr[0, ru, 0:1]) * rs
        n = gnp[r, :] * gain
        grad = n - jnp.mean(n, axis=-1, keepdims=True) - hat * jnp.mean(n * hat, axis=-1, keepdims=True)
        o_tok[ru, :] = cot[ru, :].astype(F32) + grad * rs
        return carry

    tables_()
    loaded(0, 1)
    grad_mixed(at256(own))
    loaded(1, 2)
    loop(2, lambda i: tile(0, i, c * 256, 256))
    cot_s.wait_recv()
    grad_mixed(at256(sib))
    send_grad_mixed()
    cot_p.start()
    nrm_s.wait_recv()
    loop(2, lambda i: tile(0, i, (1 - c) * 256, 256))
    grads_in(0, 0, 512)
    red_a = reduce_in(0, 0, 512)
    red_a.step()
    tiles(0, 1)
    grads_in(0, 512, 512)
    red_b = reduce_in(0, 512, 512)
    red_b.step()
    grads_down(0)
    red_a.step()
    red_c = reduce_down(0)
    red_c.step()
    tiles(1, 0)
    red_b.step()
    tiles(1, 1)
    grads_in(1, 0, 1024)
    red_a.step()
    red_d = reduce_in(1, 0, 1024)
    red_d.step()
    grads_down(1)
    red_c.step()
    red_e = reduce_down(1)
    red_e.step()
    loaded(9, 1)
    qkv_block(own)
    qkv_block(sib)
    nrm_p.wait_recv()
    nrm_f = forward(nal)
    for cp in back_do:
        cp.wait_send()
    qkv_block(par)
    nrm_f.wait_recv()
    qkv_block(dia)
    for cp in back_do:
        cp.wait_recv()
    red_b.step()
    attend(0, 3)
    red_a.step()
    attend(0, 2)
    red_d.step()
    attend(0, 1)
    attend(0, 0)
    send_back(0)
    qkv_grads(0)
    red2 = reduce_qkv(0)
    red2.step()
    attend(1, 3)
    red_c.step()
    attend(1, 2)
    attend(1, 1)
    attend(1, 0)
    send_back(1)
    red_e.step()
    qkv_grads(1)
    red3 = reduce_qkv(1)
    red3.step()
    red2.step()
    cot_p.wait_recv()
    cot_f = forward(cal)
    for g in range(2):
        bias_grads(g)
    sums = exchange(0, 0, early, plane_devices)
    cot_f.wait_recv()
    for g in range(2):
        out_grads(g)
    red4 = reduce_out()
    red4.step()
    red_d.step()
    red_a.step()
    red_b.step()
    back[0].wait_recv()
    loop(2, outputs)
    red_c.step()
    red3.step()
    red4.step()
    red2.step()
    plane_sum(early, sums)
    sums = exchange(1, 15, early, pairs_y)
    red_e.step()
    red_a.step()
    red_b.step()
    loop(2, lambda n: outputs(n + 2))
    red_d.step()
    red_c.step()
    red3.step()
    red4.step()
    red_e.step()
    red_d.step()
    red2.step()
    red_b.step()
    red_c.step()
    finish_sums(early, sums, o_small)
    back[1].wait_recv()
    project_last(theirs_at)
    loop(4, stage_strip)
    swap = [pieces(links, stage.at[pl.ds(w * 256, 256), :], rxs.at[w], sibling, PIECE) for w in range(2)]
    for cp in swap:
        cp.start()
    project_last(mine_at)
    red_e.step()
    red3.step()
    red_d.step()
    for cp in swap:
        cp.wait()
    norm_sums()
    sums = exchange(0, 0, late, plane_devices)
    lax.fori_loop(0, 8, last_strip, 0, unroll=2)
    red4.step()
    red_e.step()
    plane_sum(late, sums)
    sums = exchange(1, 15, late, pairs_y)
    for cp in (cot_s, nrm_s, cot_p, nrm_p, cot_f, nrm_f):
        cp.wait_send()
    finish_sums(late, sums, o_ln)
    for cp in back:
        cp.wait_send()
    links.whole(o_win.at[:, pl.ds(0, 2048)], *shared[0]).wait()
    links.whole(o_wqkv.at[:, pl.ds(0, 2304)], *shared[1]).wait()
    for cp, sends, arrives in finals:
        pl.when(sends)(cp.wait_send)
        pl.when(arrives)(cp.wait_recv)
    assert [r.at for r in (red_a, red_b, red_c, red_d, red_e)] == [6] * 5
    assert [r.at for r in (red2, red3, red4)] == [4] * 3
    assert (links.sends, links.recvs) == (NSEND, NRECV), (links.sends, links.recvs)


def hand_over(*refs):
    raw, small, ln = refs[:6], refs[6], refs[7]
    outs, vec, line = refs[8:14], refs[14:20], refs[20]
    for src, dst in zip(raw, outs):
        dst[...] = src[...]
    index = lax.axis_index("dp") * 4 + lax.axis_index("seq")
    for r in (3, 5):
        line[r : r + 1, 0:D] = small[0, 4:5, :] + small[1, 4:5, :]
    for r in range(2):
        for n in range(4):
            row = slice(4 * r + n, 4 * r + n + 1)
            line[r : r + 1, n * 256 : (n + 1) * 256] = ln[0, row, :] + ln[1, row, :]
    for t in range(4):
        line[4:5, t * 1024 : (t + 1) * 1024] = small[t % 2, t // 2 : t // 2 + 1, :]
        for j in range(3):
            line[2:3, pl.ds(j * 1024 + t * 256, 256)] = small[t % 2, 2 + t // 2 : 3 + t // 2, j * 256 : (j + 1) * 256]
    for r, out in enumerate(vec):
        n = out.shape[0]
        at = index * n
        part = line[r : r + 1, pl.ds(pl.multiple_of((at // 128) * 128, 128), 256)]
        part = pltpu.roll(jnp.broadcast_to(part, (8, 256)), (256 - at % 128) % 256, 1)
        out[...] = part[0, 0:n]


def on_device(tokens, lengths, ln_gain, ln_bias, w_qkv, b_qkv, w_out, b_out, w_in, b_in, w_down, b_down, cotangent):
    V = pl.BlockSpec(memory_space=pltpu.VMEM)
    H = pl.BlockSpec(memory_space=pl.ANY)
    S = pl.BlockSpec(memory_space=pltpu.SMEM)
    sds = jax.ShapeDtypeStruct
    outs = pl.pallas_call(
        kernel,
        out_shape=[
            sds((BLK, D), BF),
            sds((BLK, D), F32),
            sds((8, 3 * D), F32),
            sds((8, D), F32),
            sds((8, 4 * D), F32),
            sds((32, D), F32),
            sds((2, 8, 1024), F32),
            sds((2, 8, 256), F32),
        ],
        in_specs=[V] * 6 + [S, V, V, H, H, H, H],
        out_specs=[V] * 8,
        scratch_shapes=[pltpu.VMEM(shape, dt) for _, shape, dt in SCRATCH]
        + [pltpu.SemaphoreType.DMA((NSEND,)), pltpu.SemaphoreType.DMA((NRECV,)), pltpu.SemaphoreType.DMA((NLOC,))],
        compiler_params=pltpu.CompilerParams(collective_id=0, has_side_effects=True, vmem_limit_bytes=VMEM_LIMIT),
        name="layer",
    )(ln_gain, ln_bias, b_out, b_down, b_qkv, b_in, lengths, tokens[0], cotangent[0], w_qkv, w_out, w_in, w_down)
    vec = [sds((n // 128,), F32) for n in (D, D, 3 * D, D, 4 * D, D)]
    finals = pl.pallas_call(
        hand_over,
        out_shape=[sds(o.shape, o.dtype) for o in outs[:6]] + vec,
        in_specs=[V] * 8,
        out_specs=[V] * 12,
        scratch_shapes=[pltpu.VMEM((8, 4 * D + 128), F32)],
        name="shares",
    )(*outs)
    out, grad_tokens, g_wqkv, g_wout, g_win, g_wdn, g_gain, g_bias, g_bqkv, g_bout, g_bin, g_bdown = finals
    return (out[None], grad_tokens[None], g_gain, g_bias, g_wqkv, g_bqkv, g_wout, g_bout, g_win, g_bin, g_wdn, g_bdown)


def solution(mesh):
    act, vec, mat = P("dp", "seq", None), P(("dp", "seq")), P(("dp", "seq"), None)
    return jax.shard_map(
        on_device,
        mesh=mesh,
        in_specs=(act, P("dp", None)) + (P(),) * 10 + (act,),
        out_specs=(act, act, vec, vec, mat, vec, mat, vec, mat, vec, mat, vec),
        check_vma=False,
    )
```

```python
import math

import jax
import jax.numpy as jnp
from jax import lax
from jax.experimental import pallas as pl
from jax.experimental.pallas import tpu as pltpu
from jax.sharding import PartitionSpec as P

HEAD = 64
ROT = 16
ROW = 1024
D = 1024
BLK = 256
BF = jnp.bfloat16
F32 = jnp.float32
MESH = pl.DeviceIdType.MESH
VMEM_LIMIT = 63 * 2**20


def dot_nn(a, b):
    return lax.dot_general(a, b, (((1,), (0,)), ((), ())), preferred_element_type=F32)


def dot_nt(a, b):
    return lax.dot_general(a, b, (((1,), (1,)), ((), ())), preferred_element_type=F32)


def dot_tn(a, b):
    return lax.dot_general(a, b, (((0,), (0,)), ((), ())), preferred_element_type=F32)


def loop(count, step):
    def run(i, carry):
        step(i)
        return carry

    lax.fori_loop(0, count, run, 0)


def at256(i):
    return pl.ds(pl.multiple_of(i * 256, 256), 256)


SCRATCH = [
    ("vecs", (16, D), F32),
    ("win", (2, D, 1024), BF),
    ("wdn", (2, 1024, D), BF),
    ("wqkv", (2, 2, D, 384), BF),
    ("wout", (2, BLK, D), BF),
    ("nall", (ROW, D), BF),
    ("call", (ROW, D), BF),
    ("kt", (2, 128, ROW), BF),
    ("vt", (2, 128, ROW), BF),
    ("qh", (2, BLK, 128), BF),
    ("doh", (2, BLK, 128), BF),
    ("act", (ROW, 1024), BF),
    ("gh", (ROW, 1024), BF),
    ("g_ffn", (2, 2, 4, 4, 4, 16, 1024), BF),
    ("g_qkv", (2, 4, 2, 4, 32, 384), BF),
    ("g_out", (4, 2, 4, 16, 512), BF),
    ("outp", (512, D), F32),
    ("gnp", (512, D), F32),
    ("xo", (ROW, 1024), BF),
    ("pb", (2, ROW, BLK), BF),
    ("ds", (2, ROW, BLK), BF),
    ("dk", (ROW, 128), F32),
    ("dv", (ROW, 128), F32),
    ("dq", (128, BLK), F32),
    ("mx", (128, BLK), F32),
    ("xr", (512, 1024), BF),
    ("tab", (2, ROW, 128), F32),
    ("mr", (2, BLK, 128), F32),
    ("sm", (1, 8, 1024), F32),
    ("sp", (1, 16, 256), BF),
    ("spr", (15, 16, 256), BF),
    ("sq", (1, 16, 256), F32),
    ("sqr", (7, 16, 256), F32),
    ("ln", (16, 1, 128), F32),
    ("lnr", (15, 1, 128), F32),
    ("lnp", (1, 1, 128), F32),
    ("lnq", (7, 1, 128), F32),
    ("tsib", (BLK, D), BF),
    ("msib", (2, BLK, 128), F32),
    ("rxs", (2, BLK, D), BF),
    ("r1z_ffn", (2, 6, 2, 4, 2, 16, 512), BF),
    ("r1x_ffn", (2, 6, 2, 2, 4, 16, 512), BF),
    ("r2_ffn", (2, 2, 6, 2, 2, 16, 512), BF),
    ("r3_ffn", (2, 3, 2, 16, 1024), BF),
    ("r1z_qkv", (2, 6, 4, 32, 256), BF),
    ("r1x_qkv", (2, 6, 4, 32, 256), BF),
    ("r2_qkv", (2, 2, 7, 32, 256), BF),
    ("r1z_out", (6, 4, 16, 256), BF),
    ("r1x_out", (6, 4, 16, 256), BF),
    ("r2_out", (2, 7, 16, 256), BF),
    ("fin_ffn", (2, 2, 16, 1024), F32),
    ("fin_qkv", (2, 32, 384), F32),
    ("fin_out", (16, 512), F32),
]
PIECE = 32
NSEND = 65
NRECV = 91
NLOC = 10


class Links:
    def __init__(self, send, recv, away):
        self.send, self.recv, self.away = send, recv, away
        self.sends = self.recvs = 0

    def new_send(self):
        self.sends += 1
        return self.send.at[self.sends - 1]

    def new_recv(self):
        self.recvs += 1
        return self.recv.at[self.recvs - 1]

    def copy(self, src, dst, device, send=None, recv=None):
        return pltpu.make_async_remote_copy(
            src_ref=src,
            dst_ref=dst,
            send_sem=self.new_send() if send is None else send,
            recv_sem=self.new_recv() if recv is None else recv,
            device_id=device,
            device_id_type=MESH,
        )

    def whole(self, view, send, recv):
        return self.copy(view, view, self.away, send, recv)


class Group:
    def __init__(self, links, view, copies):
        send, recv = links.new_send(), links.new_recv()
        self.parts = [links.copy(src, dst, d, send, recv) for src, dst, d in copies]
        whole = links.whole(view, send, recv)
        self.wait, self.wait_send, self.wait_recv = whole.wait, whole.wait_send, whole.wait_recv

    def start(self):
        for cp in self.parts:
            cp.start()


def pieces(links, src, dst, device, rows):
    cuts = [pl.ds(at, rows) for at in range(0, src.shape[0], rows)]
    return Group(links, src, [(src.at[p], dst.at[p], device) for p in cuts])


def add_into(dst, sources):
    if len(dst.shape) > 2:
        for i in range(dst.shape[0]):
            add_into(dst.at[i], [s.at[i] for s in sources])
        return
    total = dst[...].astype(F32)
    for s in sources:
        total = total + s[...].astype(F32)
    dst[...] = total.astype(dst.dtype)


class Ring:
    def __init__(self, links, block, pos, right, left, land):
        self.block, self.land = block, land
        self.pos = pos
        self.rt, self.lf, self.opp = (pos + 1) % 4, (pos + 3) % 4, (pos + 2) % 4
        send, near, far = links.new_send(), links.new_recv(), links.new_recv()

        def c(t, half, slot, device):
            return links.copy(block(t, half), land.at[slot], device, send, near if slot < 2 else far)

        self.early = [c(self.opp, 0, 0, right), c(self.opp, 1, 1, left), c(self.rt, 1, 2, right), c(self.lf, 0, 3, left)]
        self.late = [c(self.rt, 0, 4, right), c(self.lf, 1, 5, left)]
        self.near = links.whole(land.at[pl.ds(0, 2)], send, near)
        self.far = links.whole(land.at[pl.ds(2, 4)], send, far)
        self.sent = links.whole(land, send, far)

    def start(self):
        for c in self.early:
            c.start()

    def middle(self):
        self.near.wait_recv()
        add_into(self.block(self.rt, 0), [self.land.at[0]])
        self.late[0].start()
        add_into(self.block(self.lf, 1), [self.land.at[1]])
        self.late[1].start()

    def finish(self):
        self.far.wait_recv()
        add_into(self.block(self.pos, 0), [self.land.at[4], self.land.at[3]])
        add_into(self.block(self.pos, 1), [self.land.at[2], self.land.at[5]])
        self.sent.wait_send()


class Reduce:
    def __init__(self, links, ref, lands, pos, at_z, at_x, last, after, col, width):
        z, x, y = pos
        every = slice(None)
        first, second = pl.ds(col, width // 2), pl.ds(col + width // 2, width // 2)
        land1z, land1x, land2z, land2x, self.land_y = lands

        def view(a, h, b, cols):
            return ref.at[a, pl.ds(h * 2, 2), b, every, cols]

        zr, zl, xr, xl = at_z(1), at_z(3), at_x(1), at_x(3)
        self.one = [
            Ring(links, lambda t, h: view(every, h, t, first), z, zr, zl, land1z),
            Ring(links, lambda t, h: view(t, h, every, second), x, xr, xl, land1x),
        ]
        self.two = [
            Ring(links, lambda t, h: view(t, h, z, first), x, xr, xl, land2z),
            Ring(links, lambda t, h: view(x, h, t, second), z, zr, zl, land2x),
        ]
        both = pl.ds(col, width)
        self.own = ref.at[x, y, z, every, both]
        self.last = Group(links, self.land_y, [(ref.at[x, ty, z, every, both], self.land_y.at[n], d) for n, (ty, d) in enumerate(last)])
        self.after = after
        self.at = 0

    def result_into(self, dst):
        total = self.own[...].astype(F32)
        for n in range(3):
            total = total + self.land_y[n].astype(F32)
        dst[...] = total

    def step(self):
        one, two = self.one, self.two
        if self.at == 0:
            for r in one:
                r.start()
        elif self.at == 1:
            for r in one:
                r.middle()
        elif self.at == 2:
            for r, n in zip(one, two):
                r.finish()
            for n in two:
                n.start()
        elif self.at == 3:
            for r in two:
                r.middle()
        elif self.at == 4:
            for r in two:
                r.finish()
            self.last.start()
        elif self.at == 5:
            self.last.wait()
            self.after(self)
        self.at += 1


class ReduceShort:
    def __init__(self, links, ref, lands, pos, at_z, at_x, far, after, half):
        z, x, yl = pos
        every = slice(None)
        cols = (pl.ds(0, half), pl.ds(half, ref.shape[-1] - half))
        land1z, land1x, land2z, land2x = lands
        self.one = [
            Ring(links, lambda t, h: ref.at[every, h, t, every, cols[0]], z, at_z(1), at_z(3), land1z),
            Ring(links, lambda t, h: ref.at[t, h, every, every, cols[1]], x, at_x(1), at_x(3), land1x),
        ]
        self.own = [ref.at[x, yl, z, :, c] for c in cols]
        self.lands = (land2z, land2x)
        self.two = [
            Group(links, land2z, [(ref.at[tx, ty, z, :, cols[0]], land2z.at[n], d) for n, (tx, ty, d) in enumerate(far[0])]),
            Group(links, land2x, [(ref.at[x, ty, tz, :, cols[1]], land2x.at[n], d) for n, (tz, ty, d) in enumerate(far[1])]),
        ]
        self.cols, self.after, self.at = cols, after, 0

    def step(self):
        if self.at == 0:
            for r in self.one:
                r.start()
        elif self.at == 1:
            for r in self.one:
                r.middle()
        elif self.at == 2:
            for r, cps in zip(self.one, self.two):
                r.finish()
                cps.start()
        elif self.at == 3:
            for cps in self.two:
                cps.wait()
            self.after(self)
        self.at += 1

    def result_into(self, dst):
        for own, land, cols in zip(self.own, self.lands, self.cols):
            total = own[...].astype(F32)
            for n in range(7):
                total = total + land[n].astype(F32)
            dst[:, cols] = total


def kernel(*refs):
    small, (lens, tokens, cot, w_qkv, w_out, w_in, w_down) = refs[:6], refs[6:13]
    (o_out, o_tok, o_wqkv, o_wout, o_win, o_wdn, o_small, o_ln) = refs[13:21]
    rest = refs[21:]
    R = {name: r for (name, _, _), r in zip(SCRATCH, rest)}
    send, recv, loc = rest[len(SCRATCH) :]

    dpi, s = lax.axis_index("dp"), lax.axis_index("seq")
    z, x, yl = dpi // 8, (dpi // 2) % 4, dpi % 2
    yh, c = s // 2, s % 2
    y, y_other = yh * 2 + yl, yh * 2 + 1 - yl

    def dev(zz, xx, yy, cc):
        return ((zz % 4) * 8 + (xx % 4) * 2 + (yy % 4) % 2, ((yy % 4) // 2) * 2 + cc)

    def at_z(d):
        return dev(z + d, x, y, c)

    def at_x(d):
        return dev(z, x + d, y, c)

    def at_y(d):
        return dev(z, x, y + d, c)

    sibling = dev(z, x, y, 1 - c)
    partner = dev(z, x, y + 2, c)
    diagonal = dev(z, x, y + 2, 1 - c)

    links = Links(send, recv, sibling)
    meet = [at_x(d) for d in (1, 2, 3)] + [at_y(d) for d in (1, 2, 3)] + [sibling, diagonal]
    for d in (1, 2, 3):
        for cc in (c, 1 - c):
            meet += [dev(z + d, x, y, cc), dev(z + d, x, y + 2, cc)]
    plane = [(dz, dx) for dz in range(4) for dx in range(4) if dz or dx]
    meet += [dev(z + dz, x + dx, y, c) for dz, dx in plane if dz and dx]
    for d in (1, 2, 3):
        meet += [dev(z + d, x, y_other, c), dev(z, x + d, y_other, c)]
    meet += [dev(z, x, y + 1, 1 - c), dev(z, x, y + 3, 1 - c)]
    barrier = pltpu.get_barrier_semaphore()
    for d in meet:
        pl.semaphore_signal(barrier, inc=1, device_id=d, device_id_type=MESH)

    loads = []

    def load(src, dst, n):
        cp = pltpu.make_async_copy(src, dst, loc.at[n])
        cp.start()
        return cp

    heads_of = (s, (1 - yh) * 2 + c)
    for w, sw in enumerate(heads_of):
        load(w_out.at[at256(sw), :], R["wout"].at[w], 0)
    loads.append(pltpu.make_async_copy(R["wout"], R["wout"], loc.at[0]))
    for a in range(2):
        for h in range(2):
            n = 1 + 4 * a + 2 * h
            wide = pl.ds(pl.multiple_of((2 * a + c) * 1024 + h * 512, 512), 512)
            loads.append(load(w_in.at[:, wide], R["win"].at[a, :, pl.ds(h * 512, 512)], n))
            loads.append(load(w_down.at[wide, :], R["wdn"].at[a, pl.ds(h * 512, 512), :], n + 1))
    for w, sw in enumerate(heads_of):
        for g in range(2):
            for j in range(3):
                cols = pl.ds(pl.multiple_of(j * 1024 + sw * 256 + g * 128, 128), 128)
                load(w_qkv.at[:, cols], R["wqkv"].at[w, g, :, pl.ds(j * 128, 128)], 9)
    loads.append(pltpu.make_async_copy(R["wqkv"], R["wqkv"], loc.at[9]))

    def loaded(first, count):
        for cp in loads[first : first + count]:
            cp.wait()

    own, sib = s, yh * 2 + 1 - c
    par, dia = (1 - yh) * 2 + c, (1 - yh) * 2 + 1 - c
    cal, nal = R["call"], R["nall"]
    cot_s = pieces(links, cot, cal.at[at256(own), :], sibling, PIECE)
    cot_p = links.copy(cot, cal.at[at256(own), :], partner)
    cal[at256(own), :] = cot[...]

    vecs, row = R["vecs"], 0
    for ref in small:
        for i in range(ref.shape[0] // D):
            vecs[row : row + 1, :] = ref[pl.ds(i * D, D)].astype(F32).reshape(1, D)
            row += 1
    gain, shift = vecs[0:1, :], vecs[1:2, :]
    mr = R["mr"]

    def norm_strip(u, carry):
        rows = pl.ds(pl.multiple_of(u * 32, 32), 32)
        xin = tokens[rows, :].astype(F32)
        mean = jnp.mean(xin, axis=-1, keepdims=True)
        cen = xin - mean
        r = lax.rsqrt(jnp.mean(cen * cen, axis=-1, keepdims=True) + 1e-05)
        mr[0, rows, :] = jnp.broadcast_to(mean, (32, 128))
        mr[1, rows, :] = jnp.broadcast_to(r, (32, 128))
        nal[pl.ds(pl.multiple_of(own * 256 + u * 32, 32), 32), :] = (cen * r * gain + shift).astype(BF)
        return carry

    lax.fori_loop(0, 8, norm_strip, 0, unroll=2)
    mine = nal.at[at256(own), :]
    nrm_s = pieces(links, mine, mine, sibling, PIECE)
    nrm_p = links.copy(mine, mine, partner)
    pl.semaphore_wait(barrier, len(meet))
    tok_s = pieces(links, tokens, R["tsib"], sibling, PIECE)
    sta_s = links.copy(mr, R["msib"], sibling)
    for cp in (cot_s, nrm_s, nrm_p, tok_s, sta_s):
        cp.start()

    sm = R["sm"]
    sm[0] = jnp.zeros((8, 1024), F32)
    sm[0, 4:5, :] = jnp.sum(cot[...].astype(F32), axis=0, keepdims=True)

    start1 = lens[0, 0]
    start2 = start1 + lens[0, 1]
    start3 = start2 + lens[0, 2]

    def first_of(t):
        return jnp.where(t >= start3, start3, jnp.where(t >= start2, start2, jnp.where(t >= start1, start1, 0)))

    tab = R["tab"]

    def tables(u):
        rows = pl.ds(pl.multiple_of(u * 64, 64), 64)
        t = lax.broadcasted_iota(jnp.int32, (64, 128), 0) + u * 64
        lane = lax.broadcasted_iota(jnp.int32, (64, 128), 1) % HEAD
        offset = (t - first_of(t)).astype(F32)
        freq = jnp.zeros((64, 128), F32)
        for i in range(ROT // 2):
            freq = jnp.where(lane % (ROT // 2) == i, math.exp(-2.0 * i * math.log(10000.0) / ROT), freq)
        angle = offset * freq
        cosine, sine = jnp.cos(angle), jnp.sin(angle)
        tab[0, rows, :] = jnp.where(lane < ROT, cosine, 1.0)
        tab[1, rows, :] = jnp.where(lane < ROT // 2, -sine, jnp.where(lane < ROT, sine, 0.0))

    def tables_():
        loop(16, tables)

    low_lane = lax.broadcasted_iota(jnp.int32, (BLK, 128), 1) % HEAD < ROT // 2

    def rotate(val, rows, sign):
        other = jnp.where(low_lane, pltpu.roll(val, 128 - ROT // 2, 1), pltpu.roll(val, ROT // 2, 1))
        return val * tab[0, rows, :] + sign * other * tab[1, rows, :]

    win, wdn, wqkv, wout = R["win"], R["wdn"], R["wqkv"], R["wout"]
    act, gh, outp, gnp = (R[n] for n in ("act", "gh", "outp", "gnp"))
    hid, ga = outp.at[:, pl.ds(0, 256)], gnp.at[:, pl.ds(0, 256)]
    kt, vt, qh, doh = (R[n] for n in ("kt", "vt", "qh", "doh"))
    xo, xr = R["xo"], R["xr"]
    q, k, v, do = ([xo.at[:, pl.ds(g * 512 + j * 128, 128)] for g in range(2)] for j in range(4))

    def qkv_block(blk):
        rows = at256(blk)
        for g in range(2):
            yv = dot_nn(nal[rows, :], wqkv[0, g])
            for j, dst in enumerate((q, k, v)):
                b = vecs[4 + j : 5 + j, pl.ds(pl.multiple_of(s * 256 + g * 128, 128), 128)]
                part = yv[:, j * 128 : (j + 1) * 128] + b
                if j < 2:
                    part = rotate(part, rows, 1.0)
                part = part.astype(BF)
                dst[g][rows, :] = part * jnp.asarray(0.125, BF) if j == 0 else part
                if j > 0:
                    (kt, vt)[j - 1][g, :, rows] = jnp.transpose(part)

    here = pl.ds(pl.multiple_of(yh * 512, 512), 512)
    there = pl.ds(pl.multiple_of((1 - yh) * 512, 512), 512)

    def grad_mixed(rows):
        for w, (dst, at) in enumerate(((do, rows), (q, pl.ds(pl.multiple_of(rows.start + (1 - 2 * yh) * 512, 256), 256)))):
            d = dot_nt(cal[rows, :], wout[w]).astype(BF)
            for g in range(2):
                dst[g][at, :] = d[:, g * 128 : (g + 1) * 128]

    def tile(a, t, at, count):
        cs = at256(t)
        near = pl.ds(pl.multiple_of(at, 256), count)
        rows = pl.ds(pl.multiple_of(yh * 512 + at, 256), count)
        hid[near, :] = dot_nn(nal[rows, :], win[a, :, cs]) + vecs[pl.ds(7 + 2 * a + c, 1), cs]
        ga[near, :] = dot_nt(cal[rows, :], wdn[a, cs, :])

        def strip(u, total):
            r = pl.ds(pl.multiple_of(at + u * 32, 32), 32)
            h = hid[r, :]
            cdf = 0.5 + 0.5 * lax.erf(h * (1.0 / math.sqrt(2.0)))
            dens = jnp.exp(-0.5 * h * h) * (1.0 / math.sqrt(2.0 * math.pi))
            to = pl.ds(pl.multiple_of(a * 512 + at + u * 32, 32), 32)
            act[to, cs] = (h * cdf).astype(BF)
            grad = (ga[r, :] * (cdf + h * dens)).astype(BF)
            gh[to, cs] = grad
            return total + jnp.sum(grad.astype(F32).reshape(4, 8, 256), axis=0)

        total = lax.fori_loop(0, count // 32, strip, jnp.zeros((8, 256), F32), unroll=2)
        sm[0, a : a + 1, cs] += jnp.sum(total, axis=0, keepdims=True)

    def tiles(a, h):
        loaded(1 + 4 * a + 2 * h, 2)
        loop(2, lambda i: tile(a, 2 * h + i, 0, 512))

    g_ffn = R["g_ffn"]

    def grads_in(a, col, width):
        half = pl.ds(a * 512, 512)

        def part(m):
            res = dot_tn(nal[here, at256(m)], gh[half, pl.ds(col, width)]).astype(BF)
            g_ffn[a, 0, :, :, m, :, pl.ds(col, width)] = res.reshape(4, 4, 16, width)

        loop(4, part)

    def grads_down(a):
        half = pl.ds(a * 512, 512)

        def part(m):
            res = dot_tn(act[half, at256(m)], cal[here, :]).astype(BF)
            g_ffn[a, 1, m] = res.reshape(4, 4, 16, 1024)

        loop(4, part)

    finals = []

    shared = [(links.new_send(), links.new_recv()) for _ in range(2)]

    def put(src, dst, device, sends, arrives):
        cp = links.copy(src, dst, device)
        finals.append((cp, sends, arrives))
        pl.when(sends)(cp.start)

    def keep(src, dst, here_too):
        @pl.when(here_too)
        def _():
            dst[...] = src[...]

    fin_ffn, fin_qkv, fin_out = R["fin_ffn"], R["fin_qkv"], R["fin_out"]

    def in_done(a, col, width):
        def done(red):
            cols = pl.ds(pl.multiple_of((2 * a + c) * 1024 + col, 512), width)
            fin = fin_ffn.at[a, 0, :, pl.ds(col, width)]
            red.result_into(fin)
            links.copy(fin.at[pl.ds(pl.multiple_of((1 - c) * 8, 8), 8), :], o_win.at[:, cols], sibling, *shared[0]).start()
            o_win[:, cols] = fin[pl.ds(pl.multiple_of(c * 8, 8), 8), :]

        return done

    def down_done(a):
        def done(red):
            red.result_into(fin_ffn.at[a, 1])
            to = dev(2 * a + c, x, y, z // 2)
            for h in range(2):
                rows, right = pl.ds(h * 16, 16), z % 2 == h
                here_too = (z == 2 * a + c) & (z // 2 == c)
                from_here = (z == 2 * c + h) & (z % 2 == c)
                sends = right & jnp.logical_not(here_too)
                arrives = (z // 2 == a) & jnp.logical_not(from_here)
                put(fin_ffn.at[a, 1], o_wdn.at[rows, :], to, sends, arrives)
                keep(fin_ffn.at[a, 1], o_wdn.at[rows, :], right & here_too)

        return done

    def qkv_done(g):
        def done(red):
            red.result_into(fin_qkv.at[g])
            for j in range(3):
                src_l = pl.ds(j * 128, 128)
                dst_l = pl.ds(pl.multiple_of(j * 1024 + s * 256 + g * 128, 128), 128)
                for d in (1, 2, 3):
                    t = (s + d) % 4
                    src = fin_qkv.at[g, pl.ds(pl.multiple_of(t * 8, 8), 8), src_l]
                    links.copy(src, o_wqkv.at[:, dst_l], (dpi, t), *shared[1]).start()
                o_wqkv[:, dst_l] = fin_qkv[g, pl.ds(pl.multiple_of(s * 8, 8), 8), src_l]

        return done

    def out_done(red):
        red.result_into(fin_out)
        for cc in range(2):
            to = dev(s, x, (z // 2) * 2 + yl, cc)
            src = fin_out.at[pl.ds(cc * 8, 8), :]
            for h in range(2):
                dst, right = o_wout.at[:, pl.ds(h * 512, 512)], z % 2 == h
                here_too = (z == s) & (z // 2 == yh) & (c == cc)
                from_here = (z == 2 * yh + h) & (s == z)
                sends = right & jnp.logical_not(here_too)
                arrives = (c == cc) & jnp.logical_not(from_here)
                put(src, dst, to, sends, arrives)
                keep(src, dst, right & here_too)

    def place(yy):
        return (yy % 2) * 2 + (yy % 4) // 2

    def reduce_ffn(a, w, col, width, done):
        last = [(place(y + d), at_y(d)) for d in (1, 2, 3)]
        half = pl.ds(col // 2, width // 2)
        lands = (R["r1z_ffn"].at[a, :, w, :, :, :, half], R["r1x_ffn"].at[a, :, w, :, :, :, half])
        lands += (R["r2_ffn"].at[a, 0, :, w, :, :, half], R["r2_ffn"].at[a, 1, :, w, :, :, half])
        lands += (R["r3_ffn"].at[a, :, w, :, pl.ds(col, width)],)
        return Reduce(links, g_ffn.at[a, w], lands, (z, x, place(y)), at_z, at_x, last, done, col, width)

    def reduce_in(a, col, width):
        return reduce_ffn(a, 0, col, width, in_done(a, col, width))

    def reduce_down(a):
        return reduce_ffn(a, 1, 0, 1024, down_done(a))

    def reduce_qkv(g):
        half = 256 if g == 0 else 128
        one, two = pl.ds(0, half), pl.ds(0, 384 - half)
        lands = (R["r1z_qkv"].at[g, :, :, :, one], R["r1x_qkv"].at[g, :, :, :, two])
        lands += (R["r2_qkv"].at[g, 0, :, :, one], R["r2_qkv"].at[g, 1, :, :, two])
        return ReduceShort(links, R["g_qkv"].at[g], lands, (z, x, yl), at_z, at_x, far, qkv_done(g), half)

    def reduce_out():
        lands = (R["r1z_out"], R["r1x_out"], R["r2_out"].at[0], R["r2_out"].at[1])
        return ReduceShort(links, R["g_out"], lands, (z, x, yl), at_z, at_x, far, out_done, 256)

    far = [
        [((x + d) % 4, ty, dev(z, x + d, ry, c)) for d in range(4) for ty, ry in ((yl, y), (1 - yl, y_other)) if d or ty is not yl],
        [((z + d) % 4, ty, dev(z + d, x, ry, c)) for d in range(4) for ty, ry in ((yl, y), (1 - yl, y_other)) if d or ty is not yl],
    ]

    pb, ds = R["pb"], R["ds"]
    dk, dv, dq, mx = (R[n] for n in ("dk", "dv", "dq", "mx"))
    g_qkv, g_out = R["g_qkv"], R["g_out"]

    def attend(g, i):
        n = 256 * (i + 1)
        rows = pl.ds(256 * i, 256)
        keys = pl.ds(0, n)
        chunks = [pl.ds(j * 256, 256) for j in range(n // 256)]

        def sc(u, ch):
            return outp.at[pl.ds(u * 256, 256), ch]

        def dp(u, ch):
            return gnp.at[pl.ds(u * 256, 256), ch]

        def fold(a, op):
            return op(a.reshape(32, 8, BLK), axis=0)

        tq = lax.broadcasted_iota(jnp.int32, (1, BLK), 1) + 256 * i
        first_key = first_of(tq)

        def allowed(j):
            tk = lax.broadcasted_iota(jnp.int32, (BLK, BLK), 0) + 256 * j
            return (tk >= first_key) & (tk <= tq) if j == i else tk >= first_key

        heads = range(2)
        tops, stats = [], []
        for u in heads:
            lanes = lax.broadcasted_iota(jnp.int32, (BLK, 128), 1) // HEAD == u
            qh[u] = jnp.where(lanes, q[g][rows, :], jnp.zeros((), BF))
            doh[u] = jnp.where(lanes, do[g][rows, :], jnp.zeros((), BF))
        for u in heads:
            top = jnp.full((8, BLK), -1e30, F32)
            for j, ch in enumerate(chunks):
                a = jnp.where(allowed(j), dot_nt(k[g][ch, :], qh[u]), -1e30)
                sc(u, ch)[...] = a
                top = jnp.maximum(top, fold(a, jnp.max))
            tops.append(jnp.max(top, axis=0, keepdims=True))
        for u in heads:
            total, inner = jnp.zeros((8, BLK), F32), jnp.zeros((8, BLK), F32)
            for ch in chunks:
                gr = dot_nt(v[g][ch, :], doh[u])
                dp(u, ch)[...] = gr
                e = jnp.exp(sc(u, ch)[...] - tops[u])
                sc(u, ch)[...] = e
                total, inner = total + fold(e, jnp.sum), inner + fold(e * gr, jnp.sum)
            inv = 1.0 / jnp.sum(total, axis=0, keepdims=True)
            stats.append((inv, jnp.sum(inner, axis=0, keepdims=True) * inv))
        for u in heads:
            inv, inner = stats[u]
            for j, ch in enumerate(chunks):
                p = sc(u, ch)[...] * inv
                p_low = p.astype(BF)
                d_low = (p * (dp(u, ch)[...] - inner)).astype(BF)
                pb[u, ch, :] = p_low
                ds[u, ch, :] = d_low
                if i == 3 and u == 0:
                    dk[ch, :] = dot_nn(d_low, qh[u])
                    dv[ch, :] = dot_nn(p_low, doh[u])
                else:
                    dk[ch, :] += dot_nn(d_low, qh[u])
                    dv[ch, :] += dot_nn(p_low, doh[u])
        for u in heads:
            hr = pl.ds(u * HEAD, HEAD)
            mx[hr, :] = dot_nn(vt[g, hr, keys], pb[u, keys, :])
            dq[hr, :] = dot_nn(kt[g, hr, keys], ds[u, keys, :])

        def place_in(j, val):
            xo[rows, pl.ds(g * 512 + j * 128, 128)] = val

        place_in(3, jnp.transpose(mx[...]).astype(BF))
        grad_q = jnp.transpose(dq[...] * 0.125).astype(BF).astype(F32)
        place_in(0, rotate(grad_q, rows, -1.0).astype(BF))
        grad_k = dk[rows, :].astype(BF).astype(F32)
        place_in(1, rotate(grad_k, rows, -1.0).astype(BF))
        place_in(2, dv[rows, :].astype(BF))

    back = []

    def start_back(g):
        cols = pl.ds(g * 512, 512)
        view = xr.at[:, cols]
        copies = [(xo.at[pl.ds(256 * i, 256), cols], xr.at[pl.ds(256 * (i % 2), 256), cols], partner) for i in range(4)]
        back.append(Group(links, view, copies))

    def send_back(g, i):
        pl.when(yh != i // 2)(back[g].parts[i].start)

    start_back(0)
    start_back(1)

    def qkv_grads(g):
        def part(m):
            res = dot_tn(nal[:, at256(m)], xo[:, pl.ds(g * 512, 384)]).astype(BF)
            g_qkv[g, :, :, m] = res.reshape(4, 2, 32, 384)

        loop(4, part)

    def bias_grads(g):
        total = jnp.zeros((8, 384), F32)

        def part(u, total):
            r = pl.ds(pl.multiple_of(u * 64, 64), 64)
            return total + jnp.sum(xo[r, pl.ds(g * 512, 384)].astype(F32).reshape(8, 8, 384), axis=0)

        total = jnp.sum(lax.fori_loop(0, 16, part, total), axis=0, keepdims=True)
        for j in range(3):
            sm[0, 2:3, pl.ds(j * 256 + g * 128, 128)] = total[:, j * 128 : (j + 1) * 128]

    def out_grads(g):
        res = dot_tn(xo[:, pl.ds(g * 512 + 384, 128)], cal[...]).astype(BF).reshape(2, 2, 2, 16, 1024)
        for h in range(2):
            for n in range(2):
                g_out[pl.ds(2 * g, 2), :, 2 * h + n] = res[:, :, h, :, n * 512 : (n + 1) * 512]

    mine_at, theirs_at = c * 256, (1 - c) * 256

    def outputs(n):
        cs = at256(n)
        top, low, every = pl.ds(0, 512), pl.ds(512, 512), pl.ds(0, 512)
        o = dot_nn(act[top, :], wdn[0, :, cs]) + dot_nn(act[low, :], wdn[1, :, cs])
        g = dot_nt(gh[top, :], win[0, cs, :]) + dot_nt(gh[low, :], win[1, cs, :])
        for src, rows, w, p in ((xo, here, 0, 0), (xo, here, 0, 1), (xr, every, 1, 0)):
            o += dot_nn(src[rows, pl.ds(p * 512 + 384, 128)], wout[w, pl.ds(p * 128, 128), cs])
            g += dot_nt(src[rows, pl.ds(p * 512, 384)], wqkv[w, p, cs, :])
        outp[:, cs], gnp[:, cs] = o, g

    def project_last(at):
        rows = pl.ds(pl.multiple_of(at, 256), 256)

        def part(n):
            cs = at256(n)
            outp[rows, cs] += dot_nn(xr[rows, pl.ds(896, 128)], wout[1, pl.ds(128, 128), cs])
            gnp[rows, cs] += dot_nt(xr[rows, pl.ds(512, 384)], wqkv[1, 1, cs, :])

        loop(4, part)

    stage, rxs = gh, R["rxs"]

    def stage_strip(u):
        r = pl.ds(pl.multiple_of(u * 64, 64), 64)
        rr = pl.ds(pl.multiple_of(theirs_at + u * 64, 64), 64)
        stage[r, :] = outp[rr, :].astype(BF)
        stage[pl.ds(pl.multiple_of(256 + u * 64, 64), 64), :] = gnp[rr, :].astype(BF)

    pairs_y = [at_y(d) for d in (1, 2, 3)] + [dev(z, x, y + d, 1 - c) for d in range(4)]
    plane_devices = [dev(z + dz, x + dx, y, c) for dz, dx in plane]
    sp, spr, sq, sqr = (R[n] for n in ("sp", "spr", "sq", "sqr"))

    def bias_plane():
        row = [sm[0, r : r + 1, n * 256 : (n + 1) * 256] for r in (0, 1, 2, 4) for n in range(4)]
        sp[0] = jnp.concatenate(row, axis=0).astype(BF)
        group = Group(links, spr, [(sp.at[0], spr.at[n], d) for n, d in enumerate(plane_devices)])
        group.start()
        return group

    def bias_chips(group):
        group.wait()
        row = [sm[0, r : r + 1, n * 256 : (n + 1) * 256] for r in (0, 1, 2, 4) for n in range(4)]
        total = jnp.concatenate(row, axis=0)
        for n in range(15):
            total = total + spr[n].astype(F32)
        sq[0] = total
        group = Group(links, sqr, [(sq.at[0], sqr.at[n], d) for n, d in enumerate(pairs_y)])
        group.start()
        return group

    def bias_done(group):
        group.wait()
        same = [(0, sq[0])] + [(d, sqr[d - 1]) for d in (1, 2, 3)]
        other = [(d, sqr[3 + d]) for d in range(4)]
        for core, parts in ((c, same), (1 - c, other)):
            total = parts[0][1] + parts[1][1] + parts[2][1] + parts[3][1]
            o_small[core, 0:8] = total[0:8]
            o_small[core, 16:24] = total[8:16]
            both = [jnp.zeros((4, 256), F32)] * 2
            for d, val in parts:
                at_high = ((y + 4 - d) % 4) // 2
                both = [acc + jnp.where(at_high == h, val[8:12], 0.0) for h, acc in enumerate(both)]
            o_small[core, 8:16] = jnp.concatenate(both, axis=0)

    def send_grad_mixed():
        for g in range(2):
            cp = links.copy(q[g].at[there, :], do[g].at[here, :], partner)
            cp.start()
            back_do.append(cp)

    back_do = []

    def forward(buf):
        rows = buf.at[at256(par), :]
        cp = pieces(links, rows, rows, sibling, PIECE)
        cp.start()
        return cp

    def sum_strip(u, carry):
        ru = pl.ds(pl.multiple_of(u * 32, 32), 32)
        for at, tok, stat in ((mine_at, tokens, mr), (theirs_at, R["tsib"], R["msib"])):
            gn = gnp[pl.ds(pl.multiple_of(at + u * 32, 32), 32), :]
            hat = (tok[ru, :].astype(F32) - stat[0, ru, 0:1]) * stat[1, ru, 0:1]
            carry = (carry[0] + jnp.sum((gn * hat).reshape(4, 8, D), axis=0), carry[1] + jnp.sum(gn.reshape(4, 8, D), axis=0))
        return carry

    ln, lnr, lnp, lnq = (R[n] for n in ("ln", "lnr", "lnp", "lnq"))

    def norm_sums():
        zero = jnp.zeros((8, D), F32)
        sg, sb = (jnp.sum(v, axis=0, keepdims=True) for v in lax.fori_loop(0, 8, sum_strip, (zero, zero)))
        low = lax.broadcasted_iota(jnp.int32, (1, 128), 1) < 64
        for n in range(8):
            g, b = sg[:, n * 128 : (n + 1) * 128], sb[:, n * 128 : (n + 1) * 128]
            swap_g, swap_b = (jnp.concatenate([v[:, 64:128], v[:, 0:64]], axis=1) for v in (g, b))
            ln[2 * n] = jnp.where(low, g, swap_b)
            ln[2 * n + 1] = jnp.where(low, swap_g, b)

    def norm_plane():
        copies = []
        for n, (dz, dx) in enumerate(plane):
            place_of = ((z + dz) % 4) * 4 + (x + dx) % 4
            copies.append((ln.at[place_of], lnr.at[n], dev(z + dz, x + dx, y, c)))
        group = Group(links, lnr, copies)
        group.start()
        return group

    def norm_chips(group):
        group.wait()
        total = ln[z * 4 + x]
        for n in range(15):
            total = total + lnr[n]
        lnp[0] = total
        group = Group(links, lnq, [(lnp.at[0], lnq.at[n], d) for n, d in enumerate(pairs_y)])
        group.start()
        return group

    def norm_done(group):
        group.wait()
        total = lnp[0]
        for n in range(7):
            total = total + lnq[n]
        o_ln[...] = total

    def last_strip(u, carry):
        ru = pl.ds(pl.multiple_of(u * 32, 32), 32)
        r = pl.ds(pl.multiple_of(mine_at + u * 32, 32), 32)
        xin = tokens[ru, :].astype(F32)
        total = outp[r, :] + rxs[0, ru, :].astype(F32)
        o_out[ru, :] = (xin + total + vecs[2:3, :] + vecs[3:4, :]).astype(BF)
        rs = mr[1, ru, 0:1]
        hat = (xin - mr[0, ru, 0:1]) * rs
        n = (gnp[r, :] + rxs[1, ru, :].astype(F32)) * gain
        grad = n - jnp.mean(n, axis=-1, keepdims=True) - hat * jnp.mean(n * hat, axis=-1, keepdims=True)
        o_tok[ru, :] = cot[ru, :].astype(F32) + grad * rs
        return carry

    tables_()
    loaded(0, 1)
    grad_mixed(at256(own))
    loaded(1, 2)
    loop(2, lambda i: tile(0, i, c * 256, 256))
    cot_s.wait_recv()
    grad_mixed(at256(sib))
    send_grad_mixed()
    cot_p.start()
    nrm_s.wait_recv()
    loop(2, lambda i: tile(0, i, (1 - c) * 256, 256))
    grads_in(0, 0, 512)
    red_a = reduce_in(0, 0, 512)
    red_a.step()
    tiles(0, 1)
    grads_in(0, 512, 512)
    red_b = reduce_in(0, 512, 512)
    red_b.step()
    grads_down(0)
    red_a.step()
    red_c = reduce_down(0)
    red_c.step()
    tiles(1, 0)
    red_b.step()
    tiles(1, 1)
    grads_in(1, 0, 1024)
    red_a.step()
    red_d = reduce_in(1, 0, 1024)
    red_d.step()
    grads_down(1)
    red_c.step()
    red_e = reduce_down(1)
    red_e.step()
    loaded(9, 1)
    qkv_block(own)
    qkv_block(sib)
    nrm_p.wait_recv()
    nrm_f = forward(nal)
    for cp in back_do:
        cp.wait_send()
    qkv_block(par)
    nrm_f.wait_recv()
    qkv_block(dia)
    for cp in back_do:
        cp.wait_recv()
    red_b.step()
    attend(0, 3)
    send_back(0, 3)
    red_d.step()
    red_a.step()
    attend(0, 2)
    send_back(0, 2)
    attend(0, 1)
    send_back(0, 1)
    attend(0, 0)
    send_back(0, 0)
    cot_p.wait_recv()
    cot_f = forward(cal)
    qkv_grads(0)
    red2 = reduce_qkv(0)
    red2.step()
    red_c.step()
    attend(1, 3)
    send_back(1, 3)
    attend(1, 2)
    send_back(1, 2)
    red_e.step()
    attend(1, 1)
    send_back(1, 1)
    attend(1, 0)
    send_back(1, 0)
    red_d.step()
    qkv_grads(1)
    red3 = reduce_qkv(1)
    red3.step()
    for g in range(2):
        bias_grads(g)
    sums = bias_plane()
    red_a.step()
    red_b.step()
    red_e.step()
    cot_f.wait_recv()
    for g in range(2):
        out_grads(g)
    red4 = reduce_out()
    red4.step()
    red2.step()
    red_d.step()
    back[0].wait_recv()
    outputs(0)
    red_c.step()
    red3.step()
    outputs(1)
    sums = bias_chips(sums)
    red_a.step()
    red_b.step()
    red4.step()
    red2.step()
    outputs(2)
    red_c.step()
    red_d.step()
    red_e.step()
    outputs(3)
    red3.step()
    red4.step()
    red_b.step()
    bias_done(sums)
    back[1].wait_recv()
    project_last(theirs_at)
    for cp in (tok_s, sta_s):
        cp.wait_recv()
    loop(4, stage_strip)
    swap = [pieces(links, stage.at[pl.ds(w * 256, 256), :], rxs.at[w], sibling, PIECE) for w in range(2)]
    for cp in swap:
        cp.start()
    red_e.step()
    red_c.step()
    red_d.step()
    red2.step()
    project_last(mine_at)
    norm_sums()
    sums = norm_plane()
    red3.step()
    red4.step()
    for cp in swap:
        cp.wait()
    lax.fori_loop(0, 8, last_strip, 0, unroll=2)
    sums = norm_chips(sums)
    red_e.step()
    for cp in (cot_s, nrm_s, cot_p, nrm_p, cot_f, nrm_f, tok_s, sta_s):
        cp.wait_send()
    norm_done(sums)
    for cp in back:
        cp.wait_send()
    links.whole(o_win.at[:, pl.ds(0, 2048)], *shared[0]).wait()
    links.whole(o_wqkv.at[:, pl.ds(0, 2304)], *shared[1]).wait()
    for cp, sends, arrives in finals:
        pl.when(sends)(cp.wait_send)
        pl.when(arrives)(cp.wait_recv)
    assert [r.at for r in (red_a, red_b, red_c, red_d, red_e)] == [6] * 5
    assert [r.at for r in (red2, red3, red4)] == [4] * 3
    assert (links.sends, links.recvs) == (NSEND, NRECV), (links.sends, links.recvs)


def hand_over(*refs):
    raw, small, ln = refs[:6], refs[6], refs[7]
    outs, vec, line = refs[8:14], refs[14:20], refs[20]
    for src, dst in zip(raw, outs):
        dst[...] = src[...]
    index = lax.axis_index("dp") * 4 + lax.axis_index("seq")
    for n in range(4):
        cols = pl.ds(n * 256, 256)
        for r in (3, 5):
            line[r : r + 1, cols] = small[0, 20 + n : 21 + n, :] + small[1, 20 + n : 21 + n, :]
        for q in range(4):
            line[4:5, pl.ds(q * 1024 + n * 256, 256)] = small[q % 2, 4 * (q // 2) + n : 4 * (q // 2) + n + 1, :]
            if n < 3:
                line[2:3, pl.ds(n * 1024 + q * 256, 256)] = small[q % 2, 8 + 4 * (q // 2) + n : 9 + 4 * (q // 2) + n, :]
    for r in range(2):
        mine = pltpu.roll(jnp.broadcast_to(ln[...], (8, 128)), (128 - (index % 8) * 8 - 64 * r) % 128, 1)
        vec[r][...] = mine[0, 0:8]
    for r, out in enumerate(vec):
        if r < 2:
            continue
        n = out.shape[0]
        at = index * n
        part = line[r : r + 1, pl.ds(pl.multiple_of((at // 128) * 128, 128), 256)]
        part = pltpu.roll(jnp.broadcast_to(part, (8, 256)), (256 - at % 128) % 256, 1)
        out[...] = part[0, 0:n]


def on_device(tokens, lengths, ln_gain, ln_bias, w_qkv, b_qkv, w_out, b_out, w_in, b_in, w_down, b_down, cotangent):
    V = pl.BlockSpec(memory_space=pltpu.VMEM)
    H = pl.BlockSpec(memory_space=pl.ANY)
    S = pl.BlockSpec(memory_space=pltpu.SMEM)
    sds = jax.ShapeDtypeStruct
    outs = pl.pallas_call(
        kernel,
        out_shape=[
            sds((BLK, D), BF),
            sds((BLK, D), F32),
            sds((8, 3 * D), F32),
            sds((8, D), F32),
            sds((8, 4 * D), F32),
            sds((32, D), F32),
            sds((2, 24, 256), F32),
            sds((1, 128), F32),
        ],
        in_specs=[V] * 6 + [S, V, V, H, H, H, H],
        out_specs=[V] * 8,
        scratch_shapes=[pltpu.VMEM(shape, dt) for _, shape, dt in SCRATCH]
        + [pltpu.SemaphoreType.DMA((NSEND,)), pltpu.SemaphoreType.DMA((NRECV,)), pltpu.SemaphoreType.DMA((NLOC,))],
        compiler_params=pltpu.CompilerParams(collective_id=0, has_side_effects=True, vmem_limit_bytes=VMEM_LIMIT),
        name="layer",
    )(ln_gain, ln_bias, b_out, b_down, b_qkv, b_in, lengths, tokens[0], cotangent[0], w_qkv, w_out, w_in, w_down)
    vec = [sds((n // 128,), F32) for n in (D, D, 3 * D, D, 4 * D, D)]
    finals = pl.pallas_call(
        hand_over,
        out_shape=[sds(o.shape, o.dtype) for o in outs[:6]] + vec,
        in_specs=[V] * 8,
        out_specs=[V] * 12,
        scratch_shapes=[pltpu.VMEM((8, 4 * D + 128), F32)],
        name="shares",
    )(*outs)
    out, grad_tokens, g_wqkv, g_wout, g_win, g_wdn, g_gain, g_bias, g_bqkv, g_bout, g_bin, g_bdown = finals
    return (out[None], grad_tokens[None], g_gain, g_bias, g_wqkv, g_bqkv, g_wout, g_bout, g_win, g_bin, g_wdn, g_bdown)


def solution(mesh):
    act, vec, mat = P("dp", "seq", None), P(("dp", "seq")), P(("dp", "seq"), None)
    return jax.shard_map(
        on_device,
        mesh=mesh,
        in_specs=(act, P("dp", None)) + (P(),) * 10 + (act,),
        out_specs=(act, act, vec, vec, mat, vec, mat, vec, mat, vec, mat, vec),
        check_vma=False,
    )
```
